32 devices in a mesh: depth: 4 (over x, core), gx: 2 (over y), gy: 4 (over z).
Axes of the slice: x: 2, y: 2, z: 4, core: 2. Of those that a mesh axis runs over, the one named last changes fastest.
Arguments:
- arrival: bfloat16 [4, 192, 2, 4, 896], P('depth', None, 'gx', 'gy'), may hold values from -6 to 6
- source: bfloat16 [4, 4, 192, 2, 4, 896], P('depth', None, None, 'gx', 'gy'), may hold values from -6 to 6
- assignment: int32 [4, 192], replicated, may hold values from 0 to 191, each once within a row
- counts: int32 [7, 12, 2, 4], P(None, None, 'gx', 'gy'), may hold values from 1 to 16
- first_map: bfloat16 [4, 2, 4, 896, 896], P('depth', 'gx', 'gy'), may hold values from -0.1875 to 0.1875
- second_map: bfloat16 [4, 2, 4, 896, 896], P('depth', 'gx', 'gy'), may hold values from -0.1875 to 0.1875
- damping: float32 [4, 2, 4, 896], P('depth', 'gx', 'gy'), may hold values from 0.2 to 0.9
Outputs:
- final_traces: bfloat16 [4, 192, 2, 4, 896], P('depth', None, 'gx', 'gy')
The draws below stay inside these ranges and needn't reach their ends.
Inputs may be any that keep to these rules, and one draw needn't show every extreme that they name: Each row of assignment is a permutation of the 192 shots.
All inputs are finite; a program needn't handle non-finite values.
Results may differ from the reference program's by a relative error of at most 0.017.
Values may be sent and summed in bfloat16 or wider, within the bound.
No kernel may reach another device: no remote copies, remote signals or barrier semaphores. Data moves between devices by JAX's collectives and lax.ppermute only.
A program may use at most 64 MiB of HBM per device.

```python
import math
import jax
import jax.numpy as jnp
from jax import lax

FX = 32
FY = 28
M = 896
SHOT_BATCH = 16
NBATCH = 12
ROUNDS = 4
SLOTS = 192
LAYERS = 4
BX = 2
BY = 4
UNITS = 7


def with_ends(values, own_key, smallest, largest):
    extent = values.shape
    spot = [jax.random.randint(jax.random.fold_in(own_key, axis), (), 0, extent[axis]) for axis in range(len(extent))]
    values = values.at[tuple(spot)].set(smallest)
    longest = extent.index(max(extent))
    spot[longest] = (spot[longest] + 1) % extent[longest]
    return values.at[tuple(spot)].set(largest)


def steps_of(stream_key, dims, pieces, smallest, largest):
    factor_of = 1.0
    for axis_at, shards_of in pieces:
        heights = jax.random.uniform(jax.random.fold_in(jax.random.fold_in(stream_key, 6), axis_at), (shards_of,), jnp.float32, smallest / len(pieces), largest / len(pieces))
        factor_of = factor_of * jnp.repeat(jnp.exp(heights), dims[axis_at] // shards_of).reshape((-1,) + (1,) * (len(dims) - 1 - axis_at))
    return factor_of


def noise(own_key, dims, width, reach, split=(), kind=jnp.bfloat16):
    values = jax.random.normal(own_key, dims, jnp.float32) * width
    if len(split) > 0:
        values = steps_of(own_key, dims, split, -0.22, 0.18) * values
    return jnp.clip(values, min=-reach, max=reach).astype(kind)


def setup_inputs(seed: int = 0) -> dict:
    keys = jax.random.split(jax.random.key(seed), 8)
    return {
        "arrival": noise(keys[0], (LAYERS, SLOTS, BX, BY, M), 1.0, 6.0, ((0, 4), (2, 2), (3, 4))),
        "source": noise(keys[1], (LAYERS, ROUNDS, SLOTS, BX, BY, M), 1.0, 6.0, ((0, 4), (3, 2), (4, 4))),
        "assignment": jax.vmap(lambda own: jax.random.permutation(own, SLOTS))(jax.random.split(keys[2], ROUNDS)).reshape((ROUNDS, SLOTS)).astype(jnp.int32),
        "counts": with_ends(jax.random.randint(keys[3], (UNITS, NBATCH, BX, BY), 1, SHOT_BATCH + 1), jax.random.fold_in(keys[3], 1), 1, SHOT_BATCH).astype(jnp.int32),
        "first_map": noise(keys[4], (LAYERS, BX, BY, M, M), M ** -0.5, 0.1875, ((0, 4), (1, 2), (2, 4))),
        "second_map": noise(keys[5], (LAYERS, BX, BY, M, M), M ** -0.5, 0.1875, ((0, 4), (1, 2), (2, 4))),
        "damping": jnp.clip(jnp.exp(math.log(0.9) - 1.50407736 * jax.random.uniform(keys[6], (LAYERS, BX, BY, M), jnp.float32) ** steps_of(keys[6], (LAYERS, BX, BY, M), ((0, 4), (1, 2), (2, 4)), -0.2, 0.2)), 0.2, 0.9),
    }


coupling_weight = 0.25


def lateral(mapped):
    slot_count = mapped.shape[0]
    face_grid = mapped.reshape(slot_count, BX, BY, FX, FY).transpose(0, 1, 3, 2, 4).reshape(slot_count, BX * FX, BY * FY)
    padded = jnp.pad(face_grid.astype(jnp.float32), ((0, 0), (1, 1), (1, 1)))
    around_sum = padded[:, 2:, 1:-1] + padded[:, :-2, 1:-1] + padded[:, 1:-1, 2:] + padded[:, 1:-1, :-2]
    regrid = around_sum.reshape(slot_count, BX, FX, BY, FY).transpose(0, 1, 3, 2, 4)
    return regrid.reshape(slot_count, BX, BY, FX * FY)


def reference(arrival, source, assignment, counts, first_map, second_map, damping):
    layer_count = arrival.shape[0]
    slot_count = arrival.shape[1]
    positions = jnp.arange(SHOT_BATCH, dtype=jnp.int32)
    incoming = arrival
    traces = arrival
    for round_number in range(ROUNDS):
        def one_layer(packed):
            layer_index, arriving, sources_now, map_first, map_second, damping_now = packed
            unit_index = (round_number - layer_index + layer_count - 1).astype(jnp.int32)
            live_counts = lax.dynamic_index_in_dim(counts, unit_index, 0, keepdims=False)
            active = (positions[None, :, None, None] < live_counts[:, None, :, :]).reshape(slot_count, BX, BY)
            active = active.astype(jnp.float32)[..., None]
            picked = jnp.take(sources_now, assignment[round_number], axis=0)
            start_trace = (active * (picked.astype(jnp.float32) + arriving.astype(jnp.float32))).astype(jnp.bfloat16)
            mapped = jnp.einsum("sijm,ijmn->sijn", start_trace.astype(jnp.float32), map_first.astype(jnp.float32)).astype(jnp.bfloat16)
            coupled = (mapped.astype(jnp.float32) + coupling_weight * lateral(mapped)).astype(jnp.bfloat16)
            imaged = jnp.einsum("sijm,ijmn->sijn", coupled.astype(jnp.float32), map_second.astype(jnp.float32))
            blended = damping_now * imaged + (1.0 - damping_now) * start_trace.astype(jnp.float32)
            return (active * blended).astype(jnp.bfloat16)

        traces = lax.map(one_layer, (jnp.arange(layer_count, dtype=jnp.int32), incoming, source[:, round_number], first_map, second_map, damping))
        incoming = jnp.concatenate([jnp.zeros_like(traces[:1]), traces[:-1]], axis=0)
    return traces
```

```python
import functools

import jax
import jax.numpy as jnp
from jax import lax
from jax.experimental import pallas as pl
from jax.experimental.pallas import tpu as pltpu
from jax.sharding import PartitionSpec as P

FX = 32
FY = 28
SHOT_BATCH = 16

coupling_weight = 0.25

LANES = 128
GROUP = LANES // 4
EDGE_AXES = (("gx", 0), ("gy", 2))


def dot(a, b):
    return jnp.dot(a, b, preferred_element_type=jnp.float32)


def dot_t(a, b):
    return lax.dot_general(a, b, (((0,), (0,)), ((), ())), preferred_element_type=jnp.float32)


def edge_selector(cells):
    row = lax.broadcasted_iota(jnp.int32, (cells, LANES), 0)
    lane = lax.broadcasted_iota(jnp.int32, (cells, LANES), 1)
    group = lane // GROUP
    spot = lane % GROUP
    along_x = group < 2
    cell = jnp.where(
        along_x,
        jnp.where(group == 0, spot, (FX - 1) * FY + spot),
        jnp.where(group == 2, spot * FY, spot * FY + FY - 1),
    )
    length = jnp.where(along_x, FY, FX)
    return jnp.where((row == cell) & (spot < length), 1.0, 0.0).astype(jnp.bfloat16)


def exchanges():
    found = []
    for axis, base in EDGE_AXES:
        for parity in range(min(lax.axis_size(axis) - 1, 2)):
            found.append((axis, parity, base))
    return found


def group_of(axis, parity, base):
    ahead = lax.axis_index(axis) % 2 == parity
    return jnp.where(ahead, base + 1, base)


def pack(edges, group):
    rows = edges.shape[0] // 4
    lane_group = lax.broadcasted_iota(jnp.int32, (rows, LANES), 1) // GROUP
    packed = jnp.zeros((rows, LANES), jnp.float32)
    for part in range(4):
        piece = edges[part * rows : (part + 1) * rows]
        piece = pltpu.roll(piece, (part - group + 4) % 4 * GROUP, 1)
        packed = jnp.where(lane_group == part, piece, packed)
    return packed.astype(jnp.bfloat16)


def unpack(packed, group):
    lane_group = lax.broadcasted_iota(jnp.int32, packed.shape, 1) // GROUP
    pieces = []
    for part in range(4):
        piece = pltpu.roll(packed, (group - part + 4) % 4 * GROUP, 1)
        pieces.append(jnp.where(lane_group == group, piece, 0.0))
    return jnp.concatenate(pieces, axis=0)


def unit_of(round_number):
    return round_number - lax.axis_index("depth") + lax.axis_size("depth") - 1


def only_active(values, counts_ref, unit):
    position = lax.broadcasted_iota(jnp.int32, (SHOT_BATCH, values.shape[1]), 0)
    pieces = []
    for batch in range(values.shape[0] // SHOT_BATCH):
        piece = values[batch * SHOT_BATCH : (batch + 1) * SHOT_BATCH]
        pieces.append(jnp.where(position < counts_ref[unit, batch], piece, 0.0))
    return jnp.concatenate(pieces, axis=0)


def opening_kernel(swaps, arrival, source, assignment, counts, first_map, *outs):
    start0, later, edge_out = outs[0], outs[1], outs[2]
    messages = outs[3:]
    rounds, slots, cells = source.shape
    first_edge = dot(first_map[...], edge_selector(cells)).astype(jnp.bfloat16)
    edge_out[:cells] = first_edge
    shot = lax.broadcasted_iota(jnp.int32, (slots, slots), 0)
    slot = lax.broadcasted_iota(jnp.int32, (1, slots), 1)
    for round_number in range(rounds):
        unit = unit_of(round_number)
        live = jnp.zeros((1, slots), jnp.int32)
        for batch in range(slots // SHOT_BATCH):
            live = jnp.where(slot // SHOT_BATCH == batch, counts[unit, batch], live)
        wanted = jnp.where(
            slot % SHOT_BATCH < live, assignment[round_number : round_number + 1], -1
        )
        chosen = jnp.where(shot == wanted, 1.0, 0.0).astype(jnp.bfloat16)
        picked = dot_t(chosen, source[round_number])
        if round_number == 0:
            picked = picked + only_active(arrival[...].astype(jnp.float32), counts, unit)
        picked = picked.astype(jnp.bfloat16)
        edges = dot(picked, first_edge)
        if round_number == 0:
            start0[...] = picked
        else:
            later[round_number - 1] = picked
            at = cells + (round_number - 1) * slots
            edge_out[at : at + slots] = edges.astype(jnp.bfloat16)
            edges = jnp.where(lax.axis_index("depth") == 0, edges, 0.0)
        at = round_number * (slots // 4)
        for message, swap in zip(messages, swaps):
            message[at : at + slots // 4] = pack(edges, group_of(*swap))


def coupled_map_kernel(start0, first_map, second_map, mapped_out, second_ext, padded):
    cells = second_map.shape[0]
    margin = 32
    mapped_out[...] = dot(start0[...], first_map[...]).astype(jnp.bfloat16)
    width = second_map.shape[1]
    padded[:margin] = jnp.zeros((margin, width), jnp.float32)
    padded[margin + cells :] = jnp.zeros((margin, width), jnp.float32)
    padded[margin : margin + cells] = second_map[...].astype(jnp.float32)
    column = lax.broadcasted_iota(jnp.int32, (cells, 1), 0) % FY
    middle = padded[margin : margin + cells]
    sides = padded[margin - FY : margin - FY + cells] + padded[margin + FY : margin + FY + cells]
    sides += jnp.where(column > 0, padded[margin - 1 : margin - 1 + cells], 0.0)
    sides += jnp.where(column < FY - 1, padded[margin + 1 : margin + 1 + cells], 0.0)
    second_ext[:cells] = (middle + coupling_weight * sides).astype(jnp.bfloat16)
    edge_rows = dot_t(edge_selector(cells), second_map[...])
    second_ext[cells:] = (coupling_weight * edge_rows).astype(jnp.bfloat16)


def whole_map_kernel(first_map, second_ext, whole_ext):
    cells = first_map.shape[0]
    whole_ext[:cells] = dot(first_map[...], second_ext[:cells]).astype(jnp.bfloat16)
    whole_ext[cells:] = second_ext[cells:]


def step_kernel(swaps, round_number, last, *refs):
    refs = list(refs)
    traces, extra, map_ext, damping, counts = refs[:5]
    opened = refs[5 : 5 + len(swaps)]
    rest = refs[5 + len(swaps) :]
    received = [None] * len(swaps)
    if round_number > 0:
        received, rest = rest[: len(swaps)], rest[len(swaps) :]
    if not last:
        edge_next, rest = rest[0], rest[1:]
    traces_out = rest[0]
    messages = rest[1:]
    slots, cells = traces.shape
    unit = unit_of(round_number)
    halo = jnp.zeros((slots, LANES), jnp.float32)
    part = slots // 4
    for first, later, swap in zip(opened, received, swaps):
        message = first[round_number * part : (round_number + 1) * part].astype(jnp.float32)
        if later is not None:
            message = message + later[...].astype(jnp.float32)
        halo = halo + unpack(message, group_of(*swap))
    halo = only_active(halo, counts, unit).astype(jnp.bfloat16)
    if round_number == 0:
        start = extra[...].astype(jnp.float32)
        row = traces[...]
    else:
        row = (traces[...].astype(jnp.float32) + extra[...].astype(jnp.float32)).astype(
            jnp.bfloat16
        )
        start = row.astype(jnp.float32)
    image = dot(jnp.concatenate([row, halo], axis=1), map_ext[...])
    damp = damping[...]
    ended = (damp * image + (1.0 - damp) * start).astype(jnp.bfloat16)
    traces_out[...] = ended
    if not last:
        at = cells + round_number * slots
        edges = dot(ended, edge_next[:cells]) + edge_next[at : at + slots].astype(jnp.float32)
        for message, swap in zip(messages, swaps):
            message[...] = pack(edges, group_of(*swap))


def call(kernel, out_shape, operands, scalars=(), scratch=()):
    spaces = [pltpu.SMEM if i in scalars else pltpu.VMEM for i in range(len(operands))]
    return pl.pallas_call(
        kernel,
        out_shape=out_shape,
        in_specs=[pl.BlockSpec(memory_space=space) for space in spaces],
        out_specs=[pl.BlockSpec(memory_space=pltpu.VMEM)] * len(out_shape),
        scratch_shapes=scratch,
        compiler_params=pltpu.CompilerParams(vmem_limit_bytes=32 * 1024 * 1024),
    )(*operands)


MESH_AXES = ("depth", "gx", "gy")


def send(x, layers, down, swap=None):
    sizes = [lax.axis_size(axis) for axis in MESH_AXES]
    pairs = []
    for layer in layers:
        for i in range(sizes[1]):
            for j in range(sizes[2]):
                to = {"depth": layer + down, "gx": i, "gy": j}
                if swap is not None:
                    axis, parity, _ = swap
                    to[axis] += 1 if to[axis] % 2 == parity else -1
                spot = [to[axis] for axis in MESH_AXES]
                if all(0 <= s < size for s, size in zip(spot, sizes)):
                    here = (layer * sizes[1] + i) * sizes[2] + j
                    there = (spot[0] * sizes[1] + spot[1]) * sizes[2] + spot[2]
                    pairs.append((here, there))
    return lax.ppermute(x, MESH_AXES, pairs)


def local(arrival, source, assignment, counts, first_map, second_map, damping):
    layers = lax.axis_size("depth")
    slots, cells = arrival.shape[1], arrival.shape[4]
    rounds = source.shape[1]
    arrival = arrival[0, :, 0, 0, :]
    source = source[0, :, :, 0, 0, :]
    counts = counts[:, :, 0, 0]
    first_map = first_map[0, 0, 0]
    second_map = second_map[0, 0, 0]
    damping = damping[0, 0]
    swaps = exchanges()
    useful = [
        [layer for layer in range(layers) if layer - r <= layers - rounds] for r in range(rounds)
    ]

    def array(*shape):
        return jax.ShapeDtypeStruct(shape, jnp.bfloat16)

    message = array(slots // 4, LANES)
    opened = call(
        functools.partial(opening_kernel, swaps),
        [
            array(slots, cells),
            array(rounds - 1, slots, cells),
            array(cells + (rounds - 1) * slots, LANES),
        ]
        + [array(rounds * (slots // 4), LANES)] * len(swaps),
        [arrival, source, assignment, counts, first_map],
        scalars=(3,),
    )
    start0, later, edge = opened[:3]
    first_received = [send(m, useful[0], 0, swap) for m, swap in zip(opened[3:], swaps)]
    received = []
    edge_next = send(edge, range(1, layers), -1)
    mapped, second_ext = call(
        coupled_map_kernel,
        [array(slots, cells), array(cells + LANES, cells)],
        [start0, first_map, second_map],
        scratch=[pltpu.VMEM((cells + 64, cells), jnp.float32)],
    )
    traces, extra, map_ext = mapped, start0, second_ext
    for round_number in range(rounds):
        last = round_number == rounds - 1
        operands = [traces, extra, map_ext, damping, counts] + first_received + received
        outs = [array(slots, cells)]
        if not last:
            operands.append(edge_next)
            outs += [message] * len(swaps)
        ended = call(
            functools.partial(step_kernel, swaps, round_number, last), outs, operands, scalars=(4,)
        )
        traces = ended[0]
        if not last:
            traces = send(traces, useful[round_number], 1)
            received = [
                send(m, useful[round_number], 1, swap) for m, swap in zip(ended[1:], swaps)
            ]
            extra = later[round_number]
            if round_number == 0:
                (map_ext,) = call(
                    whole_map_kernel, [array(cells + LANES, cells)], [first_map, second_ext]
                )
    return traces.reshape(1, slots, 1, 1, cells)


def solution(mesh):
    return jax.shard_map(
        local,
        mesh=mesh,
        in_specs=(
            P("depth", None, "gx", "gy", None),
            P("depth", None, None, "gx", "gy", None),
            P(),
            P(None, None, "gx", "gy"),
            P("depth", "gx", "gy", None, None),
            P("depth", "gx", "gy", None, None),
            P("depth", "gx", "gy", None),
        ),
        out_specs=P("depth", None, "gx", "gy", None),
        check_vma=False,
    )
```

```python
import functools

import jax
import jax.numpy as jnp
from jax import lax
from jax.experimental import pallas as pl
from jax.experimental.pallas import tpu as pltpu
from jax.sharding import PartitionSpec as P

FX = 32
FY = 28
SHOT_BATCH = 16

coupling_weight = 0.25

LANES = 128
GROUP = LANES // 4
EDGE_AXES = (("gx", 0), ("gy", 2))


def dot(a, b):
    return jnp.dot(a, b, preferred_element_type=jnp.float32)


def dot_t(a, b):
    return lax.dot_general(a, b, (((0,), (0,)), ((), ())), preferred_element_type=jnp.float32)


def edge_selector(cells):
    row = lax.broadcasted_iota(jnp.int32, (cells, LANES), 0)
    lane = lax.broadcasted_iota(jnp.int32, (cells, LANES), 1)
    group = lane // GROUP
    spot = lane % GROUP
    along_x = group < 2
    cell = jnp.where(
        along_x,
        jnp.where(group == 0, spot, (FX - 1) * FY + spot),
        jnp.where(group == 2, spot * FY, spot * FY + FY - 1),
    )
    length = jnp.where(along_x, FY, FX)
    return jnp.where((row == cell) & (spot < length), 1.0, 0.0).astype(jnp.bfloat16)


def exchanges():
    found = []
    for axis, base in EDGE_AXES:
        for parity in range(min(lax.axis_size(axis) - 1, 2)):
            found.append((axis, parity, base))
    return found


def group_of(axis, parity, base):
    ahead = lax.axis_index(axis) % 2 == parity
    return jnp.where(ahead, base + 1, base)


def pack(edges, group):
    rows = edges.shape[0] // 4
    lane_group = lax.broadcasted_iota(jnp.int32, (rows, LANES), 1) // GROUP
    packed = jnp.zeros((rows, LANES), jnp.float32)
    for part in range(4):
        piece = edges[part * rows : (part + 1) * rows]
        piece = pltpu.roll(piece, (part - group + 4) % 4 * GROUP, 1)
        packed = jnp.where(lane_group == part, piece, packed)
    return packed.astype(jnp.bfloat16)


def unpack(packed, group):
    lane_group = lax.broadcasted_iota(jnp.int32, packed.shape, 1) // GROUP
    pieces = []
    for part in range(4):
        piece = pltpu.roll(packed, (group - part + 4) % 4 * GROUP, 1)
        pieces.append(jnp.where(lane_group == group, piece, 0.0))
    return jnp.concatenate(pieces, axis=0)


def unit_of(round_number):
    return round_number - lax.axis_index("depth") + lax.axis_size("depth") - 1


def opening_kernel(swaps, arrival, source, assignment, counts, first_map, *refs):
    starts_out, live_out, edge_out = refs[:3]
    messages = refs[3 : 3 + len(swaps)]
    arrival_in, source_in, assignment_in, counts_in, first_in, sems = refs[3 + len(swaps) :]
    rounds, slots, cells = source.shape
    pairs = [(counts, counts_in), (assignment, assignment_in), (first_map, first_in)]
    pairs += [(arrival, arrival_in)]
    pairs += [(source.at[r], source_in.at[r]) for r in range(rounds)]
    copies = [
        pltpu.make_async_copy(here, there, sems.at[i]) for i, (here, there) in enumerate(pairs)
    ]
    for copy in copies:
        copy.start()
    selector = edge_selector(cells)
    shot = lax.broadcasted_iota(jnp.int32, (slots, slots), 0)
    slot = lax.broadcasted_iota(jnp.int32, (1, slots), 1)
    position = lax.broadcasted_iota(jnp.int32, (SHOT_BATCH, LANES), 0)
    copies[0].wait()
    copies[1].wait()
    chosen = []
    for round_number in range(rounds):
        unit = unit_of(round_number)
        live = jnp.zeros((1, slots), jnp.int32)
        for batch in range(slots // SHOT_BATCH):
            count = counts_in[unit, 0, 0, batch]
            live = jnp.where(slot // SHOT_BATCH == batch, count, live)
            rows = slice(batch * SHOT_BATCH, (batch + 1) * SHOT_BATCH)
            live_out[round_number, rows] = jnp.where(position < count, 1.0, 0.0).astype(
                jnp.bfloat16
            )
        wanted = jnp.where(
            slot % SHOT_BATCH < live, assignment_in[round_number : round_number + 1], -1
        )
        chosen.append(jnp.where(shot == wanted, 1.0, 0.0).astype(jnp.bfloat16))
    copies[2].wait()
    first_edge = dot(first_in[...], selector).astype(jnp.bfloat16)
    edge_out[:cells] = first_edge
    copies[3].wait()
    for round_number in range(rounds):
        copies[4 + round_number].wait()
        picked = dot_t(chosen[round_number], source_in[round_number])
        if round_number == 0:
            live = live_out[0].astype(jnp.float32)
            live = jnp.concatenate([live] * (cells // LANES), axis=1)
            picked = picked + live * arrival_in[...].astype(jnp.float32)
        picked = picked.astype(jnp.bfloat16)
        starts_out[round_number] = picked
        edges = dot(picked, first_edge)
        if round_number > 0:
            at = cells + (round_number - 1) * slots
            edge_out[at : at + slots] = edges.astype(jnp.bfloat16)
            edges = jnp.where(lax.axis_index("depth") == 0, edges, 0.0)
        at = round_number * (slots // 4)
        for message, swap in zip(messages, swaps):
            message[at : at + slots // 4] = pack(edges, group_of(*swap))


def coupled_inside(mapped):
    cells = mapped.shape[1]
    lane = lax.broadcasted_iota(jnp.int32, (1, cells), 1)
    column = lane % FY
    around = jnp.where(lane >= FY, pltpu.roll(mapped, FY, 1), 0.0)
    around += jnp.where(lane < cells - FY, pltpu.roll(mapped, cells - FY, 1), 0.0)
    around += jnp.where(column > 0, pltpu.roll(mapped, 1, 1), 0.0)
    around += jnp.where(column < FY - 1, pltpu.roll(mapped, cells - 1, 1), 0.0)
    return mapped + coupling_weight * around


def fill_whole_map(first_map, second_map, whole_ext, padded):
    cells = second_map.shape[0]
    margin = 32
    width = second_map.shape[1]
    padded[:margin] = jnp.zeros((margin, width), jnp.float32)
    padded[margin + cells :] = jnp.zeros((margin, width), jnp.float32)
    padded[margin : margin + cells] = second_map[...].astype(jnp.float32)
    column = lax.broadcasted_iota(jnp.int32, (cells, 1), 0) % FY
    middle = padded[margin : margin + cells]
    sides = padded[margin - FY : margin - FY + cells] + padded[margin + FY : margin + FY + cells]
    sides += jnp.where(column > 0, padded[margin - 1 : margin - 1 + cells], 0.0)
    sides += jnp.where(column < FY - 1, padded[margin + 1 : margin + 1 + cells], 0.0)
    coupled = (middle + coupling_weight * sides).astype(jnp.bfloat16)
    whole_ext[:cells] = dot(first_map[...], coupled).astype(jnp.bfloat16)


def inside_kernel(early_layers, starts, first_map, second_map, image_out, whole_ext, padded):
    cells = second_map.shape[0]
    early = lax.axis_index("depth") < early_layers
    edge_rows = dot_t(edge_selector(cells), second_map[...])
    whole_ext[cells:] = (coupling_weight * edge_rows).astype(jnp.bfloat16)

    @pl.when(early)
    def _():
        slots = starts.shape[1]
        for chain in range(image_out.shape[0] // slots):
            mapped = dot(starts[chain], first_map[...]).astype(jnp.bfloat16).astype(jnp.float32)
            coupled = coupled_inside(mapped).astype(jnp.bfloat16)
            image_out[chain * slots : (chain + 1) * slots] = dot(coupled, second_map[...])

    @pl.when(jnp.logical_not(early))
    def _():
        fill_whole_map(first_map, second_map, whole_ext, padded)


def whole_map_kernel(early_layers, first_map, second_map, whole_in, whole_ext, padded):
    del whole_in

    @pl.when(lax.axis_index("depth") < early_layers)
    def _():
        fill_whole_map(first_map, second_map, whole_ext, padded)


def halo_of(messages, swaps, at, part, live):
    halo = 0.0
    for parts, swap in zip(messages, swaps):
        packed = 0.0
        for ref, row in zip(parts, at):
            packed = packed + ref[row : row + part].astype(jnp.float32)
        halo = halo + unpack(packed, group_of(*swap))
    return (halo * live.astype(jnp.float32)).astype(jnp.bfloat16)


def blend(image, start, damping):
    damp = damping[...]
    return (damp * image + (1.0 - damp) * start.astype(jnp.float32)).astype(jnp.bfloat16)


def step_kernel(swaps, step, chains, *refs):
    refs = list(refs)
    starts, live, map_ext, damping, edge_next, traces = refs[:6]
    received = refs[6 : 6 + len(swaps)]
    outs = refs[6 + len(swaps) :]
    slots, cells = starts.shape[1:]
    part = slots // 4
    for chain in range(chains):
        round_number = step + chain
        halo = halo_of(
            [[ref] for ref in received], swaps, [chain * part], part, live[round_number]
        )
        rows = slice(chain * slots, (chain + 1) * slots)
        start = starts[round_number]
        if step == 0:
            image = traces[rows] + dot(halo, map_ext[cells:])
        else:
            start = start.astype(jnp.float32) + traces[rows].astype(jnp.float32)
            start = start.astype(jnp.bfloat16)
            image = dot(jnp.concatenate([start, halo], axis=1), map_ext[...])
        ended = blend(image, start, damping)
        if chain < chains - 1:
            outs[0][rows] = ended
        else:
            outs[-1][...] = ended
        at = cells + round_number * slots
        edges = dot(ended, edge_next[:cells]) + edge_next[at : at + slots].astype(jnp.float32)
        messages = outs[len(outs) - 1 - len(swaps) : len(outs) - 1]
        for message, swap in zip(messages, swaps):
            message[chain * part : (chain + 1) * part] = pack(edges, group_of(*swap))


def final_kernel(swaps, starts, live, map_ext, damping, *refs):
    rounds, slots, cells = starts.shape
    phases = []
    refs = list(refs)
    for phase in range(rounds):
        traces = refs.pop(0) if phase > 0 else None
        phases.append((traces, refs[: len(swaps)]))
        refs = refs[len(swaps) :]
    traces_out, row = refs
    part = slots // 4
    layer = lax.axis_index("depth")
    for phase, (traces, messages) in enumerate(phases):
        here = layer >= phase if phase == rounds - 1 else layer == phase

        @pl.when(here)
        def _():
            at = [messages[0].shape[0] - part]
            halo = halo_of([[ref] for ref in messages], swaps, at, part, live[rounds - 1])
            start = starts[rounds - 1]
            if traces is not None:
                start = start.astype(jnp.float32) + traces[...].astype(jnp.float32)
                start = start.astype(jnp.bfloat16)
            row[:, :cells] = start
            row[:, cells:] = halo

    image = dot(row[...], map_ext[...])
    traces_out[...] = blend(image, row[:, :cells], damping)


def call(kernel, out_shape, operands, in_hbm=False, scratch=(), aliases=None):
    space = pl.ANY if in_hbm else pltpu.VMEM
    return pl.pallas_call(
        kernel,
        out_shape=out_shape,
        in_specs=[pl.BlockSpec(memory_space=space)] * len(operands),
        out_specs=[pl.BlockSpec(memory_space=pltpu.VMEM)] * len(out_shape),
        scratch_shapes=scratch,
        input_output_aliases=aliases or {},
        compiler_params=pltpu.CompilerParams(vmem_limit_bytes=32 * 1024 * 1024),
    )(*operands)


MESH_AXES = ("depth", "gx", "gy")


def send(x, layers, down, swap=None):
    sizes = [lax.axis_size(axis) for axis in MESH_AXES]
    pairs = []
    for layer in layers:
        for i in range(sizes[1]):
            for j in range(sizes[2]):
                to = {"depth": layer + down, "gx": i, "gy": j}
                if swap is not None:
                    axis, parity, _ = swap
                    to[axis] += 1 if to[axis] % 2 == parity else -1
                spot = [to[axis] for axis in MESH_AXES]
                if all(0 <= s < size for s, size in zip(spot, sizes)):
                    here = (layer * sizes[1] + i) * sizes[2] + j
                    there = (spot[0] * sizes[1] + spot[1]) * sizes[2] + spot[2]
                    pairs.append((here, there))
    return lax.ppermute(x, MESH_AXES, pairs)


def local(arrival, source, assignment, counts, first_map, second_map, damping):
    layers = lax.axis_size("depth")
    slots, cells = arrival.shape[1], arrival.shape[4]
    rounds = source.shape[1]
    arrival = arrival[0, :, 0, 0, :]
    source = source[0, :, :, 0, 0, :]
    counts = counts.transpose(0, 2, 3, 1)
    first_map = first_map[0, 0, 0]
    second_map = second_map[0, 0, 0]
    damping = damping[0, 0]
    swaps = exchanges()
    early_layers = layers - rounds + 1

    def array(*shape, kind=jnp.bfloat16):
        return jax.ShapeDtypeStruct(shape, kind)

    part = slots // 4
    opened = call(
        functools.partial(opening_kernel, swaps),
        [
            array(rounds, slots, cells),
            array(rounds, slots, LANES),
            array(cells + (rounds - 1) * slots, LANES),
        ]
        + [array(rounds * part, LANES)] * len(swaps),
        [arrival, source, assignment, counts, first_map],
        in_hbm=True,
        scratch=[
            pltpu.VMEM(arrival.shape, arrival.dtype),
            pltpu.VMEM(source.shape, source.dtype),
            pltpu.VMEM(assignment.shape, assignment.dtype),
            pltpu.SMEM(counts.shape, counts.dtype),
            pltpu.VMEM(first_map.shape, first_map.dtype),
            pltpu.SemaphoreType.DMA((4 + rounds,)),
        ],
    )
    starts, live, edge = opened[:3]
    received = [send(m, range(early_layers), 0, swap) for m, swap in zip(opened[3:], swaps)]
    edge_next = send(edge, range(1, layers), -1)
    padded = pltpu.VMEM((cells + 64, cells), jnp.float32)
    traces, map_ext = call(
        functools.partial(inside_kernel, early_layers),
        [array((rounds - 1) * slots, cells, kind=jnp.float32), array(cells + LANES, cells)],
        [starts, first_map, second_map],
        scratch=[padded],
    )
    arrived = [list(received)]
    for step in range(rounds - 1):
        chains = rounds - 1 - step
        outs = [array((chains - 1) * slots, cells)] if chains > 1 else []
        outs += [array(chains * part, LANES)] * len(swaps) + [array(slots, cells)]
        ended = call(
            functools.partial(step_kernel, swaps, step, chains),
            outs,
            [starts, live, map_ext, damping, edge_next, traces] + received,
        )
        below = range(step, step + early_layers)
        if chains > 1:
            traces = send(ended[0], below, 1)
        received = [send(m, below, 1, swap) for m, swap in zip(ended[-1 - len(swaps) : -1], swaps)]
        leaving = send(ended[-1], below if chains == 1 else [step], 1)
        arrived.append([leaving] + received)
        if step == 0:
            (map_ext,) = call(
                functools.partial(whole_map_kernel, early_layers),
                [array(cells + LANES, cells)],
                [first_map, second_map, map_ext],
                scratch=[padded],
                aliases={2: 0},
            )
    (ended,) = call(
        functools.partial(final_kernel, swaps),
        [array(slots, cells)],
        [starts, live, map_ext, damping] + [x for phase in arrived for x in phase],
        scratch=[pltpu.VMEM((slots, cells + LANES), jnp.bfloat16)],
    )
    return ended.reshape(1, slots, 1, 1, cells)


def solution(mesh):
    return jax.shard_map(
        local,
        mesh=mesh,
        in_specs=(
            P("depth", None, "gx", "gy", None),
            P("depth", None, None, "gx", "gy", None),
            P(),
            P(None, None, "gx", "gy"),
            P("depth", "gx", "gy", None, None),
            P("depth", "gx", "gy", None, None),
            P("depth", "gx", "gy", None),
        ),
        out_specs=P("depth", None, "gx", "gy", None),
        check_vma=False,
    )
```

```python
import functools

import jax
import jax.numpy as jnp
from jax import lax
from jax.experimental import pallas as pl
from jax.experimental.pallas import tpu as pltpu
from jax.sharding import PartitionSpec as P

FX = 32
FY = 28
SHOT_BATCH = 16

coupling_weight = 0.25

LANES = 128
GROUP = LANES // 4
EDGE_AXES = (("gx", 0), ("gy", 2))


def dot(a, b):
    return jnp.dot(a, b, preferred_element_type=jnp.float32)


def dot_t(a, b):
    return lax.dot_general(a, b, (((0,), (0,)), ((), ())), preferred_element_type=jnp.float32)


def edge_selector(cells):
    row = lax.broadcasted_iota(jnp.int32, (cells, LANES), 0)
    lane = lax.broadcasted_iota(jnp.int32, (cells, LANES), 1)
    group = lane // GROUP
    spot = lane % GROUP
    along_x = group < 2
    cell = jnp.where(
        along_x,
        jnp.where(group == 0, spot, (FX - 1) * FY + spot),
        jnp.where(group == 2, spot * FY, spot * FY + FY - 1),
    )
    length = jnp.where(along_x, FY, FX)
    return jnp.where((row == cell) & (spot < length), 1.0, 0.0).astype(jnp.bfloat16)


def exchanges():
    found = []
    for axis, base in EDGE_AXES:
        for parity in range(min(lax.axis_size(axis) - 1, 2)):
            found.append((axis, parity, base))
    return found


def group_of(axis, parity, base):
    ahead = lax.axis_index(axis) % 2 == parity
    return jnp.where(ahead, base + 1, base)


def pack(edges, group):
    rows = edges.shape[0] // 4
    lane_group = lax.broadcasted_iota(jnp.int32, (rows, LANES), 1) // GROUP
    packed = jnp.zeros((rows, LANES), jnp.float32)
    for part in range(4):
        piece = edges[part * rows : (part + 1) * rows]
        piece = pltpu.roll(piece, (part - group + 4) % 4 * GROUP, 1)
        packed = jnp.where(lane_group == part, piece, packed)
    return packed.astype(jnp.bfloat16)


def unpack(packed, group):
    lane_group = lax.broadcasted_iota(jnp.int32, packed.shape, 1) // GROUP
    pieces = []
    for part in range(4):
        piece = pltpu.roll(packed, (group - part + 4) % 4 * GROUP, 1)
        pieces.append(jnp.where(lane_group == group, piece, 0.0))
    return jnp.concatenate(pieces, axis=0)


def unit_of(round_number):
    return round_number - lax.axis_index("depth") + lax.axis_size("depth") - 1


def opening_kernel(swaps, arrival, source, assignment, counts, first_map, second_map, *refs):
    starts_out, live_out, edge_out, first_in, second_in = refs[:5]
    messages = refs[5 : 5 + len(swaps)]
    arrival_in, source_in, assignment_in, counts_in, sems = refs[5 + len(swaps) :]
    rounds, slots, cells = source.shape
    pairs = [(counts, counts_in), (assignment, assignment_in), (first_map, first_in)]
    pairs += [(arrival, arrival_in)]
    pairs += [(source.at[r], source_in.at[r]) for r in range(rounds)]
    pairs += [(second_map, second_in)]
    copies = [
        pltpu.make_async_copy(here, there, sems.at[i]) for i, (here, there) in enumerate(pairs)
    ]
    for copy in copies:
        copy.start()
    selector = edge_selector(cells)
    shot = lax.broadcasted_iota(jnp.int32, (slots, slots), 0)
    slot = lax.broadcasted_iota(jnp.int32, (1, slots), 1)
    position = lax.broadcasted_iota(jnp.int32, (SHOT_BATCH, LANES), 0)
    copies[0].wait()
    copies[1].wait()
    chosen = []
    for round_number in range(rounds):
        unit = unit_of(round_number)
        live = jnp.zeros((1, slots), jnp.int32)
        for batch in range(slots // SHOT_BATCH):
            count = counts_in[unit, 0, 0, batch]
            live = jnp.where(slot // SHOT_BATCH == batch, count, live)
            rows = slice(batch * SHOT_BATCH, (batch + 1) * SHOT_BATCH)
            live_out[round_number, rows] = jnp.where(position < count, 1.0, 0.0).astype(
                jnp.bfloat16
            )
        wanted = jnp.where(
            slot % SHOT_BATCH < live, assignment_in[round_number : round_number + 1], -1
        )
        chosen.append(jnp.where(shot == wanted, 1.0, 0.0).astype(jnp.bfloat16))
    copies[2].wait()
    first_edge = dot(first_in[...], selector).astype(jnp.bfloat16)
    edge_out[:cells] = first_edge
    copies[3].wait()
    for round_number in range(rounds):
        copies[4 + round_number].wait()
        picked = dot_t(chosen[round_number], source_in[round_number])
        if round_number == 0:
            live = live_out[0].astype(jnp.float32)
            live = jnp.concatenate([live] * (cells // LANES), axis=1)
            picked = picked + live * arrival_in[...].astype(jnp.float32)
        picked = picked.astype(jnp.bfloat16)
        starts_out[round_number] = picked
        edges = dot(picked, first_edge)
        if round_number > 0:
            at = cells + (round_number - 1) * slots
            edge_out[at : at + slots] = edges.astype(jnp.bfloat16)
            edges = jnp.where(lax.axis_index("depth") == 0, edges, 0.0)
        at = round_number * (slots // 4)
        for message, swap in zip(messages, swaps):
            message[at : at + slots // 4] = pack(edges, group_of(*swap))
    copies[-1].wait()


def coupled_inside(mapped):
    cells = mapped.shape[1]
    lane = lax.broadcasted_iota(jnp.int32, (1, cells), 1)
    column = lane % FY
    around = jnp.where(lane >= FY, pltpu.roll(mapped, FY, 1), 0.0)
    around += jnp.where(lane < cells - FY, pltpu.roll(mapped, cells - FY, 1), 0.0)
    around += jnp.where(column > 0, pltpu.roll(mapped, 1, 1), 0.0)
    around += jnp.where(column < FY - 1, pltpu.roll(mapped, cells - 1, 1), 0.0)
    return mapped + coupling_weight * around


def fill_whole_map(first_map, second_map, whole_ext, padded):
    cells = second_map.shape[0]
    margin = 32
    width = second_map.shape[1]
    padded[:margin] = jnp.zeros((margin, width), jnp.float32)
    padded[margin + cells :] = jnp.zeros((margin, width), jnp.float32)
    padded[margin : margin + cells] = second_map[...].astype(jnp.float32)
    column = lax.broadcasted_iota(jnp.int32, (cells, 1), 0) % FY
    middle = padded[margin : margin + cells]
    sides = padded[margin - FY : margin - FY + cells] + padded[margin + FY : margin + FY + cells]
    sides += jnp.where(column > 0, padded[margin - 1 : margin - 1 + cells], 0.0)
    sides += jnp.where(column < FY - 1, padded[margin + 1 : margin + 1 + cells], 0.0)
    coupled = (middle + coupling_weight * sides).astype(jnp.bfloat16)
    whole_ext[:cells] = dot(first_map[...], coupled).astype(jnp.bfloat16)


def inside_kernel(early_layers, starts, first_map, second_map, image_out, whole_ext, padded):
    cells = second_map.shape[0]
    early = lax.axis_index("depth") < early_layers
    edge_rows = dot_t(edge_selector(cells), second_map[...])
    whole_ext[cells:] = (coupling_weight * edge_rows).astype(jnp.bfloat16)

    @pl.when(early)
    def _():
        chains = image_out.shape[0] // starts.shape[1]
        mapped = dot(starts[:chains].reshape(-1, cells), first_map[...]).astype(jnp.bfloat16)
        coupled = coupled_inside(mapped.astype(jnp.float32)).astype(jnp.bfloat16)
        image_out[...] = dot(coupled, second_map[...])

    @pl.when(jnp.logical_not(early))
    def _():
        fill_whole_map(first_map, second_map, whole_ext, padded)


def whole_map_kernel(early_layers, first_map, second_map, whole_in, whole_ext, padded):
    del whole_in

    @pl.when(lax.axis_index("depth") < early_layers)
    def _():
        fill_whole_map(first_map, second_map, whole_ext, padded)


def halo_of(messages, swaps, at, part, live):
    halo = 0.0
    for parts, swap in zip(messages, swaps):
        packed = 0.0
        for ref, row in zip(parts, at):
            packed = packed + ref[row : row + part].astype(jnp.float32)
        halo = halo + unpack(packed, group_of(*swap))
    return (halo * live.astype(jnp.float32)).astype(jnp.bfloat16)


def blend(image, start, damping):
    damp = damping[...]
    return (damp * image + (1.0 - damp) * start.astype(jnp.float32)).astype(jnp.bfloat16)


def step_kernel(swaps, step, chains, *refs):
    refs = list(refs)
    starts, live, map_ext, damping, edge_next, traces = refs[:6]
    received = refs[6 : 6 + len(swaps)]
    outs = refs[6 + len(swaps) :]
    slots, cells = starts.shape[1:]
    part = slots // 4
    now = slice(step, step + chains)
    halo = [
        halo_of([[ref] for ref in received], swaps, [chain * part], part, live[step + chain])
        for chain in range(chains)
    ]
    halo = jnp.concatenate(halo, axis=0)
    start = starts[now].reshape(-1, cells)
    if step == 0:
        image = traces[...] + dot(halo, map_ext[cells:])
    else:
        start = start.astype(jnp.float32) + traces[...].astype(jnp.float32)
        start = start.astype(jnp.bfloat16)
        image = dot(jnp.concatenate([start, halo], axis=1), map_ext[...])
    ended = blend(image, start, damping)
    staying = (chains - 1) * slots
    if chains > 1:
        outs[0][...] = ended[:staying]
    outs[-1][...] = ended[staying:]
    at = cells + step * slots
    edges = dot(ended, edge_next[:cells])
    edges += edge_next[at : at + chains * slots].astype(jnp.float32)
    messages = outs[len(outs) - 1 - len(swaps) : len(outs) - 1]
    for message, swap in zip(messages, swaps):
        for chain in range(chains):
            message[chain * part : (chain + 1) * part] = pack(
                edges[chain * slots : (chain + 1) * slots], group_of(*swap)
            )


def final_kernel(swaps, starts, live, map_ext, damping, *refs):
    rounds, slots, cells = starts.shape
    phases = []
    refs = list(refs)
    for phase in range(rounds):
        traces = refs.pop(0) if phase > 0 else None
        phases.append((traces, refs[: len(swaps)]))
        refs = refs[len(swaps) :]
    traces_out, row = refs
    part = slots // 4
    layer = lax.axis_index("depth")
    for phase, (traces, messages) in enumerate(phases):
        here = layer >= phase if phase == rounds - 1 else layer == phase

        @pl.when(here)
        def _():
            at = [messages[0].shape[0] - part]
            halo = halo_of([[ref] for ref in messages], swaps, at, part, live[rounds - 1])
            start = starts[rounds - 1]
            if traces is not None:
                start = start.astype(jnp.float32) + traces[...].astype(jnp.float32)
                start = start.astype(jnp.bfloat16)
            row[:, :cells] = start
            row[:, cells:] = halo

    image = dot(row[...], map_ext[...])
    traces_out[...] = blend(image, row[:, :cells], damping)


def call(kernel, out_shape, operands, in_hbm=False, scratch=(), aliases=None):
    space = pltpu.HBM if in_hbm else pltpu.VMEM
    if in_hbm:
        operands = [pltpu.with_memory_space_constraint(x, pltpu.HBM) for x in operands]
    return pl.pallas_call(
        kernel,
        out_shape=out_shape,
        in_specs=[pl.BlockSpec(memory_space=space)] * len(operands),
        out_specs=[pl.BlockSpec(memory_space=pltpu.VMEM)] * len(out_shape),
        scratch_shapes=scratch,
        input_output_aliases=aliases or {},
        compiler_params=pltpu.CompilerParams(vmem_limit_bytes=32 * 1024 * 1024),
    )(*operands)


MESH_AXES = ("depth", "gx", "gy")


def send(x, layers, down, swap=None):
    sizes = [lax.axis_size(axis) for axis in MESH_AXES]
    pairs = []
    for layer in layers:
        for i in range(sizes[1]):
            for j in range(sizes[2]):
                to = {"depth": layer + down, "gx": i, "gy": j}
                if swap is not None:
                    axis, parity, _ = swap
                    to[axis] += 1 if to[axis] % 2 == parity else -1
                spot = [to[axis] for axis in MESH_AXES]
                if all(0 <= s < size for s, size in zip(spot, sizes)):
                    here = (layer * sizes[1] + i) * sizes[2] + j
                    there = (spot[0] * sizes[1] + spot[1]) * sizes[2] + spot[2]
                    pairs.append((here, there))
    return lax.ppermute(x, MESH_AXES, pairs)


def local(arrival, source, assignment, counts, first_map, second_map, damping):
    layers = lax.axis_size("depth")
    slots, cells = arrival.shape[1], arrival.shape[4]
    rounds = source.shape[1]
    arrival = arrival[0, :, 0, 0, :]
    source = source[0, :, :, 0, 0, :]
    counts = counts.transpose(0, 2, 3, 1)
    first_map = first_map[0, 0, 0]
    second_map = second_map[0, 0, 0]
    damping = damping[0, 0]
    swaps = exchanges()
    early_layers = layers - rounds + 1

    def array(*shape, kind=jnp.bfloat16):
        return jax.ShapeDtypeStruct(shape, kind)

    part = slots // 4
    opened = call(
        functools.partial(opening_kernel, swaps),
        [
            array(rounds, slots, cells),
            array(rounds, slots, LANES),
            array(cells + (rounds - 1) * slots, LANES),
            array(*first_map.shape),
            array(*second_map.shape),
        ]
        + [array(rounds * part, LANES)] * len(swaps),
        [arrival, source, assignment, counts, first_map, second_map],
        in_hbm=True,
        scratch=[
            pltpu.VMEM(arrival.shape, arrival.dtype),
            pltpu.VMEM(source.shape, source.dtype),
            pltpu.VMEM(assignment.shape, assignment.dtype),
            pltpu.SMEM(counts.shape, counts.dtype),
            pltpu.SemaphoreType.DMA((5 + rounds,)),
        ],
    )
    starts, live, edge, first_map, second_map = opened[:5]
    received = [send(m, range(early_layers), 0, swap) for m, swap in zip(opened[5:], swaps)]
    edge_next = send(edge, range(1, layers), -1)
    padded = pltpu.VMEM((cells + 64, cells), jnp.float32)
    traces, map_ext = call(
        functools.partial(inside_kernel, early_layers),
        [array((rounds - 1) * slots, cells, kind=jnp.float32), array(cells + LANES, cells)],
        [starts, first_map, second_map],
        scratch=[padded],
    )
    arrived = [list(received)]
    for step in range(rounds - 1):
        chains = rounds - 1 - step
        outs = [array((chains - 1) * slots, cells)] if chains > 1 else []
        outs += [array(chains * part, LANES)] * len(swaps) + [array(slots, cells)]
        ended = call(
            functools.partial(step_kernel, swaps, step, chains),
            outs,
            [starts, live, map_ext, damping, edge_next, traces] + received,
        )
        below = range(step, step + early_layers)
        if chains > 1:
            traces = send(ended[0], below, 1)
        received = [send(m, below, 1, swap) for m, swap in zip(ended[-1 - len(swaps) : -1], swaps)]
        leaving = send(ended[-1], below if chains == 1 else [step], 1)
        arrived.append([leaving] + received)
        if step == 0:
            (map_ext,) = call(
                functools.partial(whole_map_kernel, early_layers),
                [array(cells + LANES, cells)],
                [first_map, second_map, map_ext],
                scratch=[padded],
                aliases={2: 0},
            )
    (ended,) = call(
        functools.partial(final_kernel, swaps),
        [array(slots, cells)],
        [starts, live, map_ext, damping] + [x for phase in arrived for x in phase],
        scratch=[pltpu.VMEM((slots, cells + LANES), jnp.bfloat16)],
    )
    return ended.reshape(1, slots, 1, 1, cells)


def solution(mesh):
    return jax.shard_map(
        local,
        mesh=mesh,
        in_specs=(
            P("depth", None, "gx", "gy", None),
            P("depth", None, None, "gx", "gy", None),
            P(),
            P(None, None, "gx", "gy"),
            P("depth", "gx", "gy", None, None),
            P("depth", "gx", "gy", None, None),
            P("depth", "gx", "gy", None),
        ),
        out_specs=P("depth", None, "gx", "gy", None),
        check_vma=False,
    )
```

```python
import functools

import jax
import jax.numpy as jnp
import numpy as np
from jax import lax
from jax.experimental import pallas as pl
from jax.experimental.pallas import tpu as pltpu
from jax.sharding import PartitionSpec as P

FX = 32
FY = 28
SHOT_BATCH = 16

coupling_weight = 0.25

LANES = 128
GROUP = LANES // 4
EDGE_AXES = (("gx", 0), ("gy", 2))


def dot(a, b):
    return jnp.dot(a, b, preferred_element_type=jnp.float32)


def dot_t(a, b):
    return lax.dot_general(a, b, (((0,), (0,)), ((), ())), preferred_element_type=jnp.float32)


def edge_selector(cells):
    row = lax.broadcasted_iota(jnp.int32, (cells, LANES), 0)
    lane = lax.broadcasted_iota(jnp.int32, (cells, LANES), 1)
    group = lane // GROUP
    spot = lane % GROUP
    along_x = group < 2
    cell = jnp.where(
        along_x,
        jnp.where(group == 0, spot, (FX - 1) * FY + spot),
        jnp.where(group == 2, spot * FY, spot * FY + FY - 1),
    )
    length = jnp.where(along_x, FY, FX)
    return jnp.where((row == cell) & (spot < length), 1.0, 0.0).astype(jnp.bfloat16)


def exchanges():
    found = []
    for axis, base in EDGE_AXES:
        for parity in range(min(lax.axis_size(axis) - 1, 2)):
            found.append((axis, parity, base))
    return found[::-1]


def group_of(axis, parity, base):
    ahead = lax.axis_index(axis) % 2 == parity
    return jnp.where(ahead, base + 1, base)


def pack(edges, group):
    rows = edges.shape[0] // 4
    lane_group = lax.broadcasted_iota(jnp.int32, (rows, LANES), 1) // GROUP
    packed = jnp.zeros((rows, LANES), jnp.float32)
    for part in range(4):
        piece = edges[part * rows : (part + 1) * rows]
        piece = pltpu.roll(piece, (part - group + 4) % 4 * GROUP, 1)
        packed = jnp.where(lane_group == part, piece, packed)
    return packed.astype(jnp.bfloat16)


def unpack(packed, group):
    lane_group = lax.broadcasted_iota(jnp.int32, packed.shape, 1) // GROUP
    pieces = []
    for part in range(4):
        piece = pltpu.roll(packed, (group - part + 4) % 4 * GROUP, 1)
        pieces.append(jnp.where(lane_group == group, piece, 0.0))
    return jnp.concatenate(pieces, axis=0)


def unit_of(round_number):
    return round_number - lax.axis_index("depth") + lax.axis_size("depth") - 1


def opening_kernel(swaps, arrival, source, assignment, counts, first_map, band, *refs):
    starts_out, live_out, edge_out, first_in, band_in = refs[:5]
    messages = refs[5 : 5 + len(swaps)]
    arrival_in, source_in, assignment_in, counts_in, sems = refs[5 + len(swaps) :]
    rounds, slots, cells = source.shape
    pairs = [(counts, counts_in), (assignment, assignment_in), (first_map, first_in)]
    pairs += [(arrival, arrival_in)]
    pairs += [(source.at[r], source_in.at[r]) for r in range(rounds)]
    pairs += [(band, band_in)]
    copies = [
        pltpu.make_async_copy(here, there, sems.at[i]) for i, (here, there) in enumerate(pairs)
    ]
    for copy in copies:
        copy.start()
    selector = edge_selector(cells)
    shot = lax.broadcasted_iota(jnp.int32, (slots, slots), 0)
    slot = lax.broadcasted_iota(jnp.int32, (1, slots), 1)
    position = lax.broadcasted_iota(jnp.int32, (SHOT_BATCH, LANES), 0)
    copies[0].wait()
    copies[1].wait()
    chosen = []
    for round_number in range(rounds):
        unit = unit_of(round_number)
        live = jnp.zeros((1, slots), jnp.int32)
        for batch in range(slots // SHOT_BATCH):
            count = counts_in[unit, 0, 0, batch]
            live = jnp.where(slot // SHOT_BATCH == batch, count, live)
            rows = slice(batch * SHOT_BATCH, (batch + 1) * SHOT_BATCH)
            live_out[round_number, rows] = jnp.where(position < count, 1.0, 0.0).astype(
                jnp.bfloat16
            )
        wanted = jnp.where(
            slot % SHOT_BATCH < live, assignment_in[round_number : round_number + 1], -1
        )
        chosen.append(jnp.where(shot == wanted, 1.0, 0.0).astype(jnp.bfloat16))
    copies[2].wait()
    first_edge = dot(first_in[...], selector).astype(jnp.bfloat16)
    edge_out[:cells] = first_edge
    copies[3].wait()
    for round_number in range(rounds):
        copies[4 + round_number].wait()
        picked = dot_t(chosen[round_number], source_in[round_number])
        if round_number == 0:
            live = live_out[0].astype(jnp.float32)
            live = jnp.concatenate([live] * (cells // LANES), axis=1)
            picked = picked + live * arrival_in[...].astype(jnp.float32)
        picked = picked.astype(jnp.bfloat16)
        starts_out[round_number] = picked
        edges = dot(picked, first_edge)
        if round_number > 0:
            at = cells + (round_number - 1) * slots
            edge_out[at : at + slots] = edges.astype(jnp.bfloat16)
            edges = jnp.where(lax.axis_index("depth") == 0, edges, 0.0)
        at = round_number * (slots // 4)
        for message, swap in zip(messages, swaps):
            message[at : at + slots // 4] = pack(edges, group_of(*swap))
    copies[-1].wait()


def bands(cells):
    found = []
    for at in range(0, cells, 2 * LANES):
        end = min(at + 2 * LANES, cells)
        found.append((slice(max(at - LANES, 0), min(end + LANES, cells)), slice(at, end)))
    return found


def coupling_band(cells):
    cell = np.arange(cells)
    apart = np.abs(cell[:, None] - cell[None, :])
    same_row = cell[:, None] // FY == cell[None, :] // FY
    linked = (apart == FY) | ((apart == 1) & same_row)
    coupling = np.eye(cells) + coupling_weight * linked
    band = np.zeros((len(bands(cells)), 4 * LANES, 2 * LANES), np.float32)
    for block, (rows, columns) in zip(band, bands(cells)):
        piece = coupling[rows, columns]
        block[: piece.shape[0], : piece.shape[1]] = piece
    return jnp.asarray(band, jnp.bfloat16)


def coupled(x, band):
    pieces = []
    for at, (rows, columns) in enumerate(bands(x.shape[1])):
        height, width = rows.stop - rows.start, columns.stop - columns.start
        pieces.append(dot(x[:, rows], band[at, :height, :width]).astype(jnp.bfloat16))
    return jnp.concatenate(pieces, axis=1)


def fill_whole_map(first_map, band, second_map, whole_ext):
    cells = second_map.shape[0]
    whole_ext[:cells] = dot(coupled(first_map[...], band), second_map[...]).astype(jnp.bfloat16)


def inside_kernel(early_layers, starts, first_map, band, second_map, *refs):
    image_out, whole_ext, second_in, sem = refs
    cells = second_map.shape[0]
    early = lax.axis_index("depth") < early_layers
    copy = pltpu.make_async_copy(second_map, second_in, sem)
    copy.start()

    @pl.when(early)
    def _():
        chains = image_out.shape[0] // starts.shape[1]
        mapped = dot(starts[:chains].reshape(-1, cells), first_map[...]).astype(jnp.bfloat16)
        image_out[...] = coupled(mapped, band).astype(jnp.float32)

    copy.wait()

    @pl.when(early)
    def _():
        image_out[...] = dot(image_out[...].astype(jnp.bfloat16), second_in[...])

    @pl.when(jnp.logical_not(early))
    def _():
        fill_whole_map(first_map, band, second_in, whole_ext)

    edge_rows = dot_t(edge_selector(cells), second_in[...])
    whole_ext[cells:] = (coupling_weight * edge_rows).astype(jnp.bfloat16)


def whole_map_kernel(early_layers, first_map, band, second_map, whole_in, whole_ext):
    del whole_in

    @pl.when(lax.axis_index("depth") < early_layers)
    def _():
        fill_whole_map(first_map, band, second_map, whole_ext)


def halo_of(messages, swaps, at, part, live):
    halo = 0.0
    for parts, swap in zip(messages, swaps):
        packed = 0.0
        for ref, row in zip(parts, at):
            packed = packed + ref[row : row + part].astype(jnp.float32)
        halo = halo + unpack(packed, group_of(*swap))
    return (halo * live.astype(jnp.float32)).astype(jnp.bfloat16)


def blend(image, start, damping):
    damp = damping[...]
    return (damp * image + (1.0 - damp) * start.astype(jnp.float32)).astype(jnp.bfloat16)


def step_kernel(swaps, step, chains, *refs):
    refs = list(refs)
    starts, live, map_ext, damping, edge_next, traces = refs[:6]
    received = refs[6 : 6 + len(swaps)]
    others, outs = refs[6 + len(swaps) : -len(swaps) - 1], refs[-len(swaps) - 1 :]
    if chains > 1:
        others, outs = others[:-1], others[-1:] + outs
    slots, cells = starts.shape[1:]
    part = slots // 4
    now = slice(step, step + chains)
    halo = [
        halo_of([[ref] for ref in received], swaps, [chain * part], part, live[step + chain])
        for chain in range(chains)
    ]
    halo = jnp.concatenate(halo, axis=0)
    start = starts[now].reshape(-1, cells)
    if step == 0:
        image = traces[...] + dot(halo, map_ext[cells:])
    else:
        start = start.astype(jnp.float32) + traces[...].astype(jnp.float32)
        start = start.astype(jnp.bfloat16)
        image = dot(jnp.concatenate([start, halo], axis=1), map_ext[...])
    ended = blend(image, start, damping)
    staying = (chains - 1) * slots
    if chains > 1:
        outs[0][...] = ended[:staying]
    outs[-1][...] = ended[staying:]
    for layer, other in enumerate(others):

        @pl.when(lax.axis_index("depth") == layer)
        def _():
            outs[-1][...] = other[...]

    at = cells + step * slots
    edges = dot(ended, edge_next[:cells])
    edges += edge_next[at : at + chains * slots].astype(jnp.float32)
    messages = outs[len(outs) - 1 - len(swaps) : len(outs) - 1]
    for message, swap in zip(messages, swaps):
        for chain in range(chains):
            message[chain * part : (chain + 1) * part] = pack(
                edges[chain * slots : (chain + 1) * slots], group_of(*swap)
            )


def final_kernel(swaps, starts, live, map_ext, damping, traces, *refs):
    rounds, slots, cells = starts.shape
    received, (traces_out, row) = refs[:-2], refs[-2:]
    part = slots // 4
    layer = lax.axis_index("depth")
    start = starts[rounds - 1].astype(jnp.float32) + traces[...].astype(jnp.float32)
    row[:, :cells] = start.astype(jnp.bfloat16)
    for phase in range(rounds):
        messages = received[phase * len(swaps) : (phase + 1) * len(swaps)]

        @pl.when(layer >= phase if phase == rounds - 1 else layer == phase)
        def _():
            at = [messages[0].shape[0] - part]
            row[:, cells:] = halo_of([[ref] for ref in messages], swaps, at, part, live[rounds - 1])

    image = dot(row[...], map_ext[...])
    traces_out[...] = blend(image, row[:, :cells], damping)


def call(kernel, out_shape, operands, in_hbm=(), scratch=(), aliases=None):
    spaces = [pltpu.HBM if i in in_hbm else pltpu.VMEM for i in range(len(operands))]
    operands = [
        pltpu.with_memory_space_constraint(x, pltpu.HBM) if i in in_hbm else x
        for i, x in enumerate(operands)
    ]
    return pl.pallas_call(
        kernel,
        out_shape=out_shape,
        in_specs=[pl.BlockSpec(memory_space=space) for space in spaces],
        out_specs=[pl.BlockSpec(memory_space=pltpu.VMEM)] * len(out_shape),
        scratch_shapes=scratch,
        input_output_aliases=aliases or {},
        compiler_params=pltpu.CompilerParams(vmem_limit_bytes=32 * 1024 * 1024),
    )(*operands)


MESH_AXES = ("depth", "gx", "gy")


def send(x, layers, down, swap=None):
    sizes = [lax.axis_size(axis) for axis in MESH_AXES]
    pairs = []
    for layer in layers:
        for i in range(sizes[1]):
            for j in range(sizes[2]):
                to = {"depth": layer + down, "gx": i, "gy": j}
                if swap is not None:
                    axis, parity, _ = swap
                    to[axis] += 1 if to[axis] % 2 == parity else -1
                spot = [to[axis] for axis in MESH_AXES]
                if all(0 <= s < size for s, size in zip(spot, sizes)):
                    here = (layer * sizes[1] + i) * sizes[2] + j
                    there = (spot[0] * sizes[1] + spot[1]) * sizes[2] + spot[2]
                    pairs.append((here, there))
    return lax.ppermute(x, MESH_AXES, pairs)


def local(arrival, source, assignment, counts, first_map, second_map, damping):
    layers = lax.axis_size("depth")
    slots, cells = arrival.shape[1], arrival.shape[4]
    rounds = source.shape[1]
    arrival = arrival[0, :, 0, 0, :]
    source = source[0, :, :, 0, 0, :]
    counts = counts.transpose(0, 2, 3, 1)
    first_map = first_map[0, 0, 0]
    second_map = second_map[0, 0, 0]
    damping = damping[0, 0]
    swaps = exchanges()
    early_layers = layers - rounds + 1

    def array(*shape, kind=jnp.bfloat16):
        return jax.ShapeDtypeStruct(shape, kind)

    part = slots // 4
    band = coupling_band(cells)
    opened = call(
        functools.partial(opening_kernel, swaps),
        [
            array(rounds, slots, cells),
            array(rounds, slots, LANES),
            array(cells + (rounds - 1) * slots, LANES),
            array(*first_map.shape),
            array(*band.shape),
        ]
        + [array(rounds * part, LANES)] * len(swaps),
        [arrival, source, assignment, counts, first_map, band],
        in_hbm=range(6),
        scratch=[
            pltpu.VMEM(arrival.shape, arrival.dtype),
            pltpu.VMEM(source.shape, source.dtype),
            pltpu.VMEM(assignment.shape, assignment.dtype),
            pltpu.SMEM(counts.shape, counts.dtype),
            pltpu.SemaphoreType.DMA((5 + rounds,)),
        ],
    )
    starts, live, edge, first_map, band = opened[:5]
    received = [send(m, range(early_layers), 0, swap) for m, swap in zip(opened[5:], swaps)]
    edge_next = send(edge, range(1, layers), -1)
    image = array((rounds - 1) * slots, cells, kind=jnp.float32)
    traces, map_ext, second_map = call(
        functools.partial(inside_kernel, early_layers),
        [image, array(cells + LANES, cells), array(*second_map.shape)],
        [starts, first_map, band, second_map],
        in_hbm=(3,),
        scratch=[pltpu.SemaphoreType.DMA],
    )
    arrived = list(received)
    kept = []
    for step in range(rounds - 1):
        chains = rounds - 1 - step
        outs = [array((chains - 1) * slots, cells)] if chains > 1 else []
        outs += [array(chains * part, LANES)] * len(swaps) + [array(slots, cells)]
        operands = [starts, live, map_ext, damping, edge_next, traces] + received
        ended = call(
            functools.partial(step_kernel, swaps, step, chains),
            outs,
            operands + (kept if chains == 1 else []),
        )
        below = range(step, step + early_layers)
        if chains > 1:
            traces = send(ended[0], below, 1)
            kept.append(ended[-1])
        else:
            traces = send(ended[-1], range(layers - 1), 1)
        received = [send(m, below, 1, swap) for m, swap in zip(ended[-1 - len(swaps) : -1], swaps)]
        arrived += received
        if step == 0:
            (map_ext,) = call(
                functools.partial(whole_map_kernel, early_layers),
                [array(cells + LANES, cells)],
                [first_map, band, second_map, map_ext],
                aliases={3: 0},
            )
    (ended,) = call(
        functools.partial(final_kernel, swaps),
        [array(slots, cells)],
        [starts, live, map_ext, damping, traces] + arrived,
        scratch=[pltpu.VMEM((slots, cells + LANES), jnp.bfloat16)],
    )
    return ended.reshape(1, slots, 1, 1, cells)


def solution(mesh):
    return jax.shard_map(
        local,
        mesh=mesh,
        in_specs=(
            P("depth", None, "gx", "gy", None),
            P("depth", None, None, "gx", "gy", None),
            P(),
            P(None, None, "gx", "gy"),
            P("depth", "gx", "gy", None, None),
            P("depth", "gx", "gy", None, None),
            P("depth", "gx", "gy", None),
        ),
        out_specs=P("depth", None, "gx", "gy", None),
        check_vma=False,
    )
```

```python
import functools

import jax
import jax.numpy as jnp
import numpy as np
from jax import lax
from jax.experimental import pallas as pl
from jax.experimental.pallas import tpu as pltpu
from jax.sharding import PartitionSpec as P

FX = 32
FY = 28
SHOT_BATCH = 16

coupling_weight = 0.25

LANES = 128
GROUP = LANES // 4
EDGE_AXES = (("gx", 0), ("gy", 2))


def dot(a, b):
    return jnp.dot(a, b, preferred_element_type=jnp.float32)


def dot_t(a, b):
    return lax.dot_general(a, b, (((0,), (0,)), ((), ())), preferred_element_type=jnp.float32)


def edge_selector(cells):
    row = lax.broadcasted_iota(jnp.int32, (cells, LANES), 0)
    lane = lax.broadcasted_iota(jnp.int32, (cells, LANES), 1)
    group = lane // GROUP
    spot = lane % GROUP
    along_x = group < 2
    cell = jnp.where(
        along_x,
        jnp.where(group == 0, spot, (FX - 1) * FY + spot),
        jnp.where(group == 2, spot * FY, spot * FY + FY - 1),
    )
    length = jnp.where(along_x, FY, FX)
    return jnp.where((row == cell) & (spot < length), 1.0, 0.0).astype(jnp.bfloat16)


def exchanges():
    found = []
    for axis, base in EDGE_AXES:
        for parity in range(min(lax.axis_size(axis) - 1, 2)):
            found.append((axis, parity, base))
    return found[::-1]


def group_of(axis, parity, base):
    ahead = lax.axis_index(axis) % 2 == parity
    return jnp.where(ahead, base + 1, base)


def pack(edges, group):
    rows = edges.shape[0] // 4
    lane_group = lax.broadcasted_iota(jnp.int32, (rows, LANES), 1) // GROUP
    packed = jnp.zeros((rows, LANES), jnp.float32)
    for part in range(4):
        piece = edges[part * rows : (part + 1) * rows]
        piece = pltpu.roll(piece, (part - group + 4) % 4 * GROUP, 1)
        packed = jnp.where(lane_group == part, piece, packed)
    return packed.astype(jnp.bfloat16)


def unpack(packed, group):
    lane_group = lax.broadcasted_iota(jnp.int32, packed.shape, 1) // GROUP
    pieces = []
    for part in range(4):
        piece = pltpu.roll(packed, (group - part + 4) % 4 * GROUP, 1)
        pieces.append(jnp.where(lane_group == group, piece, 0.0))
    return jnp.concatenate(pieces, axis=0)


def unit_of(round_number):
    return round_number - lax.axis_index("depth") + lax.axis_size("depth") - 1


def chosen_of(wanted, counts_in, round_number):
    slots = wanted.shape[1]
    shot = lax.broadcasted_iota(jnp.int32, (slots, slots), 0)
    slot = lax.broadcasted_iota(jnp.int32, (1, slots), 1)
    live = jnp.zeros((1, slots), jnp.int32)
    for batch in range(slots // SHOT_BATCH):
        count = counts_in[unit_of(round_number), 0, 0, batch]
        live = jnp.where(slot // SHOT_BATCH == batch, count, live)
    wanted = jnp.where(slot % SHOT_BATCH < live, wanted, -1)
    return jnp.where(shot == wanted, 1.0, 0.0).astype(jnp.bfloat16)


def opening_kernel(swaps, arrival, source, assignment, counts, first_map, band, *refs):
    first_out, later_out, live_out, edge_out, own_edge, first_in, band_in = refs[:7]
    messages = refs[7 : 7 + len(swaps)]
    arrival_in, source_in, assignment_in, counts_in, sems = refs[7 + len(swaps) :]
    rounds, slots, cells = source.shape
    part = slots // 4
    soon = first_out.shape[0]
    upper = lax.axis_index("depth") == 0
    pairs = [(counts, counts_in), (assignment, assignment_in), (first_map, first_in)]
    pairs += [(arrival, arrival_in)]
    pairs += [(source.at[r], source_in.at[r]) for r in range(soon)]
    pairs += [(band, band_in), (source.at[pl.ds(soon, 2)], source_in.at[pl.ds(soon, 2)])]
    copies = [
        pltpu.make_async_copy(here, there, sems.at[i]) for i, (here, there) in enumerate(pairs)
    ]
    for copy in copies[:-1]:
        copy.start()

    @pl.when(jnp.logical_not(upper))
    def _():
        copies[-1].start()

    selector = edge_selector(cells)
    position = lax.broadcasted_iota(jnp.int32, (SHOT_BATCH, LANES), 0)
    copies[0].wait()
    for round_number in range(rounds):
        for batch in range(slots // SHOT_BATCH):
            count = counts_in[unit_of(round_number), 0, 0, batch]
            rows = slice(batch * SHOT_BATCH, (batch + 1) * SHOT_BATCH)
            live_out[round_number, rows] = jnp.where(position < count, 1.0, 0.0).astype(
                jnp.bfloat16
            )
    copies[1].wait()
    chosen = [chosen_of(assignment_in[r : r + 1], counts_in, r) for r in range(soon)]
    copies[2].wait()
    first_edge = dot(first_in[...], selector).astype(jnp.bfloat16)
    edge_out[:cells] = first_edge
    own_edge[...] = first_edge
    copies[3].wait()
    for round_number in range(soon):
        copies[4 + round_number].wait()
        picked = dot_t(chosen[round_number], source_in[round_number])
        if round_number == 0:
            live = live_out[0].astype(jnp.float32)
            live = jnp.concatenate([live] * (cells // LANES), axis=1)
            picked = picked + live * arrival_in[...].astype(jnp.float32)
        picked = picked.astype(jnp.bfloat16)
        first_out[round_number] = picked
        edges = dot(picked, first_edge)
        if round_number > 0:
            at = cells + (round_number - 1) * slots
            edge_out[at : at + slots] = edges.astype(jnp.bfloat16)
        for message, swap in zip(messages, swaps):
            message[round_number * part : (round_number + 1) * part] = pack(edges, group_of(*swap))
    copies[4 + soon].wait()

    @pl.when(jnp.logical_not(upper))
    def _():
        copies[-1].wait()
        for at, round_number in enumerate(range(soon, rounds)):
            chosen = chosen_of(assignment_in[round_number : round_number + 1], counts_in, round_number)
            picked = dot_t(chosen, source_in[round_number]).astype(jnp.bfloat16)
            later_out[at] = picked
            row = cells + (round_number - 1) * slots
            edge_out[row : row + slots] = dot(picked, own_edge[...]).astype(jnp.bfloat16)


def bands(cells):
    found = []
    for at in range(0, cells, 2 * LANES):
        end = min(at + 2 * LANES, cells)
        found.append((slice(max(at - LANES, 0), min(end + LANES, cells)), slice(at, end)))
    return found


def coupling_band(cells):
    cell = np.arange(cells)
    apart = np.abs(cell[:, None] - cell[None, :])
    same_row = cell[:, None] // FY == cell[None, :] // FY
    linked = (apart == FY) | ((apart == 1) & same_row)
    coupling = np.eye(cells) + coupling_weight * linked
    band = np.zeros((len(bands(cells)), 4 * LANES, 2 * LANES), np.float32)
    for block, (rows, columns) in zip(band, bands(cells)):
        piece = coupling[rows, columns]
        block[: piece.shape[0], : piece.shape[1]] = piece
    return jnp.asarray(band, jnp.bfloat16)


def coupled(x, band):
    pieces = []
    for at, (rows, columns) in enumerate(bands(x.shape[1])):
        height, width = rows.stop - rows.start, columns.stop - columns.start
        pieces.append(dot(x[:, rows], band[at, :height, :width]).astype(jnp.bfloat16))
    return jnp.concatenate(pieces, axis=1)


def fill_whole_map(first_map, band, second_map, whole_ext):
    cells = second_map.shape[0]
    whole_ext[:cells] = dot(coupled(first_map[...], band), second_map[...]).astype(jnp.bfloat16)


def coupled_kernel(early_layers, first, first_map, band, edge_in, coupled_out, edge_out):
    del edge_in, edge_out

    @pl.when(lax.axis_index("depth") < early_layers)
    def _():
        cells = first_map.shape[0]
        mapped = dot(first[...].reshape(-1, cells), first_map[...]).astype(jnp.bfloat16)
        coupled_out[...] = coupled(mapped, band)


def image_kernel(early_layers, inner, first_map, band, second_map, *refs):
    image_out, whole_ext, second_in, sem = refs
    cells = second_map.shape[0]
    early = lax.axis_index("depth") < early_layers
    copy = pltpu.make_async_copy(second_map, second_in, sem)
    copy.start()
    selector = edge_selector(cells)
    copy.wait()

    @pl.when(early)
    def _():
        image_out[...] = dot(inner[...], second_in[...])

    @pl.when(jnp.logical_not(early))
    def _():
        fill_whole_map(first_map, band, second_in, whole_ext)

    edge_rows = dot_t(selector, second_in[...])
    whole_ext[cells:] = (coupling_weight * edge_rows).astype(jnp.bfloat16)


def late_kernel(early_layers, swaps, source, assignment, counts, *refs):
    first_map, band, second_map, own_edge, _, _, whole_ext, later_out = refs[:8]
    messages = refs[8 : 8 + len(swaps)]
    source_in, assignment_in, counts_in, sems = refs[8 + len(swaps) :]
    rounds, slots, cells = source.shape
    part = slots // 4
    layer = lax.axis_index("depth")
    pairs = [(counts, counts_in), (assignment, assignment_in)]
    pairs += [(source.at[pl.ds(rounds - 2, 2)], source_in)]
    copies = [
        pltpu.make_async_copy(here, there, sems.at[i]) for i, (here, there) in enumerate(pairs)
    ]

    @pl.when(layer == 0)
    def _():
        for copy in copies:
            copy.start()
        for copy in copies:
            copy.wait()
        for at, round_number in enumerate(range(rounds - 2, rounds)):
            chosen = chosen_of(assignment_in[round_number : round_number + 1], counts_in, round_number)
            picked = dot_t(chosen, source_in[at]).astype(jnp.bfloat16)
            later_out[at] = picked
            edges = dot(picked, own_edge[...])
            for message, swap in zip(messages, swaps):
                message[at * part : (at + 1) * part] = pack(edges, group_of(*swap))

    @pl.when(layer < early_layers)
    def _():
        fill_whole_map(first_map, band, second_map, whole_ext)


def halo_of(messages, swaps, at, part, live):
    halo = 0.0
    for parts, swap in zip(messages, swaps):
        packed = 0.0
        for ref, row in zip(parts, at):
            packed = packed + ref[row : row + part].astype(jnp.float32)
        halo = halo + unpack(packed, group_of(*swap))
    return (halo * live.astype(jnp.float32)).astype(jnp.bfloat16)


def blend(image, start, damping):
    damp = damping[...]
    return (damp * image + (1.0 - damp) * start.astype(jnp.float32)).astype(jnp.bfloat16)


def rounds_of(first, later, begin, end):
    soon = first.shape[0]
    found = [first[r] if r < soon else later[r - soon] for r in range(begin, end)]
    return jnp.concatenate(found, axis=0)


def step_kernel(swaps, step, chains, keeps, waiting, *refs):
    first, later, live, map_ext, damping, edge_next, traces = refs[:7]
    received = refs[7 : 7 + len(swaps)]
    others = refs[7 + len(swaps) :]
    messages, others = others[-len(swaps) :], others[: -len(swaps)]
    kept_out = None
    if keeps:
        kept_out, others = others[-1], others[:-1]
    traces_out, others = others[-1], others[:-1]
    slots, cells = first.shape[1:]
    part = slots // 4
    halo = [
        halo_of([[ref] for ref in received], swaps, [chain * part], part, live[step + chain])
        for chain in range(chains)
    ]
    halo = jnp.concatenate(halo, axis=0)
    start = rounds_of(first, later, step, step + chains)
    if step == 0:
        image = traces[...] + dot(halo, map_ext[cells:])
    else:
        start = start.astype(jnp.float32) + traces[...].astype(jnp.float32)
        start = start.astype(jnp.bfloat16)
        image = dot(jnp.concatenate([start, halo], axis=1), map_ext[...])
    ended = blend(image, start, damping)
    going = (chains - 1 if keeps else chains) * slots
    traces_out[...] = ended[:going]
    if keeps:
        kept_out[...] = ended[going:]
    at = cells + step * slots
    edges = dot(ended, edge_next[:cells])
    edges += edge_next[at : at + chains * slots].astype(jnp.float32)
    for message, swap in zip(messages, swaps):
        for chain in range(chains):
            message[chain * part : (chain + 1) * part] = pack(
                edges[chain * slots : (chain + 1) * slots], group_of(*swap)
            )
    layer = lax.axis_index("depth")
    if waiting:

        @pl.when(layer == 0)
        def _():
            for message, other in zip(messages, others):
                message[...] = other[...]

    else:
        for at, other in enumerate(others):

            @pl.when(layer == at + 1)
            def _():
                traces_out[...] = other[...]


def final_kernel(swaps, picks, live, later, map_ext, damping, traces, *refs):
    slots, cells = traces.shape
    received, (traces_out, row) = refs[:-2], refs[-2:]
    part = slots // 4
    layer = lax.axis_index("depth")
    start = later[later.shape[0] - 1].astype(jnp.float32) + traces[...].astype(jnp.float32)
    row[:, :cells] = start.astype(jnp.bfloat16)

    def take(phase):
        messages = received[phase * len(swaps) : (phase + 1) * len(swaps)]
        at = [messages[0].shape[0] - part]
        mask = live[live.shape[0] - 1]
        row[:, cells:] = halo_of([[ref] for ref in messages], swaps, at, part, mask)

    by_rule = layer < 0
    for at, phase in picks:
        by_rule = by_rule | (layer == at)
        pl.when(layer == at)(functools.partial(take, phase))
    pl.when(jnp.logical_not(by_rule))(functools.partial(take, len(received) // len(swaps) - 1))
    image = dot(row[...], map_ext[...])
    traces_out[...] = blend(image, row[:, :cells], damping)


def call(kernel, out_shape, operands, in_hbm=(), scratch=(), aliases=None):
    spaces = [pltpu.HBM if i in in_hbm else pltpu.VMEM for i in range(len(operands))]
    operands = [
        pltpu.with_memory_space_constraint(x, pltpu.HBM) if i in in_hbm else x
        for i, x in enumerate(operands)
    ]
    return pl.pallas_call(
        kernel,
        out_shape=out_shape,
        in_specs=[pl.BlockSpec(memory_space=space) for space in spaces],
        out_specs=[pl.BlockSpec(memory_space=pltpu.VMEM)] * len(out_shape),
        scratch_shapes=scratch,
        input_output_aliases=aliases or {},
        compiler_params=pltpu.CompilerParams(vmem_limit_bytes=32 * 1024 * 1024),
    )(*operands)


MESH_AXES = ("depth", "gx", "gy")


def send(x, moves, swap=None):
    sizes = [lax.axis_size(axis) for axis in MESH_AXES]
    pairs = []
    for layer, below in moves:
        for i in range(sizes[1]):
            for j in range(sizes[2]):
                to = {"depth": below, "gx": i, "gy": j}
                if swap is not None:
                    axis, parity, _ = swap
                    to[axis] += 1 if to[axis] % 2 == parity else -1
                spot = [to[axis] for axis in MESH_AXES]
                if all(0 <= s < size for s, size in zip(spot, sizes)):
                    here = (layer * sizes[1] + i) * sizes[2] + j
                    there = (spot[0] * sizes[1] + spot[1]) * sizes[2] + spot[2]
                    pairs.append((here, there))
    return lax.ppermute(x, MESH_AXES, pairs)


def local(arrival, source, assignment, counts, first_map, second_map, damping):
    layers = lax.axis_size("depth")
    slots, cells = arrival.shape[1], arrival.shape[4]
    rounds = source.shape[1]
    arrival = arrival[0, :, 0, 0, :]
    source = source[0, :, :, 0, 0, :]
    counts = counts.transpose(0, 2, 3, 1)
    first_map = first_map[0, 0, 0]
    second_map = second_map[0, 0, 0]
    damping = damping[0, 0]
    swaps = exchanges()
    early_layers = layers - rounds + 1
    soon = rounds - 2

    def array(*shape, kind=jnp.bfloat16):
        return jax.ShapeDtypeStruct(shape, kind)

    def scratch(x):
        return pltpu.VMEM(x.shape, x.dtype)

    part = slots // 4
    band = coupling_band(cells)
    later = array(2, slots, cells)
    whole = array(cells + LANES, cells)
    counts_in = pltpu.SMEM(counts.shape, counts.dtype)
    opened = call(
        functools.partial(opening_kernel, swaps),
        [
            array(soon, slots, cells),
            later,
            array(rounds, slots, LANES),
            array(cells + (rounds - 1) * slots, LANES),
            array(cells, LANES),
            array(*first_map.shape),
            array(*band.shape),
        ]
        + [array(soon * part, LANES)] * len(swaps),
        [arrival, source, assignment, counts, first_map, band],
        in_hbm=range(6),
        scratch=[
            scratch(arrival),
            scratch(source),
            scratch(assignment),
            counts_in,
            pltpu.SemaphoreType.DMA((6 + soon,)),
        ],
    )
    first, later, live, edge, own_edge, first_map, band = opened[:7]
    received = [
        send(m, [(layer, layer) for layer in range(early_layers)], swap)
        for m, swap in zip(opened[7:], swaps)
    ]
    inner, edge = call(
        functools.partial(coupled_kernel, early_layers),
        [array(soon * slots, cells), array(*edge.shape)],
        [first, first_map, band, edge],
        aliases={3: 1},
    )
    edge_next = send(edge, [(layer, layer - 1) for layer in range(1, layers)])
    traces, map_ext, second_map = call(
        functools.partial(image_kernel, early_layers),
        [array(soon * slots, cells, kind=jnp.float32), whole, array(*second_map.shape)],
        [inner, first_map, band, second_map],
        in_hbm=(3,),
        scratch=[pltpu.SemaphoreType.DMA],
    )
    arrived = []
    picks = []
    kept = []
    for step in range(rounds - 1):
        chains = min(rounds - 1 - step, soon)
        last = step == rounds - 2
        before_last = step == rounds - 3
        keeps = step + chains == rounds - 1 and not last
        going = (chains - 1 if keeps else chains) * slots
        outs = [array(going, cells)] + [array(slots, cells)] * keeps
        outs += [array(chains * part, LANES)] * len(swaps)
        operands = [first, later, live, map_ext, damping, edge_next, traces] + received
        if last:
            operands += kept
        if before_last:
            operands += waiting
        ended = call(
            functools.partial(step_kernel, swaps, step, chains, keeps, before_last), outs, operands
        )
        moves = [(layer, layer + 1) for layer in range(step, step + early_layers)]
        traces = send(ended[0], [(layer, layer + 1) for layer in range(layers - 1)] if last else moves)
        if keeps:
            kept.append(ended[1])
            picks.append((step + 1, len(arrived) // len(swaps)))
        if before_last:
            moves.append((0, 0))
            picks.append((0, len(arrived) // len(swaps)))
        if last:
            moves.append((0, 1))
        received = [send(m, moves, swap) for m, swap in zip(ended[-len(swaps) :], swaps)]
        if step > 0:
            arrived += received
        if step == 0:
            late = call(
                functools.partial(late_kernel, early_layers, swaps),
                [whole, array(*later.shape)] + [array(2 * part, LANES)] * len(swaps),
                [source, assignment, counts, first_map, band, second_map, own_edge, map_ext, later],
                in_hbm=range(3),
                scratch=[
                    scratch(later),
                    scratch(assignment),
                    counts_in,
                    pltpu.SemaphoreType.DMA((3,)),
                ],
                aliases={7: 0, 8: 1},
            )
            map_ext, later, waiting = late[0], late[1], list(late[2:])
    (ended,) = call(
        functools.partial(final_kernel, swaps, picks),
        [array(slots, cells)],
        [live, later, map_ext, damping, traces] + arrived,
        scratch=[pltpu.VMEM((slots, cells + LANES), jnp.bfloat16)],
    )
    return ended.reshape(1, slots, 1, 1, cells)


def solution(mesh):
    return jax.shard_map(
        local,
        mesh=mesh,
        in_specs=(
            P("depth", None, "gx", "gy", None),
            P("depth", None, None, "gx", "gy", None),
            P(),
            P(None, None, "gx", "gy"),
            P("depth", "gx", "gy", None, None),
            P("depth", "gx", "gy", None, None),
            P("depth", "gx", "gy", None),
        ),
        out_specs=P("depth", None, "gx", "gy", None),
        check_vma=False,
    )
```

```python
import functools

import jax
import jax.numpy as jnp
import numpy as np
from jax import lax
from jax.experimental import pallas as pl
from jax.experimental.pallas import tpu as pltpu
from jax.sharding import PartitionSpec as P

FX = 32
FY = 28
SHOT_BATCH = 16

coupling_weight = 0.25

LANES = 128
GROUP = LANES // 4
EDGE_AXES = (("gx", 0), ("gy", 2))


def dot(a, b):
    return jnp.dot(a, b, preferred_element_type=jnp.float32)


def dot_t(a, b):
    return lax.dot_general(a, b, (((0,), (0,)), ((), ())), preferred_element_type=jnp.float32)


def edge_selector(cells):
    row = lax.broadcasted_iota(jnp.int32, (cells, LANES), 0)
    lane = lax.broadcasted_iota(jnp.int32, (cells, LANES), 1)
    return select_edges(row, lane)


def select_edges(row, lane):
    group = lane // GROUP
    spot = lane % GROUP
    along_x = group < 2
    cell = jnp.where(
        along_x,
        jnp.where(group == 0, spot, (FX - 1) * FY + spot),
        jnp.where(group == 2, spot * FY, spot * FY + FY - 1),
    )
    length = jnp.where(along_x, FY, FX)
    return jnp.where((row == cell) & (spot < length), 1.0, 0.0).astype(jnp.bfloat16)


def edge_rows_selector(cells):
    lane = lax.broadcasted_iota(jnp.int32, (LANES, cells), 0)
    row = lax.broadcasted_iota(jnp.int32, (LANES, cells), 1)
    return select_edges(row, lane)


def exchanges():
    found = []
    for axis, base in EDGE_AXES:
        for parity in range(min(lax.axis_size(axis) - 1, 2)):
            found.append((axis, parity, base))
    return found[::-1]


def group_of(axis, parity, base):
    ahead = lax.axis_index(axis) % 2 == parity
    return jnp.where(ahead, base + 1, base)


def pack(edges, group):
    rows = edges.shape[0] // 4
    lane_group = lax.broadcasted_iota(jnp.int32, (rows, LANES), 1) // GROUP
    packed = jnp.zeros((rows, LANES), jnp.float32)
    for part in range(4):
        piece = edges[part * rows : (part + 1) * rows]
        piece = pltpu.roll(piece, (part - group + 4) % 4 * GROUP, 1)
        packed = jnp.where(lane_group == part, piece, packed)
    return packed.astype(jnp.bfloat16)


def unpack(packed, group):
    lane_group = lax.broadcasted_iota(jnp.int32, packed.shape, 1) // GROUP
    pieces = []
    for part in range(4):
        piece = pltpu.roll(packed, (group - part + 4) % 4 * GROUP, 1)
        pieces.append(jnp.where(lane_group == group, piece, 0.0))
    return jnp.concatenate(pieces, axis=0)


def unit_of(round_number):
    return round_number - lax.axis_index("depth") + lax.axis_size("depth") - 1


def chosen_of(wanted, counts_in, round_number):
    slots = wanted.shape[1]
    shot = lax.broadcasted_iota(jnp.int32, (slots, slots), 0)
    slot = lax.broadcasted_iota(jnp.int32, (1, slots), 1)
    live = jnp.zeros((1, slots), jnp.int32)
    for batch in range(slots // SHOT_BATCH):
        count = counts_in[unit_of(round_number), 0, 0, batch]
        live = jnp.where(slot // SHOT_BATCH == batch, count, live)
    wanted = jnp.where(slot % SHOT_BATCH < live, wanted, -1)
    return jnp.where(shot == wanted, 1.0, 0.0).astype(jnp.bfloat16)


def started(pairs, sems):
    copies = [
        pltpu.make_async_copy(here, there, sems.at[i]) for i, (here, there) in enumerate(pairs)
    ]
    for copy in copies:
        copy.start()
    return copies


def fill_live(live_out, counts_in):
    position = lax.broadcasted_iota(jnp.int32, (SHOT_BATCH, LANES), 0)
    rounds, slots = live_out.shape[:2]
    for round_number in range(rounds):
        for batch in range(slots // SHOT_BATCH):
            count = counts_in[unit_of(round_number), 0, 0, batch]
            rows = slice(batch * SHOT_BATCH, (batch + 1) * SHOT_BATCH)
            live_out[round_number, rows] = jnp.where(position < count, 1.0, 0.0).astype(
                jnp.bfloat16
            )


def edges_kernel(source, assignment, counts, first_map, band, second_map, *refs):
    edge_out, first_out, later_out, live_out, first_in, band_in, second_in = refs[:7]
    source_in, assignment_in, counts_in, sems = refs[7:]
    rounds, slots, cells = source.shape
    soon = first_out.shape[0]

    @pl.when(lax.axis_index("depth") > 0)
    def _():
        pairs = [(counts, counts_in), (assignment, assignment_in), (first_map, first_in)]
        pairs += [(source.at[r], source_in.at[r]) for r in range(1, rounds)]
        pairs += [(band, band_in), (second_map, second_in)]
        copies = started(pairs, sems)
        selector = edge_selector(cells)
        copies[0].wait()
        fill_live(live_out, counts_in)
        copies[1].wait()
        copies[2].wait()
        first_edge = dot(first_in[...], selector).astype(jnp.bfloat16)
        edge_out[:cells] = first_edge
        for r in range(1, rounds):
            copies[2 + r].wait()
            chosen = chosen_of(assignment_in[r : r + 1], counts_in, r)
            picked = dot_t(chosen, source_in[r]).astype(jnp.bfloat16)
            if r < soon:
                first_out[r] = picked
            else:
                later_out[r - soon] = picked
            at = cells + (r - 1) * slots
            edge_out[at : at + slots] = dot(picked, first_edge).astype(jnp.bfloat16)
        copies[-2].wait()
        copies[-1].wait()


def opening_kernel(early_layers, swaps, arrival, source, assignment, counts, *refs):
    first_map, band, second_map = refs[:3]
    first_out, live_out, first_in, band_in, second_in, own_edge, edge_cells = refs[8:15]
    messages = refs[15 : 15 + len(swaps)]
    arrival_in, source_in, assignment_in, counts_in, sems = refs[15 + len(swaps) :]
    slots, cells = arrival.shape
    part = slots // 4
    soon = first_out.shape[0]
    early = lax.axis_index("depth") < early_layers

    @pl.when(jnp.logical_not(early))
    def _():
        edge_cells[...] = edge_rows_selector(cells)

    @pl.when(early)
    def _():
        pairs = [(counts, counts_in), (assignment, assignment_in), (first_map, first_in)]
        pairs += [(arrival, arrival_in)]
        pairs += [(source.at[r], source_in.at[r]) for r in range(soon)]
        pairs += [(band, band_in), (second_map, second_in)]
        copies = started(pairs, sems)
        edge_cells[...] = edge_rows_selector(cells)
        selector = edge_selector(cells)
        copies[0].wait()
        fill_live(live_out, counts_in)
        copies[1].wait()
        chosen = [chosen_of(assignment_in[r : r + 1], counts_in, r) for r in range(soon)]
        copies[2].wait()
        first_edge = dot(first_in[...], selector).astype(jnp.bfloat16)
        own_edge[...] = first_edge
        copies[3].wait()
        for r in range(soon):
            copies[4 + r].wait()
            picked = dot_t(chosen[r], source_in[r])
            if r == 0:
                live = live_out[0].astype(jnp.float32)
                live = jnp.concatenate([live] * (cells // LANES), axis=1)
                picked = picked + live * arrival_in[...].astype(jnp.float32)
            picked = picked.astype(jnp.bfloat16)
            first_out[r] = picked
            edges = dot(picked, first_edge)
            for message, swap in zip(messages, swaps):
                message[r * part : (r + 1) * part] = pack(edges, group_of(*swap))
        copies[-2].wait()
        copies[-1].wait()


def bands(cells):
    found = []
    for at in range(0, cells, 2 * LANES):
        end = min(at + 2 * LANES, cells)
        found.append((slice(max(at - LANES, 0), min(end + LANES, cells)), slice(at, end)))
    return found


def coupling_band(cells):
    cell = np.arange(cells)
    apart = np.abs(cell[:, None] - cell[None, :])
    same_row = cell[:, None] // FY == cell[None, :] // FY
    linked = (apart == FY) | ((apart == 1) & same_row)
    coupling = np.eye(cells) + coupling_weight * linked
    band = np.zeros((len(bands(cells)), 4 * LANES, 2 * LANES), np.float32)
    for block, (rows, columns) in zip(band, bands(cells)):
        piece = coupling[rows, columns]
        block[: piece.shape[0], : piece.shape[1]] = piece
    return jnp.asarray(band, jnp.bfloat16)


def coupled(x, band):
    pieces = []
    for at, (rows, columns) in enumerate(bands(x.shape[1])):
        height, width = rows.stop - rows.start, columns.stop - columns.start
        pieces.append(dot(x[:, rows], band[at, :height, :width]).astype(jnp.bfloat16))
    return jnp.concatenate(pieces, axis=1)


def fill_whole_map(first_map, band, second_map, whole_ext):
    cells = second_map.shape[0]
    whole_ext[:cells] = dot(coupled(first_map[...], band), second_map[...]).astype(jnp.bfloat16)


def inside_kernel(early_layers, first, first_map, band, second_map, edge_cells, *refs):
    image_out, whole_ext = refs
    cells = second_map.shape[0]
    early = lax.axis_index("depth") < early_layers

    @pl.when(early)
    def _():
        mapped = dot(first[...].reshape(-1, cells), first_map[...]).astype(jnp.bfloat16)
        image_out[...] = dot(coupled(mapped, band), second_map[...])

    @pl.when(jnp.logical_not(early))
    def _():
        fill_whole_map(first_map, band, second_map, whole_ext)

    edge_rows = dot(edge_cells[...], second_map[...])
    whole_ext[cells:] = (coupling_weight * edge_rows).astype(jnp.bfloat16)


def waiting_kernel(early_layers, swaps, source, assignment, counts, *refs):
    first_map, band, second_map, own_edge, _, _, whole_ext, later_out = refs[:8]
    messages = refs[8 : 8 + len(swaps)]
    source_in, assignment_in, counts_in, sems = refs[8 + len(swaps) :]
    rounds, slots = source.shape[:2]
    part = slots // 4
    layer = lax.axis_index("depth")

    @pl.when(layer == 0)
    def _():
        pairs = [(counts, counts_in), (assignment, assignment_in)]
        pairs += [(source.at[pl.ds(rounds - 2, 2)], source_in)]
        for copy in started(pairs, sems):
            copy.wait()
        for at, r in enumerate(range(rounds - 2, rounds)):
            chosen = chosen_of(assignment_in[r : r + 1], counts_in, r)
            picked = dot_t(chosen, source_in[at]).astype(jnp.bfloat16)
            later_out[at] = picked
            edges = dot(picked, own_edge[...])
            for message, swap in zip(messages, swaps):
                message[at * part : (at + 1) * part] = pack(edges, group_of(*swap))

    @pl.when((layer > 0) & (layer < early_layers))
    def _():
        fill_whole_map(first_map, band, second_map, whole_ext)


def last_map_kernel(first_map, band, second_map, whole_in, whole_ext):
    del whole_in

    @pl.when(lax.axis_index("depth") == 0)
    def _():
        fill_whole_map(first_map, band, second_map, whole_ext)


def halo_of(messages, swaps, at, part, live):
    halo = 0.0
    for parts, swap in zip(messages, swaps):
        packed = 0.0
        for ref, row in zip(parts, at):
            packed = packed + ref[row : row + part].astype(jnp.float32)
        halo = halo + unpack(packed, group_of(*swap))
    return (halo * live.astype(jnp.float32)).astype(jnp.bfloat16)


def blend(image, start, damping):
    damp = damping[...]
    return (damp * image + (1.0 - damp) * start.astype(jnp.float32)).astype(jnp.bfloat16)


def rounds_of(first, later, begin, end):
    soon = first.shape[0]
    found = [first[r] if r < soon else later[r - soon] for r in range(begin, end)]
    return jnp.concatenate(found, axis=0)


def step_kernel(swaps, step, chains, keeps, waiting, early_layers, *refs):
    first, later, live, map_ext, damping, edge_next, traces = refs[:7]
    received = refs[7 : 7 + len(swaps)]
    others = refs[7 + len(swaps) :]
    messages, others = others[-len(swaps) :], others[: -len(swaps)]
    kept_out = None
    if keeps:
        kept_out, others = others[-1], others[:-1]
    traces_out, others = others[-1], others[:-1]
    slots, cells = first.shape[1:]
    part = slots // 4
    layer = lax.axis_index("depth")
    here = (layer >= step) & (layer < step + early_layers)
    if not keeps and step > 0:
        here = here | (layer == 0)

    @pl.when(here)
    def _():
        halo = [
            halo_of([[ref] for ref in received], swaps, [chain * part], part, live[step + chain])
            for chain in range(chains)
        ]
        halo = jnp.concatenate(halo, axis=0)
        start = rounds_of(first, later, step, step + chains)
        if step == 0:
            image = traces[...] + dot(halo, map_ext[cells:])
        else:
            start = start.astype(jnp.float32) + traces[...].astype(jnp.float32)
            start = start.astype(jnp.bfloat16)
            image = dot(jnp.concatenate([start, halo], axis=1), map_ext[...])
        ended = blend(image, start, damping)
        going = (chains - 1 if keeps else chains) * slots
        traces_out[...] = ended[:going]
        if keeps:
            kept_out[...] = ended[going:]
        at = cells + step * slots
        edges = dot(ended, edge_next[:cells])
        edges += edge_next[at : at + chains * slots].astype(jnp.float32)
        for message, swap in zip(messages, swaps):
            for chain in range(chains):
                message[chain * part : (chain + 1) * part] = pack(
                    edges[chain * slots : (chain + 1) * slots], group_of(*swap)
                )

    if waiting:

        @pl.when(layer == 0)
        def _():
            for message, other in zip(messages, others):
                message[...] = other[...]

    else:
        for at, other in enumerate(others):

            @pl.when(layer == at + 1)
            def _():
                traces_out[...] = other[...]


def final_kernel(swaps, picks, live, later, map_ext, damping, traces, *refs):
    slots, cells = traces.shape
    received, (traces_out, row) = refs[:-2], refs[-2:]
    part = slots // 4
    layer = lax.axis_index("depth")
    start = later[later.shape[0] - 1].astype(jnp.float32) + traces[...].astype(jnp.float32)
    row[:, :cells] = start.astype(jnp.bfloat16)

    def take(phase):
        messages = received[phase * len(swaps) : (phase + 1) * len(swaps)]
        at = [messages[0].shape[0] - part]
        mask = live[live.shape[0] - 1]
        row[:, cells:] = halo_of([[ref] for ref in messages], swaps, at, part, mask)

    by_rule = layer < 0
    for at, phase in picks:
        by_rule = by_rule | (layer == at)
        pl.when(layer == at)(functools.partial(take, phase))
    pl.when(jnp.logical_not(by_rule))(functools.partial(take, len(received) // len(swaps) - 1))
    image = dot(row[...], map_ext[...])
    traces_out[...] = blend(image, row[:, :cells], damping)


def call(kernel, out_shape, operands, in_hbm=(), scratch=(), aliases=None):
    spaces = [pltpu.HBM if i in in_hbm else pltpu.VMEM for i in range(len(operands))]
    operands = [
        pltpu.with_memory_space_constraint(x, pltpu.HBM) if i in in_hbm else x
        for i, x in enumerate(operands)
    ]
    return pl.pallas_call(
        kernel,
        out_shape=out_shape,
        in_specs=[pl.BlockSpec(memory_space=space) for space in spaces],
        out_specs=[pl.BlockSpec(memory_space=pltpu.VMEM)] * len(out_shape),
        scratch_shapes=scratch,
        input_output_aliases=aliases or {},
        compiler_params=pltpu.CompilerParams(vmem_limit_bytes=32 * 1024 * 1024),
    )(*operands)


MESH_AXES = ("depth", "gx", "gy")


def send(x, moves, swap=None):
    sizes = [lax.axis_size(axis) for axis in MESH_AXES]
    pairs = []
    for layer, below in moves:
        for i in range(sizes[1]):
            for j in range(sizes[2]):
                to = {"depth": below, "gx": i, "gy": j}
                if swap is not None:
                    axis, parity, _ = swap
                    to[axis] += 1 if to[axis] % 2 == parity else -1
                spot = [to[axis] for axis in MESH_AXES]
                if all(0 <= s < size for s, size in zip(spot, sizes)):
                    here = (layer * sizes[1] + i) * sizes[2] + j
                    there = (spot[0] * sizes[1] + spot[1]) * sizes[2] + spot[2]
                    pairs.append((here, there))
    return lax.ppermute(x, MESH_AXES, pairs)


def local(arrival, source, assignment, counts, first_map, second_map, damping):
    layers = lax.axis_size("depth")
    slots, cells = arrival.shape[1], arrival.shape[4]
    rounds = source.shape[1]
    arrival = arrival[0, :, 0, 0, :]
    source = source[0, :, :, 0, 0, :]
    counts = counts.transpose(0, 2, 3, 1)
    first_map = first_map[0, 0, 0]
    second_map = second_map[0, 0, 0]
    damping = damping[0, 0]
    swaps = exchanges()
    early_layers = layers - rounds + 1
    soon = rounds - 2

    def array(*shape, kind=jnp.bfloat16):
        return jax.ShapeDtypeStruct(shape, kind)

    def scratch(x):
        return pltpu.VMEM(x.shape, x.dtype)

    part = slots // 4
    band = coupling_band(cells)
    later = array(2, slots, cells)
    whole = array(cells + LANES, cells)
    edge = array(cells + (rounds - 1) * slots, LANES)
    counts_in = pltpu.SMEM(counts.shape, counts.dtype)
    maps = [first_map, band, second_map]
    own = [array(soon, slots, cells), array(rounds, slots, LANES)]
    own += [array(*x.shape) for x in maps]
    copied = [scratch(source), scratch(assignment), counts_in]
    edge, first, later, live, *maps_in = call(
        edges_kernel,
        [edge, own[0], later] + own[1:],
        [source, assignment, counts] + maps,
        in_hbm=range(6),
        scratch=copied + [pltpu.SemaphoreType.DMA((4 + rounds,))],
    )
    edge_next = send(edge, [(layer, layer - 1) for layer in range(1, layers)])
    opened = call(
        functools.partial(opening_kernel, early_layers, swaps),
        own + [array(cells, LANES), array(LANES, cells)] + [array(soon * part, LANES)] * len(swaps),
        [arrival, source, assignment, counts] + maps + [first, live] + maps_in,
        in_hbm=range(7),
        scratch=[scratch(arrival)] + copied + [pltpu.SemaphoreType.DMA((6 + soon,))],
        aliases={7 + i: i for i in range(5)},
    )
    first, live, first_map, band, second_map, own_edge, edge_cells = opened[:7]
    received = [
        send(m, [(layer, layer) for layer in range(early_layers)], swap)
        for m, swap in zip(opened[7:], swaps)
    ]
    traces, map_ext = call(
        functools.partial(inside_kernel, early_layers),
        [array(soon * slots, cells, kind=jnp.float32), whole],
        [first, first_map, band, second_map, edge_cells],
    )
    arrived = []
    picks = []
    kept = []
    for step in range(rounds - 1):
        chains = min(rounds - 1 - step, soon)
        last = step == rounds - 2
        before_last = step == rounds - 3
        keeps = step + chains == rounds - 1 and not last
        going = (chains - 1 if keeps else chains) * slots
        outs = [array(going, cells)] + [array(slots, cells)] * keeps
        outs += [array(chains * part, LANES)] * len(swaps)
        operands = [first, later, live, map_ext, damping, edge_next, traces] + received
        if last:
            operands += kept
        if before_last:
            operands += waiting
        ended = call(
            functools.partial(step_kernel, swaps, step, chains, keeps, before_last, early_layers),
            outs,
            operands,
        )
        moves = [(layer, layer + 1) for layer in range(step, step + early_layers)]
        traces = send(ended[0], [(layer, layer + 1) for layer in range(layers - 1)] if last else moves)
        if keeps:
            kept.append(ended[1])
            picks.append((step + 1, len(arrived) // len(swaps)))
        if before_last:
            moves.append((0, 0))
            picks.append((0, len(arrived) // len(swaps)))
        if last:
            moves.append((0, 1))
        received = [send(m, moves, swap) for m, swap in zip(ended[-len(swaps) :], swaps)]
        if step > 0:
            arrived += received
        if step == 0:
            late = call(
                functools.partial(waiting_kernel, early_layers, swaps),
                [whole, array(*later.shape)] + [array(2 * part, LANES)] * len(swaps),
                [source, assignment, counts, first_map, band, second_map, own_edge, map_ext, later],
                in_hbm=range(3),
                scratch=[
                    scratch(later),
                    scratch(assignment),
                    counts_in,
                    pltpu.SemaphoreType.DMA((3,)),
                ],
                aliases={7: 0, 8: 1},
            )
            map_ext, later, waiting = late[0], late[1], list(late[2:])
        if before_last:
            (map_ext,) = call(
                last_map_kernel,
                [whole],
                [first_map, band, second_map, map_ext],
                aliases={3: 0},
            )
    (ended,) = call(
        functools.partial(final_kernel, swaps, picks),
        [array(slots, cells)],
        [live, later, map_ext, damping, traces] + arrived,
        scratch=[pltpu.VMEM((slots, cells + LANES), jnp.bfloat16)],
    )
    return ended.reshape(1, slots, 1, 1, cells)


def solution(mesh):
    return jax.shard_map(
        local,
        mesh=mesh,
        in_specs=(
            P("depth", None, "gx", "gy", None),
            P("depth", None, None, "gx", "gy", None),
            P(),
            P(None, None, "gx", "gy"),
            P("depth", "gx", "gy", None, None),
            P("depth", "gx", "gy", None, None),
            P("depth", "gx", "gy", None),
        ),
        out_specs=P("depth", None, "gx", "gy", None),
        check_vma=False,
    )
```

```python
import functools

import jax
import jax.numpy as jnp
import numpy as np
from jax import lax
from jax.experimental import pallas as pl
from jax.experimental.pallas import tpu as pltpu
from jax.sharding import PartitionSpec as P

FX = 32
FY = 28
SHOT_BATCH = 16

coupling_weight = 0.25

LANES = 128
GROUP = LANES // 4
EDGE_AXES = (("gx", 0), ("gy", 2))


def dot(a, b):
    return jnp.dot(a, b, preferred_element_type=jnp.float32)


def dot_t(a, b):
    return lax.dot_general(a, b, (((0,), (0,)), ((), ())), preferred_element_type=jnp.float32)


def edge_selector(cells):
    row = lax.broadcasted_iota(jnp.int32, (cells, LANES), 0)
    lane = lax.broadcasted_iota(jnp.int32, (cells, LANES), 1)
    return select_edges(row, lane)


def select_edges(row, lane):
    group = lane // GROUP
    spot = lane % GROUP
    along_x = group < 2
    cell = jnp.where(
        along_x,
        jnp.where(group == 0, spot, (FX - 1) * FY + spot),
        jnp.where(group == 2, spot * FY, spot * FY + FY - 1),
    )
    length = jnp.where(along_x, FY, FX)
    return jnp.where((row == cell) & (spot < length), 1.0, 0.0).astype(jnp.bfloat16)


def edge_rows_selector(cells):
    lane = lax.broadcasted_iota(jnp.int32, (LANES, cells), 0)
    row = lax.broadcasted_iota(jnp.int32, (LANES, cells), 1)
    return select_edges(row, lane)


def exchanges():
    found = []
    for axis, base in EDGE_AXES:
        for parity in range(min(lax.axis_size(axis) - 1, 2)):
            found.append((axis, parity, base))
    return found[::-1]


def group_of(axis, parity, base):
    ahead = lax.axis_index(axis) % 2 == parity
    return jnp.where(ahead, base + 1, base)


def pack(edges, group):
    rows = edges.shape[0] // 4
    lane_group = lax.broadcasted_iota(jnp.int32, (rows, LANES), 1) // GROUP
    packed = jnp.zeros((rows, LANES), jnp.float32)
    for part in range(4):
        piece = edges[part * rows : (part + 1) * rows]
        piece = pltpu.roll(piece, (part - group + 4) % 4 * GROUP, 1)
        packed = jnp.where(lane_group == part, piece, packed)
    return packed.astype(jnp.bfloat16)


def unpack(packed, group):
    lane_group = lax.broadcasted_iota(jnp.int32, packed.shape, 1) // GROUP
    pieces = []
    for part in range(4):
        piece = pltpu.roll(packed, (group - part + 4) % 4 * GROUP, 1)
        pieces.append(jnp.where(lane_group == group, piece, 0.0))
    return jnp.concatenate(pieces, axis=0)


def unit_of(round_number):
    return round_number - lax.axis_index("depth") + lax.axis_size("depth") - 1


def chosen_of(wanted, counts_in, round_number):
    slots = wanted.shape[1]
    shot = lax.broadcasted_iota(jnp.int32, (slots, slots), 0)
    slot = lax.broadcasted_iota(jnp.int32, (1, slots), 1)
    live = jnp.zeros((1, slots), jnp.int32)
    for batch in range(slots // SHOT_BATCH):
        count = counts_in[unit_of(round_number), 0, 0, batch]
        live = jnp.where(slot // SHOT_BATCH == batch, count, live)
    wanted = jnp.where(slot % SHOT_BATCH < live, wanted, -1)
    return jnp.where(shot == wanted, 1.0, 0.0).astype(jnp.bfloat16)


def started(pairs, sems):
    copies = [
        pltpu.make_async_copy(here, there, sems.at[i]) for i, (here, there) in enumerate(pairs)
    ]
    for copy in copies:
        copy.start()
    return copies


def fill_live(live_out, counts_in):
    position = lax.broadcasted_iota(jnp.int32, (SHOT_BATCH, LANES), 0)
    rounds, slots = live_out.shape[:2]
    for round_number in range(rounds):
        for batch in range(slots // SHOT_BATCH):
            count = counts_in[unit_of(round_number), 0, 0, batch]
            rows = slice(batch * SHOT_BATCH, (batch + 1) * SHOT_BATCH)
            live_out[round_number, rows] = jnp.where(position < count, 1.0, 0.0).astype(
                jnp.bfloat16
            )


def edges_kernel(source, assignment, counts, first_map, band, second_map, *refs):
    edge_out, first_out, later_out, live_out, first_in, band_in, second_in = refs[:7]
    source_in, assignment_in, counts_in, sems = refs[7:]
    rounds, slots, cells = source.shape
    soon = first_out.shape[0]

    @pl.when(lax.axis_index("depth") > 0)
    def _():
        pairs = [(counts, counts_in), (assignment, assignment_in), (first_map, first_in)]
        pairs += [(source.at[r], source_in.at[r]) for r in range(1, rounds)]
        pairs += [(band, band_in), (second_map, second_in)]
        copies = started(pairs, sems)
        selector = edge_selector(cells)
        copies[0].wait()
        fill_live(live_out, counts_in)
        copies[1].wait()
        copies[2].wait()
        first_edge = dot(first_in[...], selector).astype(jnp.bfloat16)
        edge_out[:cells] = first_edge
        for r in range(1, rounds):
            copies[2 + r].wait()
            chosen = chosen_of(assignment_in[r : r + 1], counts_in, r)
            picked = dot_t(chosen, source_in[r]).astype(jnp.bfloat16)
            if r < soon:
                first_out[r] = picked
            else:
                later_out[r - soon] = picked
            at = cells + (r - 1) * slots
            edge_out[at : at + slots] = dot(picked, first_edge).astype(jnp.bfloat16)
        copies[-2].wait()
        copies[-1].wait()


def opening_kernel(early_layers, swaps, arrival, source, assignment, counts, *refs):
    first_map, band, second_map = refs[:3]
    first_out, live_out, first_in, band_in, second_in, own_edge, edge_cells = refs[8:15]
    messages = refs[15 : 15 + len(swaps)]
    arrival_in, source_in, assignment_in, counts_in, sems = refs[15 + len(swaps) :]
    slots, cells = arrival.shape
    part = slots // 4
    soon = first_out.shape[0]
    early = lax.axis_index("depth") < early_layers

    @pl.when(jnp.logical_not(early))
    def _():
        edge_cells[...] = edge_rows_selector(cells)

    @pl.when(early)
    def _():
        pairs = [(counts, counts_in), (assignment, assignment_in), (first_map, first_in)]
        pairs += [(arrival, arrival_in)]
        pairs += [(source.at[r], source_in.at[r]) for r in range(soon)]
        pairs += [(band, band_in), (second_map, second_in)]
        copies = started(pairs, sems)
        edge_cells[...] = edge_rows_selector(cells)
        selector = edge_selector(cells)
        copies[0].wait()
        fill_live(live_out, counts_in)
        copies[1].wait()
        chosen = [chosen_of(assignment_in[r : r + 1], counts_in, r) for r in range(soon)]
        copies[2].wait()
        first_edge = dot(first_in[...], selector).astype(jnp.bfloat16)
        own_edge[...] = first_edge
        copies[3].wait()
        for r in range(soon):
            copies[4 + r].wait()
            picked = dot_t(chosen[r], source_in[r])
            if r == 0:
                live = live_out[0].astype(jnp.float32)
                live = jnp.concatenate([live] * (cells // LANES), axis=1)
                picked = picked + live * arrival_in[...].astype(jnp.float32)
            picked = picked.astype(jnp.bfloat16)
            first_out[r] = picked
            edges = dot(picked, first_edge)
            for message, swap in zip(messages, swaps):
                message[r * part : (r + 1) * part] = pack(edges, group_of(*swap))
        copies[-2].wait()
        copies[-1].wait()


def bands(cells):
    found = []
    for at in range(0, cells, 2 * LANES):
        end = min(at + 2 * LANES, cells)
        found.append((slice(max(at - LANES, 0), min(end + LANES, cells)), slice(at, end)))
    return found


def coupling_band(cells):
    cell = np.arange(cells)
    apart = np.abs(cell[:, None] - cell[None, :])
    same_row = cell[:, None] // FY == cell[None, :] // FY
    linked = (apart == FY) | ((apart == 1) & same_row)
    coupling = np.eye(cells) + coupling_weight * linked
    band = np.zeros((len(bands(cells)), 4 * LANES, 2 * LANES), np.float32)
    for block, (rows, columns) in zip(band, bands(cells)):
        piece = coupling[rows, columns]
        block[: piece.shape[0], : piece.shape[1]] = piece
    return jnp.asarray(band, jnp.bfloat16)


def coupled(x, band):
    pieces = []
    for at, (rows, columns) in enumerate(bands(x.shape[1])):
        height, width = rows.stop - rows.start, columns.stop - columns.start
        pieces.append(dot(x[:, rows], band[at, :height, :width]).astype(jnp.bfloat16))
    return jnp.concatenate(pieces, axis=1)


def fill_whole_map(first_map, band, second_map, whole_ext):
    cells = second_map.shape[0]
    whole_ext[:cells] = dot(coupled(first_map[...], band), second_map[...]).astype(jnp.bfloat16)


def inside_kernel(early_layers, first, first_map, band, second_map, edge_cells, *refs):
    image_out, whole_ext = refs
    cells = second_map.shape[0]
    early = lax.axis_index("depth") < early_layers

    @pl.when(early)
    def _():
        mapped = dot(first[...].reshape(-1, cells), first_map[...]).astype(jnp.bfloat16)
        image_out[...] = dot(coupled(mapped, band), second_map[...])

    @pl.when(jnp.logical_not(early))
    def _():
        fill_whole_map(first_map, band, second_map, whole_ext)

    edge_rows = dot(edge_cells[...], second_map[...])
    whole_ext[cells:] = (coupling_weight * edge_rows).astype(jnp.bfloat16)


def waiting_kernel(early_layers, swaps, source, assignment, counts, *refs):
    first_map, band, second_map, own_edge, _, _, whole_ext, later_out = refs[:8]
    messages = refs[8 : 8 + len(swaps)]
    source_in, assignment_in, counts_in, sems = refs[8 + len(swaps) :]
    rounds, slots = source.shape[:2]
    part = slots // 4
    layer = lax.axis_index("depth")

    @pl.when(layer == 0)
    def _():
        pairs = [(counts, counts_in), (assignment, assignment_in)]
        pairs += [(source.at[pl.ds(rounds - 2, 2)], source_in)]
        for copy in started(pairs, sems):
            copy.wait()
        for at, r in enumerate(range(rounds - 2, rounds)):
            chosen = chosen_of(assignment_in[r : r + 1], counts_in, r)
            picked = dot_t(chosen, source_in[at]).astype(jnp.bfloat16)
            later_out[at] = picked
            edges = dot(picked, own_edge[...])
            for message, swap in zip(messages, swaps):
                message[at * part : (at + 1) * part] = pack(edges, group_of(*swap))

    @pl.when((layer > 0) & (layer < early_layers))
    def _():
        fill_whole_map(first_map, band, second_map, whole_ext)


def last_map_kernel(first_map, band, second_map, whole_in, whole_ext):
    del whole_in

    @pl.when(lax.axis_index("depth") == 0)
    def _():
        fill_whole_map(first_map, band, second_map, whole_ext)


def halo_of(messages, swaps, at, part, live):
    halo = 0.0
    for parts, swap in zip(messages, swaps):
        packed = 0.0
        for ref, row in zip(parts, at):
            packed = packed + ref[row : row + part].astype(jnp.float32)
        halo = halo + unpack(packed, group_of(*swap))
    return (halo * live.astype(jnp.float32)).astype(jnp.bfloat16)


def blend(image, start, damping):
    damp = damping[...]
    return (damp * image + (1.0 - damp) * start.astype(jnp.float32)).astype(jnp.bfloat16)


def rounds_of(first, later, begin, end):
    soon = first.shape[0]
    found = [first[r] if r < soon else later[r - soon] for r in range(begin, end)]
    return jnp.concatenate(found, axis=0)


def step_kernel(swaps, step, chains, keeps, waiting, early_layers, *refs):
    first, later, live, map_ext, damping, edge_next, traces = refs[:7]
    received = refs[7 : 7 + len(swaps)]
    others = refs[7 + len(swaps) :]
    messages, others = others[-len(swaps) :], others[: -len(swaps)]
    kept_out = None
    if keeps:
        kept_out, others = others[-1], others[:-1]
    traces_out, others = others[-1], others[:-1]
    slots, cells = first.shape[1:]
    part = slots // 4
    layer = lax.axis_index("depth")
    here = (layer >= step) & (layer < step + early_layers)
    if not keeps and step > 0:
        here = here | (layer == 0)

    @pl.when(here)
    def _():
        halo = [
            halo_of([[ref] for ref in received], swaps, [chain * part], part, live[step + chain])
            for chain in range(chains)
        ]
        halo = jnp.concatenate(halo, axis=0)
        start = rounds_of(first, later, step, step + chains)
        if step == 0:
            image = traces[...] + dot(halo, map_ext[cells:])
        else:
            start = start.astype(jnp.float32) + traces[...].astype(jnp.float32)
            start = start.astype(jnp.bfloat16)
            image = dot(jnp.concatenate([start, halo], axis=1), map_ext[...])
        ended = blend(image, start, damping)
        going = (chains - 1 if keeps else chains) * slots
        traces_out[...] = ended[:going]
        if keeps:
            kept_out[...] = ended[going:]
        at = cells + step * slots
        edges = dot(ended, edge_next[:cells])
        edges += edge_next[at : at + chains * slots].astype(jnp.float32)
        for message, swap in zip(messages, swaps):
            for chain in range(chains):
                message[chain * part : (chain + 1) * part] = pack(
                    edges[chain * slots : (chain + 1) * slots], group_of(*swap)
                )

    if waiting:

        @pl.when(layer == 0)
        def _():
            for message, other in zip(messages, others):
                message[...] = other[...]


def final_kernel(swaps, picks, others, live, later, map_ext, damping, traces, *refs):
    slots, cells = traces.shape
    kept, received, (traces_out, row) = refs[:others], refs[others:-2], refs[-2:]
    part = slots // 4
    layer = lax.axis_index("depth")
    start = later[later.shape[0] - 1].astype(jnp.float32) + traces[...].astype(jnp.float32)
    for other in kept:
        start = start + other[...].astype(jnp.float32)
    row[:, :cells] = start.astype(jnp.bfloat16)

    def take(phase):
        messages = received[phase * len(swaps) : (phase + 1) * len(swaps)]
        at = [messages[0].shape[0] - part]
        mask = live[live.shape[0] - 1]
        row[:, cells:] = halo_of([[ref] for ref in messages], swaps, at, part, mask)

    by_rule = layer < 0
    for at, phase in picks:
        by_rule = by_rule | (layer == at)
        pl.when(layer == at)(functools.partial(take, phase))
    pl.when(jnp.logical_not(by_rule))(functools.partial(take, len(received) // len(swaps) - 1))
    image = dot(row[...], map_ext[...])
    traces_out[...] = blend(image, row[:, :cells], damping)


def call(kernel, out_shape, operands, in_hbm=(), scratch=(), aliases=None):
    spaces = [pltpu.HBM if i in in_hbm else pltpu.VMEM for i in range(len(operands))]
    operands = [
        pltpu.with_memory_space_constraint(x, pltpu.HBM) if i in in_hbm else x
        for i, x in enumerate(operands)
    ]
    return pl.pallas_call(
        kernel,
        out_shape=out_shape,
        in_specs=[pl.BlockSpec(memory_space=space) for space in spaces],
        out_specs=[pl.BlockSpec(memory_space=pltpu.VMEM)] * len(out_shape),
        scratch_shapes=scratch,
        input_output_aliases=aliases or {},
        compiler_params=pltpu.CompilerParams(vmem_limit_bytes=32 * 1024 * 1024),
    )(*operands)


MESH_AXES = ("depth", "gx", "gy")


def send(x, moves, swap=None):
    sizes = [lax.axis_size(axis) for axis in MESH_AXES]
    pairs = []
    for layer, below in moves:
        for i in range(sizes[1]):
            for j in range(sizes[2]):
                to = {"depth": below, "gx": i, "gy": j}
                if swap is not None:
                    axis, parity, _ = swap
                    to[axis] += 1 if to[axis] % 2 == parity else -1
                spot = [to[axis] for axis in MESH_AXES]
                if all(0 <= s < size for s, size in zip(spot, sizes)):
                    here = (layer * sizes[1] + i) * sizes[2] + j
                    there = (spot[0] * sizes[1] + spot[1]) * sizes[2] + spot[2]
                    pairs.append((here, there))
    return lax.ppermute(x, MESH_AXES, pairs)


def local(arrival, source, assignment, counts, first_map, second_map, damping):
    layers = lax.axis_size("depth")
    slots, cells = arrival.shape[1], arrival.shape[4]
    rounds = source.shape[1]
    arrival = arrival[0, :, 0, 0, :]
    source = source[0, :, :, 0, 0, :]
    counts = counts.transpose(0, 2, 3, 1)
    first_map = first_map[0, 0, 0]
    second_map = second_map[0, 0, 0]
    damping = damping[0, 0]
    swaps = exchanges()
    early_layers = layers - rounds + 1
    soon = rounds - 2

    def array(*shape, kind=jnp.bfloat16):
        return jax.ShapeDtypeStruct(shape, kind)

    def scratch(x):
        return pltpu.VMEM(x.shape, x.dtype)

    part = slots // 4
    band = coupling_band(cells)
    later = array(2, slots, cells)
    whole = array(cells + LANES, cells)
    edge = array(cells + (rounds - 1) * slots, LANES)
    counts_in = pltpu.SMEM(counts.shape, counts.dtype)
    maps = [first_map, band, second_map]
    own = [array(soon, slots, cells), array(rounds, slots, LANES)]
    own += [array(*x.shape) for x in maps]
    copied = [scratch(source), scratch(assignment), counts_in]
    edge, first, later, live, *maps_in = call(
        edges_kernel,
        [edge, own[0], later] + own[1:],
        [source, assignment, counts] + maps,
        in_hbm=range(6),
        scratch=copied + [pltpu.SemaphoreType.DMA((4 + rounds,))],
    )
    edge_next = send(edge, [(layer, layer - 1) for layer in range(1, layers)])
    opened = call(
        functools.partial(opening_kernel, early_layers, swaps),
        own + [array(cells, LANES), array(LANES, cells)] + [array(soon * part, LANES)] * len(swaps),
        [arrival, source, assignment, counts] + maps + [first, live] + maps_in,
        in_hbm=range(7),
        scratch=[scratch(arrival)] + copied + [pltpu.SemaphoreType.DMA((6 + soon,))],
        aliases={7 + i: i for i in range(5)},
    )
    first, live, first_map, band, second_map, own_edge, edge_cells = opened[:7]
    received = [
        send(m, [(layer, layer) for layer in range(early_layers)], swap)
        for m, swap in zip(opened[7:], swaps)
    ]
    traces, map_ext = call(
        functools.partial(inside_kernel, early_layers),
        [array(soon * slots, cells, kind=jnp.float32), whole],
        [first, first_map, band, second_map, edge_cells],
    )
    arrived = []
    picks = []
    kept = []
    for step in range(rounds - 1):
        chains = min(rounds - 1 - step, soon)
        last = step == rounds - 2
        before_last = step == rounds - 3
        keeps = step + chains == rounds - 1 and not last
        going = (chains - 1 if keeps else chains) * slots
        outs = [array(going, cells)] + [array(slots, cells)] * keeps
        outs += [array(chains * part, LANES)] * len(swaps)
        operands = [first, later, live, map_ext, damping, edge_next, traces] + received
        if before_last:
            operands += waiting
        ended = call(
            functools.partial(step_kernel, swaps, step, chains, keeps, before_last, early_layers),
            outs,
            operands,
        )
        moves = [(layer, layer + 1) for layer in range(step, step + early_layers)]
        traces = send(ended[0], moves + [(0, 1)] if last else moves)
        if keeps:
            kept.append(send(ended[1], [(step, step + 1)]))
            picks.append((step + 1, len(arrived) // len(swaps)))
        if before_last:
            moves.append((0, 0))
            picks.append((0, len(arrived) // len(swaps)))
        if last:
            moves.append((0, 1))
        received = [send(m, moves, swap) for m, swap in zip(ended[-len(swaps) :], swaps)]
        if step > 0:
            arrived += received
        if step == 0:
            late = call(
                functools.partial(waiting_kernel, early_layers, swaps),
                [whole, array(*later.shape)] + [array(2 * part, LANES)] * len(swaps),
                [source, assignment, counts, first_map, band, second_map, own_edge, map_ext, later],
                in_hbm=range(3),
                scratch=[
                    scratch(later),
                    scratch(assignment),
                    counts_in,
                    pltpu.SemaphoreType.DMA((3,)),
                ],
                aliases={7: 0, 8: 1},
            )
            map_ext, later, waiting = late[0], late[1], list(late[2:])
        if before_last:
            (map_ext,) = call(
                last_map_kernel,
                [whole],
                [first_map, band, second_map, map_ext],
                aliases={3: 0},
            )
    (ended,) = call(
        functools.partial(final_kernel, swaps, picks, len(kept)),
        [array(slots, cells)],
        [live, later, map_ext, damping, traces] + kept + arrived,
        scratch=[pltpu.VMEM((slots, cells + LANES), jnp.bfloat16)],
    )
    return ended.reshape(1, slots, 1, 1, cells)


def solution(mesh):
    return jax.shard_map(
        local,
        mesh=mesh,
        in_specs=(
            P("depth", None, "gx", "gy", None),
            P("depth", None, None, "gx", "gy", None),
            P(),
            P(None, None, "gx", "gy"),
            P("depth", "gx", "gy", None, None),
            P("depth", "gx", "gy", None, None),
            P("depth", "gx", "gy", None),
        ),
        out_specs=P("depth", None, "gx", "gy", None),
        check_vma=False,
    )
```

```python
import functools

import jax
import jax.numpy as jnp
import numpy as np
from jax import lax
from jax.experimental import pallas as pl
from jax.experimental.pallas import tpu as pltpu
from jax.sharding import PartitionSpec as P

FX = 32
FY = 28
SHOT_BATCH = 16

coupling_weight = 0.25

LANES = 128
GROUP = LANES // 4
EDGE_AXES = (("gx", 0), ("gy", 2))


def dot(a, b):
    return jnp.dot(a, b, preferred_element_type=jnp.float32)


def dot_t(a, b):
    return lax.dot_general(a, b, (((0,), (0,)), ((), ())), preferred_element_type=jnp.float32)


def edge_selector(cells):
    row = lax.broadcasted_iota(jnp.int32, (cells, LANES), 0)
    lane = lax.broadcasted_iota(jnp.int32, (cells, LANES), 1)
    return select_edges(row, lane)


def select_edges(row, lane):
    group = lane // GROUP
    spot = lane % GROUP
    along_x = group < 2
    cell = jnp.where(
        along_x,
        jnp.where(group == 0, spot, (FX - 1) * FY + spot),
        jnp.where(group == 2, spot * FY, spot * FY + FY - 1),
    )
    length = jnp.where(along_x, FY, FX)
    return jnp.where((row == cell) & (spot < length), 1.0, 0.0).astype(jnp.bfloat16)


def edge_rows_selector(cells):
    lane = lax.broadcasted_iota(jnp.int32, (LANES, cells), 0)
    row = lax.broadcasted_iota(jnp.int32, (LANES, cells), 1)
    return select_edges(row, lane)


def exchanges():
    found = []
    for axis, base in EDGE_AXES:
        for parity in range(min(lax.axis_size(axis) - 1, 2)):
            found.append((axis, parity, base))
    return found[::-1]


def group_of(axis, parity, base):
    ahead = lax.axis_index(axis) % 2 == parity
    return jnp.where(ahead, base + 1, base)


def pack(edges, group):
    rows = edges.shape[0] // 4
    lane_group = lax.broadcasted_iota(jnp.int32, (rows, LANES), 1) // GROUP
    packed = jnp.zeros((rows, LANES), jnp.float32)
    for part in range(4):
        piece = edges[part * rows : (part + 1) * rows]
        piece = pltpu.roll(piece, (part - group + 4) % 4 * GROUP, 1)
        packed = jnp.where(lane_group == part, piece, packed)
    return packed.astype(jnp.bfloat16)


def unpack(packed, group):
    lane_group = lax.broadcasted_iota(jnp.int32, packed.shape, 1) // GROUP
    pieces = []
    for part in range(4):
        piece = pltpu.roll(packed, (group - part + 4) % 4 * GROUP, 1)
        pieces.append(jnp.where(lane_group == group, piece, 0.0))
    return jnp.concatenate(pieces, axis=0)


def unit_of(round_number):
    return round_number - lax.axis_index("depth") + lax.axis_size("depth") - 1


def chosen_of(wanted, counts_in, round_number):
    slots = wanted.shape[1]
    shot = lax.broadcasted_iota(jnp.int32, (slots, slots), 0)
    slot = lax.broadcasted_iota(jnp.int32, (1, slots), 1)
    live = jnp.zeros((1, slots), jnp.int32)
    for batch in range(slots // SHOT_BATCH):
        count = counts_in[unit_of(round_number), 0, 0, batch]
        live = jnp.where(slot // SHOT_BATCH == batch, count, live)
    wanted = jnp.where(slot % SHOT_BATCH < live, wanted, -1)
    return jnp.where(shot == wanted, 1.0, 0.0).astype(jnp.bfloat16)


def started(pairs, sems):
    copies = [
        pltpu.make_async_copy(here, there, sems.at[i]) for i, (here, there) in enumerate(pairs)
    ]
    for copy in copies:
        copy.start()
    return copies


def fill_live(live_out, counts_in):
    position = lax.broadcasted_iota(jnp.int32, (SHOT_BATCH, LANES), 0)
    rounds, slots = live_out.shape[:2]
    for round_number in range(rounds):
        for batch in range(slots // SHOT_BATCH):
            count = counts_in[unit_of(round_number), 0, 0, batch]
            rows = slice(batch * SHOT_BATCH, (batch + 1) * SHOT_BATCH)
            live_out[round_number, rows] = jnp.where(position < count, 1.0, 0.0).astype(
                jnp.bfloat16
            )


def edges_kernel(source, assignment, counts, first_map, edge_out, starts_out, live_out, *refs):
    source_in, assignment_in, counts_in, first_in, sems = refs
    rounds, slots, cells = source.shape

    @pl.when(lax.axis_index("depth") > 0)
    def _():
        pairs = [(counts, counts_in), (assignment, assignment_in), (first_map, first_in)]
        pairs += [(source.at[r], source_in.at[r]) for r in range(1, rounds)]
        copies = started(pairs, sems)
        selector = edge_selector(cells)
        copies[0].wait()
        fill_live(live_out, counts_in)
        copies[1].wait()
        copies[2].wait()
        first_edge = dot(first_in[...], selector).astype(jnp.bfloat16)
        edge_out[:cells] = first_edge
        for r in range(1, rounds):
            copies[2 + r].wait()
            chosen = chosen_of(assignment_in[r : r + 1], counts_in, r)
            starts_out[r] = dot_t(chosen, source_in[r]).astype(jnp.bfloat16)
        edges = dot(starts_out[1:].reshape(-1, cells), first_edge)
        edge_out[cells:] = edges.astype(jnp.bfloat16)


def opening_kernel(early_layers, swaps, source, assignment, counts, arrival, first_map, *refs):
    starts_out, live_out, edge_cells = refs[2:5]
    messages = refs[5 : 5 + len(swaps)]
    source_in, assignment_in, counts_in, sems = refs[5 + len(swaps) :]
    rounds, slots, cells = source.shape
    part = slots // 4
    early = lax.axis_index("depth") < early_layers

    @pl.when(jnp.logical_not(early))
    def _():
        edge_cells[...] = edge_rows_selector(cells)

    @pl.when(early)
    def _():
        pairs = [(counts, counts_in), (assignment, assignment_in)]
        pairs += [(source.at[r], source_in.at[r]) for r in range(rounds)]
        copies = started(pairs, sems)
        edge_cells[...] = edge_rows_selector(cells)
        first_edge = dot(first_map[...], edge_selector(cells)).astype(jnp.bfloat16)
        copies[0].wait()
        fill_live(live_out, counts_in)
        copies[1].wait()
        for r in range(rounds):
            chosen = chosen_of(assignment_in[r : r + 1], counts_in, r)
            copies[2 + r].wait()
            picked = dot_t(chosen, source_in[r])
            if r == 0:
                live = live_out[0].astype(jnp.float32)
                live = jnp.concatenate([live] * (cells // LANES), axis=1)
                picked = picked + live * arrival[...].astype(jnp.float32)
            starts_out[r] = picked.astype(jnp.bfloat16)
        edges = dot(starts_out[...].reshape(-1, cells), first_edge)
        for message, swap in zip(messages, swaps):
            for r in range(rounds):
                message[r * part : (r + 1) * part] = pack(
                    edges[r * slots : (r + 1) * slots], group_of(*swap)
                )


def bands(cells):
    found = []
    for at in range(0, cells, 2 * LANES):
        end = min(at + 2 * LANES, cells)
        found.append((slice(max(at - LANES, 0), min(end + LANES, cells)), slice(at, end)))
    return found


def coupling_band(cells):
    cell = np.arange(cells)
    apart = np.abs(cell[:, None] - cell[None, :])
    same_row = cell[:, None] // FY == cell[None, :] // FY
    linked = (apart == FY) | ((apart == 1) & same_row)
    coupling = np.eye(cells) + coupling_weight * linked
    band = np.zeros((len(bands(cells)), 4 * LANES, 2 * LANES), np.float32)
    for block, (rows, columns) in zip(band, bands(cells)):
        piece = coupling[rows, columns]
        block[: piece.shape[0], : piece.shape[1]] = piece
    return jnp.asarray(band, jnp.bfloat16)


def coupled(x, band):
    pieces = []
    for at, (rows, columns) in enumerate(bands(x.shape[1])):
        height, width = rows.stop - rows.start, columns.stop - columns.start
        pieces.append(dot(x[:, rows], band[at, :height, :width]).astype(jnp.bfloat16))
    return jnp.concatenate(pieces, axis=1)


def fill_whole_map(first_map, band, second_map, whole_ext):
    cells = second_map.shape[0]
    whole_ext[:cells] = dot(coupled(first_map[...], band), second_map[...]).astype(jnp.bfloat16)


def inside_kernel(early_layers, starts, first_map, band, second_map, edge_cells, *refs):
    image_out, whole_ext = refs
    slots, cells = starts.shape[1:]
    chains = image_out.shape[0] // slots
    early = lax.axis_index("depth") < early_layers

    @pl.when(early)
    def _():
        mapped = dot(starts[:chains].reshape(-1, cells), first_map[...]).astype(jnp.bfloat16)
        image_out[...] = dot(coupled(mapped, band), second_map[...])

    @pl.when(jnp.logical_not(early))
    def _():
        fill_whole_map(first_map, band, second_map, whole_ext)

    edge_rows = dot(edge_cells[...], second_map[...])
    whole_ext[cells:] = (coupling_weight * edge_rows).astype(jnp.bfloat16)


def whole_map_kernel(early_layers, first_map, band, second_map, whole_in, whole_ext):
    del whole_in

    @pl.when(lax.axis_index("depth") < early_layers)
    def _():
        fill_whole_map(first_map, band, second_map, whole_ext)


def halo_of(messages, swaps, live):
    halo = 0.0
    for message, swap in zip(messages, swaps):
        halo = halo + unpack(message.astype(jnp.float32), group_of(*swap))
    return (halo * live.astype(jnp.float32)).astype(jnp.bfloat16)


def blend(image, start, damping):
    damp = damping[...]
    return (damp * image + (1.0 - damp) * start.astype(jnp.float32)).astype(jnp.bfloat16)


def step_kernel(swaps, step, chains, keeps, early_layers, *refs):
    starts, live, map_ext, damping, edge_next, traces = refs[:6]
    received = refs[6 : 6 + len(swaps)]
    opened = refs[6 + len(swaps) : -1 - len(swaps) - keeps]
    outs = refs[-1 - len(swaps) - keeps :]
    traces_out, messages = outs[0], outs[1 + keeps :]
    slots, cells = starts.shape[1:]
    part = slots // 4
    layer = lax.axis_index("depth")
    here = (layer >= step) & (layer < step + early_layers)
    if opened:
        here = here | (layer == 0)

    @pl.when(here)
    def _():
        halo = []
        for chain in range(chains):
            packed = [ref[chain * part : (chain + 1) * part] for ref in received]
            if opened:
                at = (step + chain) * part
                packed = [
                    jnp.where(layer == 0, ref[at : at + part].astype(jnp.float32), x)
                    for ref, x in zip(opened, packed)
                ]
            halo.append(halo_of(packed, swaps, live[step + chain]))
        halo = jnp.concatenate(halo, axis=0)
        start = starts[step : step + chains].reshape(-1, cells)
        if step == 0:
            image = traces[...] + dot(halo, map_ext[cells:])
        else:
            start = start.astype(jnp.float32) + traces[...].astype(jnp.float32)
            start = start.astype(jnp.bfloat16)
            image = dot(jnp.concatenate([start, halo], axis=1), map_ext[...])
        ended = blend(image, start, damping)
        going = traces_out.shape[0]
        traces_out[...] = ended[:going]
        if keeps:
            outs[1][...] = ended[going:]
        at = cells + step * slots
        edges = dot(ended, edge_next[:cells])
        edges += edge_next[at : at + chains * slots].astype(jnp.float32)
        for message, swap in zip(messages, swaps):
            for chain in range(chains):
                message[chain * part : (chain + 1) * part] = pack(
                    edges[chain * slots : (chain + 1) * slots], group_of(*swap)
                )


def final_kernel(swaps, picks, others, live, starts, map_ext, damping, traces, *refs):
    slots, cells = traces.shape
    kept, received, (traces_out, row) = refs[:others], refs[others:-2], refs[-2:]
    part = slots // 4
    layer = lax.axis_index("depth")
    start = starts[starts.shape[0] - 1].astype(jnp.float32) + traces[...].astype(jnp.float32)
    for other in kept:
        start = start + other[...].astype(jnp.float32)
    row[:, :cells] = start.astype(jnp.bfloat16)

    def take(phase):
        messages = received[phase * len(swaps) : (phase + 1) * len(swaps)]
        messages = [ref[ref.shape[0] - part :] for ref in messages]
        row[:, cells:] = halo_of(messages, swaps, live[live.shape[0] - 1])

    by_rule = layer < 0
    for at, phase in picks:
        by_rule = by_rule | (layer == at)
        pl.when(layer == at)(functools.partial(take, phase))
    pl.when(jnp.logical_not(by_rule))(functools.partial(take, len(received) // len(swaps) - 1))
    image = dot(row[...], map_ext[...])
    traces_out[...] = blend(image, row[:, :cells], damping)


def call(kernel, out_shape, operands, in_hbm=(), scratch=(), aliases=None):
    spaces = [pltpu.HBM if i in in_hbm else pltpu.VMEM for i in range(len(operands))]
    operands = [
        pltpu.with_memory_space_constraint(x, pltpu.HBM) if i in in_hbm else x
        for i, x in enumerate(operands)
    ]
    return pl.pallas_call(
        kernel,
        out_shape=out_shape,
        in_specs=[pl.BlockSpec(memory_space=space) for space in spaces],
        out_specs=[pl.BlockSpec(memory_space=pltpu.VMEM)] * len(out_shape),
        scratch_shapes=scratch,
        input_output_aliases=aliases or {},
        compiler_params=pltpu.CompilerParams(vmem_limit_bytes=32 * 1024 * 1024),
    )(*operands)


MESH_AXES = ("depth", "gx", "gy")


def send(x, moves, swap=None):
    sizes = [lax.axis_size(axis) for axis in MESH_AXES]
    pairs = []
    for layer, below in moves:
        for i in range(sizes[1]):
            for j in range(sizes[2]):
                to = {"depth": below, "gx": i, "gy": j}
                if swap is not None:
                    axis, parity, _ = swap
                    to[axis] += 1 if to[axis] % 2 == parity else -1
                spot = [to[axis] for axis in MESH_AXES]
                if all(0 <= s < size for s, size in zip(spot, sizes)):
                    here = (layer * sizes[1] + i) * sizes[2] + j
                    there = (spot[0] * sizes[1] + spot[1]) * sizes[2] + spot[2]
                    pairs.append((here, there))
    return lax.ppermute(x, MESH_AXES, pairs)


def local(arrival, source, assignment, counts, first_map, second_map, damping):
    layers = lax.axis_size("depth")
    slots, cells = arrival.shape[1], arrival.shape[4]
    rounds = source.shape[1]
    arrival = arrival[0, :, 0, 0, :]
    source = source[0, :, :, 0, 0, :]
    counts = counts.transpose(0, 2, 3, 1)
    first_map = first_map[0, 0, 0]
    second_map = second_map[0, 0, 0]
    damping = damping[0, 0]
    swaps = exchanges()
    early_layers = layers - rounds + 1
    soon = rounds - 2

    def array(*shape, kind=jnp.bfloat16):
        return jax.ShapeDtypeStruct(shape, kind)

    def scratch(x):
        return pltpu.VMEM(x.shape, x.dtype)

    part = slots // 4
    band = coupling_band(cells)
    whole = array(cells + LANES, cells)
    own = [array(rounds, slots, cells), array(rounds, slots, LANES)]
    copied = [scratch(source), scratch(assignment), pltpu.SMEM(counts.shape, counts.dtype)]
    edge, starts, live = call(
        edges_kernel,
        [array(cells + (rounds - 1) * slots, LANES)] + own,
        [source, assignment, counts, first_map],
        in_hbm=range(4),
        scratch=copied + [scratch(first_map), pltpu.SemaphoreType.DMA((2 + rounds,))],
    )
    edge_next = send(edge, [(layer, layer - 1) for layer in range(1, layers)])
    opened = call(
        functools.partial(opening_kernel, early_layers, swaps),
        own + [array(LANES, cells)] + [array(rounds * part, LANES)] * len(swaps),
        [source, assignment, counts, arrival, first_map, starts, live],
        in_hbm=range(3),
        scratch=copied + [pltpu.SemaphoreType.DMA((2 + rounds,))],
        aliases={5: 0, 6: 1},
    )
    starts, live, edge_cells = opened[:3]
    received = [
        send(m, [(layer, layer) for layer in range(early_layers)], swap)
        for m, swap in zip(opened[3:], swaps)
    ]
    traces, map_ext = call(
        functools.partial(inside_kernel, early_layers),
        [array(soon * slots, cells, kind=jnp.float32), whole],
        [starts, first_map, band, second_map, edge_cells],
    )
    opened = received
    arrived = list(opened)
    picks = [(0, 0)]
    kept = []
    for step in range(rounds - 1):
        chains = min(rounds - 1 - step, soon)
        last = step == rounds - 2
        keeps = step + chains == rounds - 1 and not last
        going = (chains - 1 if keeps else chains) * slots
        outs = [array(going, cells)] + [array(slots, cells)] * keeps
        outs += [array(chains * part, LANES)] * len(swaps)
        operands = [starts, live, map_ext, damping, edge_next, traces] + received
        ended = call(
            functools.partial(step_kernel, swaps, step, chains, keeps, early_layers),
            outs,
            operands + (opened if last else []),
        )
        moves = [(layer, layer + 1) for layer in range(step, step + early_layers)]
        if last:
            moves.append((0, 1))
        traces = send(ended[0], moves)
        if keeps:
            kept.append(send(ended[1], [(step, step + 1)]))
            picks.append((step + 1, len(arrived) // len(swaps)))
        received = [send(m, moves, swap) for m, swap in zip(ended[-len(swaps) :], swaps)]
        if step > 0:
            arrived += received
        if step == 0:
            (map_ext,) = call(
                functools.partial(whole_map_kernel, early_layers),
                [whole],
                [first_map, band, second_map, map_ext],
                aliases={3: 0},
            )
    (ended,) = call(
        functools.partial(final_kernel, swaps, picks, len(kept)),
        [array(slots, cells)],
        [live, starts, map_ext, damping, traces] + kept + arrived,
        scratch=[pltpu.VMEM((slots, cells + LANES), jnp.bfloat16)],
    )
    return ended.reshape(1, slots, 1, 1, cells)


def solution(mesh):
    return jax.shard_map(
        local,
        mesh=mesh,
        in_specs=(
            P("depth", None, "gx", "gy", None),
            P("depth", None, None, "gx", "gy", None),
            P(),
            P(None, None, "gx", "gy"),
            P("depth", "gx", "gy", None, None),
            P("depth", "gx", "gy", None, None),
            P("depth", "gx", "gy", None),
        ),
        out_specs=P("depth", None, "gx", "gy", None),
        check_vma=False,
    )
```

```python
import functools

import jax
import jax.numpy as jnp
import numpy as np
from jax import lax
from jax.experimental import pallas as pl
from jax.experimental.pallas import tpu as pltpu
from jax.sharding import PartitionSpec as P

FX = 32
FY = 28
SHOT_BATCH = 16

coupling_weight = 0.25

LANES = 128
GROUP = LANES // 4
EDGE_AXES = (("gx", 0), ("gy", 2))


def dot(a, b):
    return jnp.dot(a, b, preferred_element_type=jnp.float32)


def dot_t(a, b):
    return lax.dot_general(a, b, (((0,), (0,)), ((), ())), preferred_element_type=jnp.float32)


def group_at(lane):
    return lax.shift_right_logical(lane, GROUP.bit_length() - 1)


def edge_cells_of(lane):
    group, spot = group_at(lane), lane & (GROUP - 1)
    along_y = jnp.where(group == 0, spot, spot + (FX - 1) * FY)
    along_x = jnp.where(group == 2, spot * FY, spot * FY + FY - 1)
    cell = jnp.where(group < 2, along_y, along_x)
    return jnp.where(spot < jnp.where(group < 2, FY, FX), cell, -1)


def edge_selector(cells):
    cell = edge_cells_of(lax.broadcasted_iota(jnp.int32, (1, LANES), 1))
    row = lax.broadcasted_iota(jnp.int32, (cells, LANES), 0)
    return jnp.where(row == cell, 1.0, 0.0).astype(jnp.bfloat16)


def edge_rows_selector(cells):
    cell = edge_cells_of(lax.broadcasted_iota(jnp.int32, (LANES, 1), 0))
    row = lax.broadcasted_iota(jnp.int32, (LANES, cells), 1)
    return jnp.where(row == cell, 1.0, 0.0).astype(jnp.bfloat16)


def exchanges():
    found = []
    for axis, base in EDGE_AXES:
        for parity in range(min(lax.axis_size(axis) - 1, 2)):
            found.append((axis, parity, base))
    return found[::-1]


def group_of(axis, parity, base):
    ahead = (lax.axis_index(axis) & 1) == parity
    return jnp.where(ahead, base + 1, base)


def pack(edges, group):
    rows = edges.shape[0] // 4
    lane_group = group_at(lax.broadcasted_iota(jnp.int32, (rows, LANES), 1))
    packed = jnp.zeros((rows, LANES), jnp.float32)
    for part in range(4):
        piece = edges[part * rows : (part + 1) * rows]
        piece = pltpu.roll(piece, ((part - group) & 3) * GROUP, 1)
        packed = jnp.where(lane_group == part, piece, packed)
    return packed.astype(jnp.bfloat16)


def unpack(packed, group):
    lane_group = group_at(lax.broadcasted_iota(jnp.int32, packed.shape, 1))
    pieces = []
    for part in range(4):
        piece = pltpu.roll(packed, ((group - part) & 3) * GROUP, 1)
        pieces.append(jnp.where(lane_group == group, piece, 0.0))
    return jnp.concatenate(pieces, axis=0)


def unit_of(round_number):
    return round_number - lax.axis_index("depth") + lax.axis_size("depth") - 1


def chosen_of(wanted, counts_in, round_number):
    slots = wanted.shape[1]
    shot = lax.broadcasted_iota(jnp.int32, (slots, slots), 0)
    slot = lax.broadcasted_iota(jnp.int32, (1, slots), 1)
    live = jnp.zeros((1, slots), jnp.int32)
    for batch in range(slots // SHOT_BATCH):
        count = counts_in[unit_of(round_number), 0, 0, batch]
        live = jnp.where(slot >= batch * SHOT_BATCH, count + batch * SHOT_BATCH, live)
    wanted = jnp.where(slot < live, wanted, -1)
    return jnp.where(shot == wanted, 1.0, 0.0).astype(jnp.bfloat16)


def started(pairs, sems):
    copies = [
        pltpu.make_async_copy(here, there, sems.at[i]) for i, (here, there) in enumerate(pairs)
    ]
    for copy in copies:
        copy.start()
    return copies


def fill_live(live_out, counts_in):
    position = lax.broadcasted_iota(jnp.int32, (SHOT_BATCH, LANES), 0)
    rounds, slots = live_out.shape[:2]
    for round_number in range(rounds):
        for batch in range(slots // SHOT_BATCH):
            count = counts_in[unit_of(round_number), 0, 0, batch]
            rows = slice(batch * SHOT_BATCH, (batch + 1) * SHOT_BATCH)
            live_out[round_number, rows] = jnp.where(position < count, 1.0, 0.0).astype(
                jnp.bfloat16
            )


def edges_kernel(source, assignment, counts, first_map, edge_out, starts_out, live_out, *refs):
    source_in, assignment_in, counts_in, first_in, sems = refs
    rounds, slots, cells = source.shape

    @pl.when(lax.axis_index("depth") > 0)
    def _():
        pairs = [(counts, counts_in), (assignment, assignment_in), (first_map, first_in)]
        pairs += [(source.at[r], source_in.at[r]) for r in range(1, rounds)]
        copies = started(pairs, sems)
        selector = edge_selector(cells)
        copies[0].wait()
        fill_live(live_out, counts_in)
        copies[1].wait()
        copies[2].wait()
        first_edge = dot(first_in[...], selector).astype(jnp.bfloat16)
        edge_out[:cells] = first_edge
        for r in range(1, rounds):
            copies[2 + r].wait()
            chosen = chosen_of(assignment_in[r : r + 1], counts_in, r)
            starts_out[r] = dot_t(chosen, source_in[r]).astype(jnp.bfloat16)
        edges = dot(starts_out[1:].reshape(-1, cells), first_edge)
        edge_out[cells:] = edges.astype(jnp.bfloat16)


def opening_kernel(early_layers, swaps, source, assignment, counts, arrival, first_map, *refs):
    starts_out, live_out, edge_cells = refs[2:5]
    messages = refs[5 : 5 + len(swaps)]
    source_in, assignment_in, counts_in, sems = refs[5 + len(swaps) :]
    rounds, slots, cells = source.shape
    part = slots // 4
    early = lax.axis_index("depth") < early_layers

    @pl.when(jnp.logical_not(early))
    def _():
        edge_cells[...] = edge_rows_selector(cells)

    @pl.when(early)
    def _():
        pairs = [(counts, counts_in), (assignment, assignment_in)]
        pairs += [(source.at[r], source_in.at[r]) for r in range(rounds)]
        copies = started(pairs, sems)
        edge_cells[...] = edge_rows_selector(cells)
        first_edge = dot(first_map[...], edge_selector(cells)).astype(jnp.bfloat16)
        copies[0].wait()
        fill_live(live_out, counts_in)
        copies[1].wait()
        for r in range(rounds):
            chosen = chosen_of(assignment_in[r : r + 1], counts_in, r)
            copies[2 + r].wait()
            picked = dot_t(chosen, source_in[r])
            if r == 0:
                live = live_out[0].astype(jnp.float32)
                live = jnp.concatenate([live] * (cells // LANES), axis=1)
                picked = picked + live * arrival[...].astype(jnp.float32)
            starts_out[r] = picked.astype(jnp.bfloat16)
        edges = dot(starts_out[...].reshape(-1, cells), first_edge)
        for message, swap in zip(messages, swaps):
            for r in range(rounds):
                message[r * part : (r + 1) * part] = pack(
                    edges[r * slots : (r + 1) * slots], group_of(*swap)
                )


def bands(cells):
    found = []
    for at in range(0, cells, 2 * LANES):
        end = min(at + 2 * LANES, cells)
        found.append((slice(max(at - LANES, 0), min(end + LANES, cells)), slice(at, end)))
    return found


def coupling_band(cells):
    cell = np.arange(cells)
    apart = np.abs(cell[:, None] - cell[None, :])
    same_row = cell[:, None] // FY == cell[None, :] // FY
    linked = (apart == FY) | ((apart == 1) & same_row)
    coupling = np.eye(cells) + coupling_weight * linked
    band = np.zeros((len(bands(cells)), 4 * LANES, 2 * LANES), np.float32)
    for block, (rows, columns) in zip(band, bands(cells)):
        piece = coupling[rows, columns]
        block[: piece.shape[0], : piece.shape[1]] = piece
    return jnp.asarray(band, jnp.bfloat16)


def coupled(x, band):
    pieces = []
    for at, (rows, columns) in enumerate(bands(x.shape[1])):
        height, width = rows.stop - rows.start, columns.stop - columns.start
        pieces.append(dot(x[:, rows], band[at, :height, :width]).astype(jnp.bfloat16))
    return jnp.concatenate(pieces, axis=1)


def fill_whole_map(first_map, band, second_map, whole_ext):
    cells = second_map.shape[0]
    whole_ext[:cells] = dot(coupled(first_map[...], band), second_map[...]).astype(jnp.bfloat16)


def inside_kernel(early_layers, starts, first_map, band, second_map, edge_cells, *refs):
    image_out, whole_ext = refs
    slots, cells = starts.shape[1:]
    chains = image_out.shape[0] // slots
    early = lax.axis_index("depth") < early_layers

    @pl.when(early)
    def _():
        mapped = dot(starts[:chains].reshape(-1, cells), first_map[...]).astype(jnp.bfloat16)
        image_out[...] = dot(coupled(mapped, band), second_map[...])

    @pl.when(jnp.logical_not(early))
    def _():
        fill_whole_map(first_map, band, second_map, whole_ext)

    edge_rows = dot(edge_cells[...], second_map[...])
    whole_ext[cells:] = (coupling_weight * edge_rows).astype(jnp.bfloat16)


def whole_map_kernel(early_layers, first_map, band, second_map, whole_in, whole_ext):
    del whole_in

    @pl.when(lax.axis_index("depth") < early_layers)
    def _():
        fill_whole_map(first_map, band, second_map, whole_ext)


def halo_of(messages, swaps, live):
    halo = 0.0
    for message, swap in zip(messages, swaps):
        halo = halo + unpack(message.astype(jnp.float32), group_of(*swap))
    return (halo * live.astype(jnp.float32)).astype(jnp.bfloat16)


def blend(image, start, damp):
    return (damp * image + (1.0 - damp) * start.astype(jnp.float32)).astype(jnp.bfloat16)


def step_kernel(swaps, step, chains, keeps, early_layers, *refs):
    starts, live, map_ext, damping, edge_next, traces = refs[:6]
    received = refs[6 : 6 + len(swaps)]
    opened = refs[6 + len(swaps) : -1 - len(swaps) - keeps]
    outs = refs[-1 - len(swaps) - keeps :]
    traces_out, messages = outs[0], outs[1 + keeps :]
    slots, cells = starts.shape[1:]
    part = slots // 4
    layer = lax.axis_index("depth")
    here = (layer >= step) & (layer < step + early_layers)
    if opened:
        here = here | (layer == 0)

    @pl.when(here)
    def _():
        halo = []
        for chain in range(chains):
            packed = [ref[chain * part : (chain + 1) * part] for ref in received]
            if opened:
                at = (step + chain) * part
                packed = [
                    jnp.where(layer == 0, ref[at : at + part].astype(jnp.float32), x)
                    for ref, x in zip(opened, packed)
                ]
            halo.append(halo_of(packed, swaps, live[step + chain]))
        halo = jnp.concatenate(halo, axis=0)
        start = starts[step : step + chains].reshape(-1, cells)
        if step == 0:
            image = traces[...] + dot(halo, map_ext[cells:])
        else:
            start = start.astype(jnp.float32) + traces[...].astype(jnp.float32)
            start = start.astype(jnp.bfloat16)
            image = dot(jnp.concatenate([start, halo], axis=1), map_ext[...])
        ended = blend(image, start, damping[...])
        going = traces_out.shape[0]
        traces_out[...] = ended[:going]
        if keeps:
            outs[1][...] = ended[going:]
        at = cells + step * slots
        edges = dot(ended, edge_next[:cells])
        edges += edge_next[at : at + chains * slots].astype(jnp.float32)
        for message, swap in zip(messages, swaps):
            for chain in range(chains):
                message[chain * part : (chain + 1) * part] = pack(
                    edges[chain * slots : (chain + 1) * slots], group_of(*swap)
                )


def final_kernel(swaps, picks, others, live, starts, map_ext, damping, traces, *refs):
    slots, cells = traces.shape
    kept, received = refs[:others], refs[others:-4]
    traces_out, row, ended, sems = refs[-4:]
    part = slots // 4
    layer = lax.axis_index("depth")
    start = starts[starts.shape[0] - 1].astype(jnp.float32) + traces[...].astype(jnp.float32)
    for other in kept:
        start = start + other[...].astype(jnp.float32)
    row[:, :cells] = start.astype(jnp.bfloat16)

    def take(phase):
        messages = received[phase * len(swaps) : (phase + 1) * len(swaps)]
        messages = [ref[ref.shape[0] - part :] for ref in messages]
        row[:, cells:] = halo_of(messages, swaps, live[live.shape[0] - 1])

    by_rule = layer < 0
    for at, phase in picks:
        by_rule = by_rule | (layer == at)
        pl.when(layer == at)(functools.partial(take, phase))
    pl.when(jnp.logical_not(by_rule))(functools.partial(take, len(received) // len(swaps) - 1))
    copies = []
    half = cells // LANES // 2 * LANES
    for at, columns in enumerate([slice(0, half), slice(half, cells)]):
        image = dot(row[...], map_ext[:, columns])
        ended[:, columns] = blend(image, row[:, columns], damping[:, columns])
        copies.append(
            pltpu.make_async_copy(ended.at[:, columns], traces_out.at[:, columns], sems.at[at])
        )
        copies[-1].start()
    for copy in copies:
        copy.wait()


def call(kernel, out_shape, operands, in_hbm=(), scratch=(), aliases=None, to_hbm=False):
    spaces = [pltpu.HBM if i in in_hbm else pltpu.VMEM for i in range(len(operands))]
    operands = [
        pltpu.with_memory_space_constraint(x, pltpu.HBM) if i in in_hbm else x
        for i, x in enumerate(operands)
    ]
    return pl.pallas_call(
        kernel,
        out_shape=out_shape,
        in_specs=[pl.BlockSpec(memory_space=space) for space in spaces],
        out_specs=[pl.BlockSpec(memory_space=pl.ANY if to_hbm else pltpu.VMEM)] * len(out_shape),
        scratch_shapes=scratch,
        input_output_aliases=aliases or {},
        compiler_params=pltpu.CompilerParams(vmem_limit_bytes=32 * 1024 * 1024),
    )(*operands)


MESH_AXES = ("depth", "gx", "gy")


def send(x, moves, swap=None):
    sizes = [lax.axis_size(axis) for axis in MESH_AXES]
    pairs = []
    for layer, below in moves:
        for i in range(sizes[1]):
            for j in range(sizes[2]):
                to = {"depth": below, "gx": i, "gy": j}
                if swap is not None:
                    axis, parity, _ = swap
                    to[axis] += 1 if to[axis] % 2 == parity else -1
                spot = [to[axis] for axis in MESH_AXES]
                if all(0 <= s < size for s, size in zip(spot, sizes)):
                    here = (layer * sizes[1] + i) * sizes[2] + j
                    there = (spot[0] * sizes[1] + spot[1]) * sizes[2] + spot[2]
                    pairs.append((here, there))
    return lax.ppermute(x, MESH_AXES, pairs)


def local(arrival, source, assignment, counts, first_map, second_map, damping):
    layers = lax.axis_size("depth")
    slots, cells = arrival.shape[1], arrival.shape[4]
    rounds = source.shape[1]
    arrival = arrival[0, :, 0, 0, :]
    source = source[0, :, :, 0, 0, :]
    counts = counts.transpose(0, 2, 3, 1)
    first_map = first_map[0, 0, 0]
    second_map = second_map[0, 0, 0]
    damping = damping[0, 0]
    swaps = exchanges()
    early_layers = layers - rounds + 1
    soon = rounds - 2

    def array(*shape, kind=jnp.bfloat16):
        return jax.ShapeDtypeStruct(shape, kind)

    def scratch(x):
        return pltpu.VMEM(x.shape, x.dtype)

    part = slots // 4
    band = coupling_band(cells)
    whole = array(cells + LANES, cells)
    own = [array(rounds, slots, cells), array(rounds, slots, LANES)]
    copied = [scratch(source), scratch(assignment), pltpu.SMEM(counts.shape, counts.dtype)]
    edge, starts, live = call(
        edges_kernel,
        [array(cells + (rounds - 1) * slots, LANES)] + own,
        [source, assignment, counts, first_map],
        in_hbm=range(4),
        scratch=copied + [scratch(first_map), pltpu.SemaphoreType.DMA((2 + rounds,))],
    )
    edge_next = send(edge, [(layer, layer - 1) for layer in range(1, layers)])
    opened = call(
        functools.partial(opening_kernel, early_layers, swaps),
        own + [array(LANES, cells)] + [array(rounds * part, LANES)] * len(swaps),
        [source, assignment, counts, arrival, first_map, starts, live],
        in_hbm=range(3),
        scratch=copied + [pltpu.SemaphoreType.DMA((2 + rounds,))],
        aliases={5: 0, 6: 1},
    )
    starts, live, edge_cells = opened[:3]
    received = [
        send(m, [(layer, layer) for layer in range(early_layers)], swap)
        for m, swap in zip(opened[3:], swaps)
    ]
    traces, map_ext = call(
        functools.partial(inside_kernel, early_layers),
        [array(soon * slots, cells, kind=jnp.float32), whole],
        [starts, first_map, band, second_map, edge_cells],
    )
    opened = received
    arrived = list(opened)
    picks = [(0, 0)]
    kept = []
    for step in range(rounds - 1):
        chains = min(rounds - 1 - step, soon)
        last = step == rounds - 2
        keeps = step + chains == rounds - 1 and not last
        going = (chains - 1 if keeps else chains) * slots
        outs = [array(going, cells)] + [array(slots, cells)] * keeps
        outs += [array(chains * part, LANES)] * len(swaps)
        operands = [starts, live, map_ext, damping, edge_next, traces] + received
        ended = call(
            functools.partial(step_kernel, swaps, step, chains, keeps, early_layers),
            outs,
            operands + (opened if last else []),
        )
        moves = [(layer, layer + 1) for layer in range(step, step + early_layers)]
        if last:
            moves.append((0, 1))
        traces = send(ended[0], moves)
        if keeps:
            kept.append(send(ended[1], [(step, step + 1)]))
            picks.append((step + 1, len(arrived) // len(swaps)))
        received = [send(m, moves, swap) for m, swap in zip(ended[-len(swaps) :], swaps)]
        if step > 0:
            arrived += received
        if step == 0:
            (map_ext,) = call(
                functools.partial(whole_map_kernel, early_layers),
                [whole],
                [first_map, band, second_map, map_ext],
                aliases={3: 0},
            )
    (ended,) = call(
        functools.partial(final_kernel, swaps, picks, len(kept)),
        [array(slots, cells)],
        [live, starts, map_ext, damping, traces] + kept + arrived,
        scratch=[
            pltpu.VMEM((slots, cells + LANES), jnp.bfloat16),
            scratch(arrival),
            pltpu.SemaphoreType.DMA((2,)),
        ],
        to_hbm=True,
    )
    return ended.reshape(1, slots, 1, 1, cells)


def solution(mesh):
    return jax.shard_map(
        local,
        mesh=mesh,
        in_specs=(
            P("depth", None, "gx", "gy", None),
            P("depth", None, None, "gx", "gy", None),
            P(),
            P(None, None, "gx", "gy"),
            P("depth", "gx", "gy", None, None),
            P("depth", "gx", "gy", None, None),
            P("depth", "gx", "gy", None),
        ),
        out_specs=P("depth", None, "gx", "gy", None),
        check_vma=False,
    )
```

```python
import functools

import jax
import jax.numpy as jnp
import numpy as np
from jax import lax
from jax.experimental import pallas as pl
from jax.experimental.pallas import tpu as pltpu
from jax.sharding import PartitionSpec as P

FX = 32
FY = 28
SHOT_BATCH = 16

coupling_weight = 0.25

LANES = 128
GROUP = LANES // 4
EDGE_AXES = (("gx", 0), ("gy", 2))


def dot(a, b):
    return jnp.dot(a, b, preferred_element_type=jnp.float32)


def dot_t(a, b):
    return lax.dot_general(a, b, (((0,), (0,)), ((), ())), preferred_element_type=jnp.float32)


def group_at(lane):
    return lax.shift_right_logical(lane, GROUP.bit_length() - 1)


def edge_cells_of(lane):
    group, spot = group_at(lane), lane & (GROUP - 1)
    along_y = jnp.where(group == 0, spot, spot + (FX - 1) * FY)
    along_x = jnp.where(group == 2, spot * FY, spot * FY + FY - 1)
    cell = jnp.where(group < 2, along_y, along_x)
    return jnp.where(spot < jnp.where(group < 2, FY, FX), cell, -1)


def edge_selector(cells):
    cell = edge_cells_of(lax.broadcasted_iota(jnp.int32, (1, LANES), 1))
    row = lax.broadcasted_iota(jnp.int32, (cells, LANES), 0)
    return jnp.where(row == cell, 1.0, 0.0).astype(jnp.bfloat16)


def edge_rows_selector(cells):
    cell = edge_cells_of(lax.broadcasted_iota(jnp.int32, (LANES, 1), 0))
    row = lax.broadcasted_iota(jnp.int32, (LANES, cells), 1)
    return jnp.where(row == cell, 1.0, 0.0).astype(jnp.bfloat16)


def exchanges():
    found = []
    for axis, base in EDGE_AXES:
        for parity in range(min(lax.axis_size(axis) - 1, 2)):
            found.append((axis, parity, base))
    return found[::-1]


def group_of(axis, parity, base):
    ahead = (lax.axis_index(axis) & 1) == parity
    return jnp.where(ahead, base + 1, base)


def pack(edges, group):
    rows = edges.shape[0] // 4
    lane_group = group_at(lax.broadcasted_iota(jnp.int32, (rows, LANES), 1))
    packed = jnp.zeros((rows, LANES), jnp.float32)
    for part in range(4):
        piece = edges[part * rows : (part + 1) * rows]
        piece = pltpu.roll(piece, ((part - group) & 3) * GROUP, 1)
        packed = jnp.where(lane_group == part, piece, packed)
    return packed.astype(jnp.bfloat16)


def unpack(packed, group):
    lane_group = group_at(lax.broadcasted_iota(jnp.int32, packed.shape, 1))
    pieces = []
    for part in range(4):
        piece = pltpu.roll(packed, ((group - part) & 3) * GROUP, 1)
        pieces.append(jnp.where(lane_group == group, piece, 0.0))
    return jnp.concatenate(pieces, axis=0)


def unit_of(round_number):
    return round_number - lax.axis_index("depth") + lax.axis_size("depth") - 1


def chosen_of(wanted, counts_in, round_number):
    slots = wanted.shape[1]
    shot = lax.broadcasted_iota(jnp.int32, (slots, slots), 0)
    slot = lax.broadcasted_iota(jnp.int32, (1, slots), 1)
    live = jnp.zeros((1, slots), jnp.int32)
    for batch in range(slots // SHOT_BATCH):
        count = counts_in[unit_of(round_number), 0, 0, batch]
        live = jnp.where(slot >= batch * SHOT_BATCH, count + batch * SHOT_BATCH, live)
    wanted = jnp.where(slot < live, wanted, -1)
    return jnp.where(shot == wanted, 1.0, 0.0).astype(jnp.bfloat16)


def started(pairs, sems):
    copies = [
        pltpu.make_async_copy(here, there, sems.at[i]) for i, (here, there) in enumerate(pairs)
    ]
    for copy in copies:
        copy.start()
    return copies


def fill_live(live_out, counts_in):
    position = lax.broadcasted_iota(jnp.int32, (SHOT_BATCH, LANES), 0)
    rounds, slots = live_out.shape[:2]
    for round_number in range(rounds):
        for batch in range(slots // SHOT_BATCH):
            count = counts_in[unit_of(round_number), 0, 0, batch]
            rows = slice(batch * SHOT_BATCH, (batch + 1) * SHOT_BATCH)
            live_out[round_number, rows] = jnp.where(position < count, 1.0, 0.0).astype(
                jnp.bfloat16
            )


def edges_kernel(source, assignment, counts, first_map, edge_out, starts_out, live_out, *refs):
    source_in, assignment_in, counts_in, first_in, sems = refs
    rounds, slots, cells = source.shape

    @pl.when(lax.axis_index("depth") > 0)
    def _():
        pairs = [(counts, counts_in), (assignment, assignment_in), (first_map, first_in)]
        pairs += [(source.at[r], source_in.at[r]) for r in range(1, rounds)]
        copies = started(pairs, sems)
        selector = edge_selector(cells)
        copies[0].wait()
        fill_live(live_out, counts_in)
        copies[1].wait()
        copies[2].wait()
        first_edge = dot(first_in[...], selector).astype(jnp.bfloat16)
        edge_out[:cells] = first_edge
        for r in range(1, rounds):
            copies[2 + r].wait()
            chosen = chosen_of(assignment_in[r : r + 1], counts_in, r)
            starts_out[r] = dot_t(chosen, source_in[r]).astype(jnp.bfloat16)
        edges = dot(starts_out[1:].reshape(-1, cells), first_edge)
        edge_out[cells:] = edges.astype(jnp.bfloat16)


def opening_kernel(early_layers, swaps, source, assignment, counts, arrival, first_map, *refs):
    starts_out, live_out, edge_cells = refs[2:5]
    messages = refs[5 : 5 + len(swaps)]
    source_in, assignment_in, counts_in, sems = refs[5 + len(swaps) :]
    rounds, slots, cells = source.shape
    part = slots // 4
    early = lax.axis_index("depth") < early_layers

    @pl.when(jnp.logical_not(early))
    def _():
        edge_cells[...] = edge_rows_selector(cells)

    @pl.when(early)
    def _():
        pairs = [(counts, counts_in), (assignment, assignment_in)]
        pairs += [(source.at[r], source_in.at[r]) for r in range(rounds)]
        copies = started(pairs, sems)
        edge_cells[...] = edge_rows_selector(cells)
        first_edge = dot(first_map[...], edge_selector(cells)).astype(jnp.bfloat16)
        copies[0].wait()
        fill_live(live_out, counts_in)
        copies[1].wait()
        for r in range(rounds):
            chosen = chosen_of(assignment_in[r : r + 1], counts_in, r)
            copies[2 + r].wait()
            picked = dot_t(chosen, source_in[r])
            if r == 0:
                live = live_out[0].astype(jnp.float32)
                live = jnp.concatenate([live] * (cells // LANES), axis=1)
                picked = picked + live * arrival[...].astype(jnp.float32)
            picked = picked.astype(jnp.bfloat16)
            starts_out[r] = picked
            edges = dot(picked, first_edge)
            for message, swap in zip(messages, swaps):
                message[r * part : (r + 1) * part] = pack(edges, group_of(*swap))


def bands(cells):
    found = []
    for at in range(0, cells, 2 * LANES):
        end = min(at + 2 * LANES, cells)
        found.append((slice(max(at - LANES, 0), min(end + LANES, cells)), slice(at, end)))
    return found


def coupling_band(cells):
    cell = np.arange(cells)
    apart = np.abs(cell[:, None] - cell[None, :])
    same_row = cell[:, None] // FY == cell[None, :] // FY
    linked = (apart == FY) | ((apart == 1) & same_row)
    coupling = np.eye(cells) + coupling_weight * linked
    band = np.zeros((len(bands(cells)), 4 * LANES, 2 * LANES), np.float32)
    for block, (rows, columns) in zip(band, bands(cells)):
        piece = coupling[rows, columns]
        block[: piece.shape[0], : piece.shape[1]] = piece
    return jnp.asarray(band, jnp.bfloat16)


def coupled(x, band):
    pieces = []
    for at, (rows, columns) in enumerate(bands(x.shape[1])):
        height, width = rows.stop - rows.start, columns.stop - columns.start
        pieces.append(dot(x[:, rows], band[at, :height, :width]).astype(jnp.bfloat16))
    return jnp.concatenate(pieces, axis=1)


def fill_whole_map(first_map, band, second_map, whole_ext):
    cells = second_map.shape[0]
    whole_ext[:cells] = dot(coupled(first_map[...], band), second_map[...]).astype(jnp.bfloat16)


def inside_kernel(early_layers, starts, first_map, second_map, edge_cells, band, *refs):
    image_out, whole_ext, band_in, sem = refs
    slots, cells = starts.shape[1:]
    chains = image_out.shape[0] // slots
    early = lax.axis_index("depth") < early_layers
    copy = pltpu.make_async_copy(band, band_in, sem)
    copy.start()
    edge_rows = dot(edge_cells[...], second_map[...])
    whole_ext[cells:] = (coupling_weight * edge_rows).astype(jnp.bfloat16)

    @pl.when(early)
    def _():
        mapped = dot(starts[:chains].reshape(-1, cells), first_map[...]).astype(jnp.bfloat16)
        copy.wait()
        image_out[...] = dot(coupled(mapped, band_in), second_map[...])

    @pl.when(jnp.logical_not(early))
    def _():
        copy.wait()
        fill_whole_map(first_map, band_in, second_map, whole_ext)


def whole_map_kernel(early_layers, first_map, band, second_map, whole_in, whole_ext):
    del whole_in

    @pl.when(lax.axis_index("depth") < early_layers)
    def _():
        fill_whole_map(first_map, band, second_map, whole_ext)


def halo_of(messages, swaps, live):
    halo = 0.0
    for message, swap in zip(messages, swaps):
        halo = halo + unpack(message.astype(jnp.float32), group_of(*swap))
    return (halo * live.astype(jnp.float32)).astype(jnp.bfloat16)


def blend(image, start, damp):
    return (damp * image + (1.0 - damp) * start.astype(jnp.float32)).astype(jnp.bfloat16)


def step_kernel(swaps, step, chains, keeps, early_layers, *refs):
    starts, live, map_ext, damping, edge_next, traces = refs[:6]
    received = refs[6 : 6 + len(swaps)]
    opened = refs[6 + len(swaps) : -1 - len(swaps) - keeps]
    outs = refs[-1 - len(swaps) - keeps :]
    traces_out, messages = outs[0], outs[1 + keeps :]
    slots, cells = starts.shape[1:]
    part = slots // 4
    layer = lax.axis_index("depth")
    here = (layer >= step) & (layer < step + early_layers)
    if opened:
        here = here | (layer == 0)

    @pl.when(here)
    def _():
        halo = []
        for chain in range(chains):
            packed = [ref[chain * part : (chain + 1) * part] for ref in received]
            if opened:
                at = (step + chain) * part
                packed = [
                    jnp.where(layer == 0, ref[at : at + part].astype(jnp.float32), x)
                    for ref, x in zip(opened, packed)
                ]
            halo.append(halo_of(packed, swaps, live[step + chain]))
        halo = jnp.concatenate(halo, axis=0)
        start = starts[step : step + chains].reshape(-1, cells)
        if step == 0:
            image = traces[...] + dot(halo, map_ext[cells:])
        else:
            start = start.astype(jnp.float32) + traces[...].astype(jnp.float32)
            start = start.astype(jnp.bfloat16)
            image = dot(jnp.concatenate([start, halo], axis=1), map_ext[...])
        ended = blend(image, start, damping[...])
        going = traces_out.shape[0]
        traces_out[...] = ended[:going]
        if keeps:
            outs[1][...] = ended[going:]
        at = cells + step * slots
        edges = dot(ended, edge_next[:cells])
        edges += edge_next[at : at + chains * slots].astype(jnp.float32)
        for message, swap in zip(messages, swaps):
            for chain in range(chains):
                message[chain * part : (chain + 1) * part] = pack(
                    edges[chain * slots : (chain + 1) * slots], group_of(*swap)
                )


def final_kernel(swaps, picks, others, live, starts, map_ext, damping, traces, *refs):
    slots, cells = traces.shape
    kept, received = refs[:others], refs[others:-4]
    traces_out, row, ended, sems = refs[-4:]
    part = slots // 4
    layer = lax.axis_index("depth")
    start = starts[starts.shape[0] - 1].astype(jnp.float32) + traces[...].astype(jnp.float32)
    for other in kept:
        start = start + other[...].astype(jnp.float32)
    row[:, :cells] = start.astype(jnp.bfloat16)

    def take(phase):
        messages = received[phase * len(swaps) : (phase + 1) * len(swaps)]
        messages = [ref[ref.shape[0] - part :] for ref in messages]
        row[:, cells:] = halo_of(messages, swaps, live[live.shape[0] - 1])

    by_rule = layer < 0
    for at, phase in picks:
        by_rule = by_rule | (layer == at)
        pl.when(layer == at)(functools.partial(take, phase))
    pl.when(jnp.logical_not(by_rule))(functools.partial(take, len(received) // len(swaps) - 1))
    copies = []
    half = cells // LANES // 2 * LANES
    for at, columns in enumerate([slice(0, half), slice(half, cells)]):
        image = dot(row[...], map_ext[:, columns])
        ended[:, columns] = blend(image, row[:, columns], damping[:, columns])
        copies.append(
            pltpu.make_async_copy(ended.at[:, columns], traces_out.at[:, columns], sems.at[at])
        )
        copies[-1].start()
    for copy in copies:
        copy.wait()


def call(kernel, out_shape, operands, in_hbm=(), scratch=(), aliases=None, to_hbm=False):
    spaces = [pltpu.HBM if i in in_hbm else pltpu.VMEM for i in range(len(operands))]
    operands = [
        pltpu.with_memory_space_constraint(x, pltpu.HBM) if i in in_hbm else x
        for i, x in enumerate(operands)
    ]
    return pl.pallas_call(
        kernel,
        out_shape=out_shape,
        in_specs=[pl.BlockSpec(memory_space=space) for space in spaces],
        out_specs=[pl.BlockSpec(memory_space=pl.ANY if to_hbm else pltpu.VMEM)] * len(out_shape),
        scratch_shapes=scratch,
        input_output_aliases=aliases or {},
        compiler_params=pltpu.CompilerParams(vmem_limit_bytes=32 * 1024 * 1024),
    )(*operands)


MESH_AXES = ("depth", "gx", "gy")


def send(x, moves, swap=None):
    sizes = [lax.axis_size(axis) for axis in MESH_AXES]
    pairs = []
    for layer, below in moves:
        for i in range(sizes[1]):
            for j in range(sizes[2]):
                to = {"depth": below, "gx": i, "gy": j}
                if swap is not None:
                    axis, parity, _ = swap
                    to[axis] += 1 if to[axis] % 2 == parity else -1
                spot = [to[axis] for axis in MESH_AXES]
                if all(0 <= s < size for s, size in zip(spot, sizes)):
                    here = (layer * sizes[1] + i) * sizes[2] + j
                    there = (spot[0] * sizes[1] + spot[1]) * sizes[2] + spot[2]
                    pairs.append((here, there))
    return lax.ppermute(x, MESH_AXES, pairs)


def local(arrival, source, assignment, counts, first_map, second_map, damping):
    layers = lax.axis_size("depth")
    slots, cells = arrival.shape[1], arrival.shape[4]
    rounds = source.shape[1]
    arrival = arrival[0, :, 0, 0, :]
    source = source[0, :, :, 0, 0, :]
    counts = counts.transpose(0, 2, 3, 1)
    first_map = first_map[0, 0, 0]
    second_map = second_map[0, 0, 0]
    damping = damping[0, 0]
    swaps = exchanges()
    early_layers = layers - rounds + 1
    soon = rounds - 2

    def array(*shape, kind=jnp.bfloat16):
        return jax.ShapeDtypeStruct(shape, kind)

    def scratch(x):
        return pltpu.VMEM(x.shape, x.dtype)

    part = slots // 4
    band = coupling_band(cells)
    whole = array(cells + LANES, cells)
    own = [array(rounds, slots, cells), array(rounds, slots, LANES)]
    copied = [scratch(source), scratch(assignment), pltpu.SMEM(counts.shape, counts.dtype)]
    edge, starts, live = call(
        edges_kernel,
        [array(cells + (rounds - 1) * slots, LANES)] + own,
        [source, assignment, counts, first_map],
        in_hbm=range(4),
        scratch=copied + [scratch(first_map), pltpu.SemaphoreType.DMA((2 + rounds,))],
    )
    edge_next = send(edge, [(layer, layer - 1) for layer in range(1, layers)])
    opened = call(
        functools.partial(opening_kernel, early_layers, swaps),
        own + [array(LANES, cells)] + [array(rounds * part, LANES)] * len(swaps),
        [source, assignment, counts, arrival, first_map, starts, live],
        in_hbm=range(3),
        scratch=copied + [pltpu.SemaphoreType.DMA((2 + rounds,))],
        aliases={5: 0, 6: 1},
    )
    starts, live, edge_cells = opened[:3]
    received = [
        send(m, [(layer, layer) for layer in range(early_layers)], swap)
        for m, swap in zip(opened[3:], swaps)
    ]
    traces, map_ext, band = call(
        functools.partial(inside_kernel, early_layers),
        [array(soon * slots, cells, kind=jnp.float32), whole, array(*band.shape)],
        [starts, first_map, second_map, edge_cells, band],
        in_hbm=(4,),
        scratch=[pltpu.SemaphoreType.DMA],
    )
    opened = received
    arrived = list(opened)
    picks = [(0, 0)]
    kept = []
    for step in range(rounds - 1):
        chains = min(rounds - 1 - step, soon)
        last = step == rounds - 2
        keeps = step + chains == rounds - 1 and not last
        going = (chains - 1 if keeps else chains) * slots
        outs = [array(going, cells)] + [array(slots, cells)] * keeps
        outs += [array(chains * part, LANES)] * len(swaps)
        operands = [starts, live, map_ext, damping, edge_next, traces] + received
        ended = call(
            functools.partial(step_kernel, swaps, step, chains, keeps, early_layers),
            outs,
            operands + (opened if last else []),
        )
        moves = [(layer, layer + 1) for layer in range(step, step + early_layers)]
        if last:
            moves.append((0, 1))
        traces = send(ended[0], moves)
        if keeps:
            kept.append(send(ended[1], [(step, step + 1)]))
            picks.append((step + 1, len(arrived) // len(swaps)))
        received = [send(m, moves, swap) for m, swap in zip(ended[-len(swaps) :], swaps)]
        if step > 0:
            arrived += received
        if step == 0:
            (map_ext,) = call(
                functools.partial(whole_map_kernel, early_layers),
                [whole],
                [first_map, band, second_map, map_ext],
                aliases={3: 0},
            )
    (ended,) = call(
        functools.partial(final_kernel, swaps, picks, len(kept)),
        [array(slots, cells)],
        [live, starts, map_ext, damping, traces] + kept + arrived,
        scratch=[
            pltpu.VMEM((slots, cells + LANES), jnp.bfloat16),
            scratch(arrival),
            pltpu.SemaphoreType.DMA((2,)),
        ],
        to_hbm=True,
    )
    return ended.reshape(1, slots, 1, 1, cells)


def solution(mesh):
    return jax.shard_map(
        local,
        mesh=mesh,
        in_specs=(
            P("depth", None, "gx", "gy", None),
            P("depth", None, None, "gx", "gy", None),
            P(),
            P(None, None, "gx", "gy"),
            P("depth", "gx", "gy", None, None),
            P("depth", "gx", "gy", None, None),
            P("depth", "gx", "gy", None),
        ),
        out_specs=P("depth", None, "gx", "gy", None),
        check_vma=False,
    )
```

```python
import functools

import jax
import jax.numpy as jnp
import numpy as np
from jax import lax
from jax.experimental import pallas as pl
from jax.experimental.pallas import tpu as pltpu
from jax.sharding import PartitionSpec as P

FX = 32
FY = 28
SHOT_BATCH = 16

coupling_weight = 0.25

LANES = 128
GROUP = LANES // 4
EDGE_AXES = (("gx", 0), ("gy", 2))


def dot(a, b):
    return jnp.dot(a, b, preferred_element_type=jnp.float32)


def dot_t(a, b):
    return lax.dot_general(a, b, (((0,), (0,)), ((), ())), preferred_element_type=jnp.float32)


def group_at(lane):
    return lax.shift_right_logical(lane, GROUP.bit_length() - 1)


def edge_cells_of(lane):
    group, spot = group_at(lane), lane & (GROUP - 1)
    along_y = jnp.where(group == 0, spot, spot + (FX - 1) * FY)
    along_x = jnp.where(group == 2, spot * FY, spot * FY + FY - 1)
    cell = jnp.where(group < 2, along_y, along_x)
    return jnp.where(spot < jnp.where(group < 2, FY, FX), cell, -1)


def edge_selector(cells):
    cell = edge_cells_of(lax.broadcasted_iota(jnp.int32, (1, LANES), 1))
    row = lax.broadcasted_iota(jnp.int32, (cells, LANES), 0)
    return jnp.where(row == cell, 1.0, 0.0).astype(jnp.bfloat16)


def edge_rows_selector(cells):
    cell = edge_cells_of(lax.broadcasted_iota(jnp.int32, (LANES, 1), 0))
    row = lax.broadcasted_iota(jnp.int32, (LANES, cells), 1)
    return jnp.where(row == cell, 1.0, 0.0).astype(jnp.bfloat16)


def exchanges():
    found = []
    for axis, base in EDGE_AXES:
        for parity in range(min(lax.axis_size(axis) - 1, 2)):
            found.append((axis, parity, base))
    return found[::-1]


def groups_of(swaps):
    index = {axis: lax.axis_index(axis) & 1 for axis, _ in EDGE_AXES}
    return [jnp.where(index[axis] == parity, base + 1, base) for axis, parity, base in swaps]


def pack(edges, group):
    rows = edges.shape[0] // 4
    lane_group = group_at(lax.broadcasted_iota(jnp.int32, (rows, LANES), 1))
    packed = jnp.zeros((rows, LANES), jnp.float32)
    for part in range(4):
        piece = edges[part * rows : (part + 1) * rows]
        piece = pltpu.roll(piece, ((part - group) & 3) * GROUP, 1)
        packed = jnp.where(lane_group == part, piece, packed)
    return packed.astype(jnp.bfloat16)


def unpack(packed, group):
    lane_group = group_at(lax.broadcasted_iota(jnp.int32, packed.shape, 1))
    pieces = []
    for part in range(4):
        piece = pltpu.roll(packed, ((group - part) & 3) * GROUP, 1)
        pieces.append(jnp.where(lane_group == group, piece, 0.0))
    return jnp.concatenate(pieces, axis=0)


def first_unit(layer):
    return lax.axis_size("depth") - 1 - layer


def chosen_of(wanted, counts_in, unit):
    slots = wanted.shape[1]
    shot = lax.broadcasted_iota(jnp.int32, (slots, slots), 0)
    slot = lax.broadcasted_iota(jnp.int32, (1, slots), 1)
    live = jnp.zeros((1, slots), jnp.int32)
    for batch in range(slots // SHOT_BATCH):
        count = counts_in[unit, 0, 0, batch]
        live = jnp.where(slot >= batch * SHOT_BATCH, count + batch * SHOT_BATCH, live)
    wanted = jnp.where(slot < live, wanted, -1)
    return jnp.where(shot == wanted, 1.0, 0.0).astype(jnp.bfloat16)


def started(pairs, sems):
    copies = [
        pltpu.make_async_copy(here, there, sems.at[i]) for i, (here, there) in enumerate(pairs)
    ]
    for copy in copies:
        copy.start()
    return copies


def fill_live(live_out, counts_in, unit):
    position = lax.broadcasted_iota(jnp.int32, (SHOT_BATCH, LANES), 0)
    rounds, slots = live_out.shape[:2]
    for round_number in range(rounds):
        for batch in range(slots // SHOT_BATCH):
            count = counts_in[unit + round_number, 0, 0, batch]
            rows = slice(batch * SHOT_BATCH, (batch + 1) * SHOT_BATCH)
            live_out[round_number, rows] = jnp.where(position < count, 1.0, 0.0).astype(
                jnp.bfloat16
            )


def edges_kernel(source, assignment, counts, first_map, edge_out, starts_out, live_out, *refs):
    source_in, assignment_in, counts_in, first_in, sems = refs
    rounds, slots, cells = source.shape
    layer = lax.axis_index("depth")

    @pl.when(layer > 0)
    def _():
        unit = first_unit(layer)
        pairs = [(counts, counts_in), (assignment, assignment_in), (first_map, first_in)]
        pairs += [(source.at[r], source_in.at[r]) for r in range(1, rounds)]
        copies = started(pairs, sems)
        selector = edge_selector(cells)
        copies[0].wait()
        fill_live(live_out, counts_in, unit)
        copies[1].wait()
        copies[2].wait()
        first_edge = dot(first_in[...], selector).astype(jnp.bfloat16)
        edge_out[:cells] = first_edge
        for r in range(1, rounds):
            copies[2 + r].wait()
            chosen = chosen_of(assignment_in[r : r + 1], counts_in, unit + r)
            starts_out[r] = dot_t(chosen, source_in[r]).astype(jnp.bfloat16)
        edges = dot(starts_out[1:].reshape(-1, cells), first_edge)
        edge_out[cells:] = edges.astype(jnp.bfloat16)


def opening_kernel(early_layers, swaps, source, assignment, counts, arrival, first_map, *refs):
    starts_out, live_out, edge_cells = refs[2:5]
    messages = refs[5 : 5 + len(swaps)]
    source_in, assignment_in, counts_in, sems = refs[5 + len(swaps) :]
    rounds, slots, cells = source.shape
    part = slots // 4
    layer = lax.axis_index("depth")
    early = layer < early_layers

    @pl.when(jnp.logical_not(early))
    def _():
        edge_cells[...] = edge_rows_selector(cells)

    @pl.when(early)
    def _():
        unit = first_unit(layer)
        groups = groups_of(swaps)
        pairs = [(counts, counts_in), (assignment, assignment_in)]
        pairs += [(source.at[r], source_in.at[r]) for r in range(rounds)]
        copies = started(pairs, sems)
        edge_cells[...] = edge_rows_selector(cells)
        first_edge = dot(first_map[...], edge_selector(cells)).astype(jnp.bfloat16)
        copies[0].wait()
        fill_live(live_out, counts_in, unit)
        copies[1].wait()
        for r in range(rounds):
            chosen = chosen_of(assignment_in[r : r + 1], counts_in, unit + r)
            copies[2 + r].wait()
            picked = dot_t(chosen, source_in[r])
            if r == 0:
                live = live_out[0].astype(jnp.float32)
                live = jnp.concatenate([live] * (cells // LANES), axis=1)
                picked = picked + live * arrival[...].astype(jnp.float32)
            picked = picked.astype(jnp.bfloat16)
            starts_out[r] = picked
            edges = dot(picked, first_edge)
            for message, group in zip(messages, groups):
                message[r * part : (r + 1) * part] = pack(edges, group)


def bands(cells):
    found = []
    for at in range(0, cells, 2 * LANES):
        end = min(at + 2 * LANES, cells)
        found.append((slice(max(at - LANES, 0), min(end + LANES, cells)), slice(at, end)))
    return found


def coupling_band(cells):
    cell = np.arange(cells)
    apart = np.abs(cell[:, None] - cell[None, :])
    same_row = cell[:, None] // FY == cell[None, :] // FY
    linked = (apart == FY) | ((apart == 1) & same_row)
    coupling = np.eye(cells) + coupling_weight * linked
    band = np.zeros((len(bands(cells)), 4 * LANES, 2 * LANES), np.float32)
    for block, (rows, columns) in zip(band, bands(cells)):
        piece = coupling[rows, columns]
        block[: piece.shape[0], : piece.shape[1]] = piece
    return jnp.asarray(band, jnp.bfloat16)


def coupled(x, band):
    pieces = []
    for at, (rows, columns) in enumerate(bands(x.shape[1])):
        height, width = rows.stop - rows.start, columns.stop - columns.start
        pieces.append(dot(x[:, rows], band[at, :height, :width]).astype(jnp.bfloat16))
    return jnp.concatenate(pieces, axis=1)


def fill_whole_map(first_map, band, second_map, whole_ext):
    cells = second_map.shape[0]
    whole_ext[:cells] = dot(coupled(first_map[...], band), second_map[...]).astype(jnp.bfloat16)


def inside_kernel(early_layers, starts, first_map, second_map, edge_cells, band, *refs):
    image_out, whole_ext, band_in, sem = refs
    slots, cells = starts.shape[1:]
    chains = image_out.shape[0] // slots
    early = lax.axis_index("depth") < early_layers
    copy = pltpu.make_async_copy(band, band_in, sem)
    copy.start()
    edge_rows = dot(edge_cells[...], second_map[...])
    whole_ext[cells:] = (coupling_weight * edge_rows).astype(jnp.bfloat16)

    @pl.when(early)
    def _():
        mapped = dot(starts[:chains].reshape(-1, cells), first_map[...]).astype(jnp.bfloat16)
        copy.wait()
        image_out[...] = dot(coupled(mapped, band_in), second_map[...])

    @pl.when(jnp.logical_not(early))
    def _():
        copy.wait()
        fill_whole_map(first_map, band_in, second_map, whole_ext)


def whole_map_kernel(early_layers, first_map, band, second_map, whole_in, whole_ext):
    del whole_in

    @pl.when(lax.axis_index("depth") < early_layers)
    def _():
        fill_whole_map(first_map, band, second_map, whole_ext)


def halo_of(messages, groups, live):
    halo = 0.0
    for message, group in zip(messages, groups):
        halo = halo + unpack(message.astype(jnp.float32), group)
    return (halo * live.astype(jnp.float32)).astype(jnp.bfloat16)


def blend(image, start, damp):
    return (damp * image + (1.0 - damp) * start.astype(jnp.float32)).astype(jnp.bfloat16)


def step_kernel(swaps, step, chains, keeps, early_layers, *refs):
    starts, live, map_ext, damping, edge_next, traces = refs[:6]
    received = refs[6 : 6 + len(swaps)]
    opened = refs[6 + len(swaps) : -1 - len(swaps) - keeps]
    outs = refs[-1 - len(swaps) - keeps :]
    traces_out, messages = outs[0], outs[1 + keeps :]
    slots, cells = starts.shape[1:]
    part = slots // 4
    layer = lax.axis_index("depth")
    here = (layer >= step) & (layer < step + early_layers)
    if opened:
        here = here | (layer == 0)

    @pl.when(here)
    def _():
        groups = groups_of(swaps)
        halo = []
        for chain in range(chains):
            packed = [ref[chain * part : (chain + 1) * part] for ref in received]
            if opened:
                at = (step + chain) * part
                packed = [
                    jnp.where(layer == 0, ref[at : at + part].astype(jnp.float32), x)
                    for ref, x in zip(opened, packed)
                ]
            halo.append(halo_of(packed, groups, live[step + chain]))
        halo = jnp.concatenate(halo, axis=0)
        start = starts[step : step + chains].reshape(-1, cells)
        if step == 0:
            image = traces[...] + dot(halo, map_ext[cells:])
        else:
            start = start.astype(jnp.float32) + traces[...].astype(jnp.float32)
            start = start.astype(jnp.bfloat16)
            image = dot(jnp.concatenate([start, halo], axis=1), map_ext[...])
        ended = blend(image, start, damping[...])
        going = traces_out.shape[0]
        traces_out[...] = ended[:going]
        if keeps:
            outs[1][...] = ended[going:]
        at = cells + step * slots
        edges = dot(ended, edge_next[:cells])
        edges += edge_next[at : at + chains * slots].astype(jnp.float32)
        for message, group in zip(messages, groups):
            for chain in range(chains):
                message[chain * part : (chain + 1) * part] = pack(
                    edges[chain * slots : (chain + 1) * slots], group
                )


def final_kernel(swaps, picks, others, live, starts, map_ext, damping, traces, *refs):
    slots, cells = traces.shape
    kept, received = refs[:others], refs[others:-4]
    traces_out, row, ended, sems = refs[-4:]
    part = slots // 4
    layer = lax.axis_index("depth")
    start = starts[starts.shape[0] - 1].astype(jnp.float32) + traces[...].astype(jnp.float32)
    for other in kept:
        start = start + other[...].astype(jnp.float32)
    row[:, :cells] = start.astype(jnp.bfloat16)

    groups = groups_of(swaps)

    def take(phase):
        messages = received[phase * len(swaps) : (phase + 1) * len(swaps)]
        messages = [ref[ref.shape[0] - part :] for ref in messages]
        row[:, cells:] = halo_of(messages, groups, live[live.shape[0] - 1])

    by_rule = layer < 0
    for at, phase in picks:
        by_rule = by_rule | (layer == at)
        pl.when(layer == at)(functools.partial(take, phase))
    pl.when(jnp.logical_not(by_rule))(functools.partial(take, len(received) // len(swaps) - 1))
    copies = []
    half = cells // LANES // 2 * LANES
    for at, columns in enumerate([slice(0, half), slice(half, cells)]):
        image = dot(row[...], map_ext[:, columns])
        ended[:, columns] = blend(image, row[:, columns], damping[:, columns])
        copies.append(
            pltpu.make_async_copy(ended.at[:, columns], traces_out.at[:, columns], sems.at[at])
        )
        copies[-1].start()
    for copy in copies:
        copy.wait()


def call(kernel, out_shape, operands, in_hbm=(), scratch=(), aliases=None, to_hbm=False):
    spaces = [pltpu.HBM if i in in_hbm else pltpu.VMEM for i in range(len(operands))]
    operands = [
        pltpu.with_memory_space_constraint(x, pltpu.HBM) if i in in_hbm else x
        for i, x in enumerate(operands)
    ]
    return pl.pallas_call(
        kernel,
        out_shape=out_shape,
        in_specs=[pl.BlockSpec(memory_space=space) for space in spaces],
        out_specs=[pl.BlockSpec(memory_space=pl.ANY if to_hbm else pltpu.VMEM)] * len(out_shape),
        scratch_shapes=scratch,
        input_output_aliases=aliases or {},
        compiler_params=pltpu.CompilerParams(vmem_limit_bytes=32 * 1024 * 1024),
    )(*operands)


MESH_AXES = ("depth", "gx", "gy")


def send(x, moves, swap=None):
    sizes = [lax.axis_size(axis) for axis in MESH_AXES]
    pairs = []
    for layer, below in moves:
        for i in range(sizes[1]):
            for j in range(sizes[2]):
                to = {"depth": below, "gx": i, "gy": j}
                if swap is not None:
                    axis, parity, _ = swap
                    to[axis] += 1 if to[axis] % 2 == parity else -1
                spot = [to[axis] for axis in MESH_AXES]
                if all(0 <= s < size for s, size in zip(spot, sizes)):
                    here = (layer * sizes[1] + i) * sizes[2] + j
                    there = (spot[0] * sizes[1] + spot[1]) * sizes[2] + spot[2]
                    pairs.append((here, there))
    return lax.ppermute(x, MESH_AXES, pairs)


def local(arrival, source, assignment, counts, first_map, second_map, damping):
    layers = lax.axis_size("depth")
    slots, cells = arrival.shape[1], arrival.shape[4]
    rounds = source.shape[1]
    arrival = arrival[0, :, 0, 0, :]
    source = source[0, :, :, 0, 0, :]
    counts = counts.transpose(0, 2, 3, 1)
    first_map = first_map[0, 0, 0]
    second_map = second_map[0, 0, 0]
    damping = damping[0, 0]
    swaps = exchanges()
    early_layers = layers - rounds + 1
    soon = rounds - 2

    def array(*shape, kind=jnp.bfloat16):
        return jax.ShapeDtypeStruct(shape, kind)

    def scratch(x):
        return pltpu.VMEM(x.shape, x.dtype)

    part = slots // 4
    band = coupling_band(cells)
    whole = array(cells + LANES, cells)
    own = [array(rounds, slots, cells), array(rounds, slots, LANES)]
    copied = [scratch(source), scratch(assignment), pltpu.SMEM(counts.shape, counts.dtype)]
    edge, starts, live = call(
        edges_kernel,
        [array(cells + (rounds - 1) * slots, LANES)] + own,
        [source, assignment, counts, first_map],
        in_hbm=range(4),
        scratch=copied + [scratch(first_map), pltpu.SemaphoreType.DMA((2 + rounds,))],
    )
    edge_next = send(edge, [(layer, layer - 1) for layer in range(1, layers)])
    opened = call(
        functools.partial(opening_kernel, early_layers, swaps),
        own + [array(LANES, cells)] + [array(rounds * part, LANES)] * len(swaps),
        [source, assignment, counts, arrival, first_map, starts, live],
        in_hbm=range(3),
        scratch=copied + [pltpu.SemaphoreType.DMA((2 + rounds,))],
        aliases={5: 0, 6: 1},
    )
    starts, live, edge_cells = opened[:3]
    received = [
        send(m, [(layer, layer) for layer in range(early_layers)], swap)
        for m, swap in zip(opened[3:], swaps)
    ]
    traces, map_ext, band = call(
        functools.partial(inside_kernel, early_layers),
        [array(soon * slots, cells, kind=jnp.float32), whole, array(*band.shape)],
        [starts, first_map, second_map, edge_cells, band],
        in_hbm=(4,),
        scratch=[pltpu.SemaphoreType.DMA],
    )
    opened = received
    arrived = list(opened)
    picks = [(0, 0)]
    kept = []
    for step in range(rounds - 1):
        chains = min(rounds - 1 - step, soon)
        last = step == rounds - 2
        keeps = step + chains == rounds - 1 and not last
        going = (chains - 1 if keeps else chains) * slots
        outs = [array(going, cells)] + [array(slots, cells)] * keeps
        outs += [array(chains * part, LANES)] * len(swaps)
        operands = [starts, live, map_ext, damping, edge_next, traces] + received
        ended = call(
            functools.partial(step_kernel, swaps, step, chains, keeps, early_layers),
            outs,
            operands + (opened if last else []),
        )
        moves = [(layer, layer + 1) for layer in range(step, step + early_layers)]
        if last:
            moves.append((0, 1))
        traces = send(ended[0], moves)
        if keeps:
            kept.append(send(ended[1], [(step, step + 1)]))
            picks.append((step + 1, len(arrived) // len(swaps)))
        received = [send(m, moves, swap) for m, swap in zip(ended[-len(swaps) :], swaps)]
        if step > 0:
            arrived += received
        if step == 0:
            (map_ext,) = call(
                functools.partial(whole_map_kernel, early_layers),
                [whole],
                [first_map, band, second_map, map_ext],
                aliases={3: 0},
            )
    (ended,) = call(
        functools.partial(final_kernel, swaps, picks, len(kept)),
        [array(slots, cells)],
        [live, starts, map_ext, damping, traces] + kept + arrived,
        scratch=[
            pltpu.VMEM((slots, cells + LANES), jnp.bfloat16),
            scratch(arrival),
            pltpu.SemaphoreType.DMA((2,)),
        ],
        to_hbm=True,
    )
    return ended.reshape(1, slots, 1, 1, cells)


def solution(mesh):
    return jax.shard_map(
        local,
        mesh=mesh,
        in_specs=(
            P("depth", None, "gx", "gy", None),
            P("depth", None, None, "gx", "gy", None),
            P(),
            P(None, None, "gx", "gy"),
            P("depth", "gx", "gy", None, None),
            P("depth", "gx", "gy", None, None),
            P("depth", "gx", "gy", None),
        ),
        out_specs=P("depth", None, "gx", "gy", None),
        check_vma=False,
    )
```

```python
import functools

import jax
import jax.numpy as jnp
import numpy as np
from jax import lax
from jax.experimental import pallas as pl
from jax.experimental.pallas import tpu as pltpu
from jax.sharding import PartitionSpec as P

FX = 32
FY = 28
SHOT_BATCH = 16

coupling_weight = 0.25

LANES = 128
GROUP = LANES // 4
EDGE_AXES = (("gx", 0), ("gy", 2))


def dot(a, b):
    return jnp.dot(a, b, preferred_element_type=jnp.float32)


def dot_t(a, b):
    return lax.dot_general(a, b, (((0,), (0,)), ((), ())), preferred_element_type=jnp.float32)


def group_at(lane):
    return lax.shift_right_logical(lane, GROUP.bit_length() - 1)


def edge_cells_of(lane):
    group, spot = group_at(lane), lane & (GROUP - 1)
    along_y = jnp.where(group == 0, spot, spot + (FX - 1) * FY)
    along_x = jnp.where(group == 2, spot * FY, spot * FY + FY - 1)
    cell = jnp.where(group < 2, along_y, along_x)
    return jnp.where(spot < jnp.where(group < 2, FY, FX), cell, -1)


def edge_selector(cells):
    cell = edge_cells_of(lax.broadcasted_iota(jnp.int32, (1, LANES), 1))
    row = lax.broadcasted_iota(jnp.int32, (cells, LANES), 0)
    return jnp.where(row == cell, 1.0, 0.0).astype(jnp.bfloat16)


def edge_rows_selector(cells):
    cell = edge_cells_of(lax.broadcasted_iota(jnp.int32, (LANES, 1), 0))
    row = lax.broadcasted_iota(jnp.int32, (LANES, cells), 1)
    return jnp.where(row == cell, 1.0, 0.0).astype(jnp.bfloat16)


def exchanges():
    found = []
    for axis, base in EDGE_AXES:
        for parity in range(min(lax.axis_size(axis) - 1, 2)):
            found.append((axis, parity, base))
    return found[::-1]


def groups_of(swaps):
    index = {axis: lax.axis_index(axis) & 1 for axis, _ in EDGE_AXES}
    return [jnp.where(index[axis] == parity, base + 1, base) for axis, parity, base in swaps]


def pack(edges, group):
    rows = edges.shape[0] // 4
    lane_group = group_at(lax.broadcasted_iota(jnp.int32, (rows, LANES), 1))
    packed = jnp.zeros((rows, LANES), jnp.float32)
    for part in range(4):
        piece = edges[part * rows : (part + 1) * rows]
        piece = pltpu.roll(piece, ((part - group) & 3) * GROUP, 1)
        packed = jnp.where(lane_group == part, piece, packed)
    return packed.astype(jnp.bfloat16)


def unpack(packed, group):
    lane_group = group_at(lax.broadcasted_iota(jnp.int32, packed.shape, 1))
    pieces = []
    for part in range(4):
        piece = pltpu.roll(packed, ((group - part) & 3) * GROUP, 1)
        pieces.append(jnp.where(lane_group == group, piece, 0.0))
    return jnp.concatenate(pieces, axis=0)


def first_unit(layer):
    return lax.axis_size("depth") - 1 - layer


def chosen_of(wanted, counts):
    slots = wanted.shape[1]
    shot = lax.broadcasted_iota(jnp.int32, (slots, slots), 0)
    slot = lax.broadcasted_iota(jnp.int32, (1, slots), 1)
    live = jnp.zeros((1, slots), jnp.int32)
    for batch in range(slots // SHOT_BATCH):
        count = jnp.broadcast_to(counts[:, batch : batch + 1], (1, slots))
        live = jnp.where(slot >= batch * SHOT_BATCH, count + batch * SHOT_BATCH, live)
    wanted = jnp.where(slot < live, wanted, -1)
    return jnp.where(shot == wanted, 1.0, 0.0).astype(jnp.bfloat16)


def started(pairs, sems):
    copies = [
        pltpu.make_async_copy(here, there, sems.at[i]) for i, (here, there) in enumerate(pairs)
    ]
    for copy in copies:
        copy.start()
    return copies


def fill_live(live_out, counts):
    position = lax.broadcasted_iota(jnp.int32, (SHOT_BATCH, LANES), 0)
    for r, own in enumerate(counts):
        for batch in range(own.shape[1]):
            count = jnp.broadcast_to(own[:, batch : batch + 1], (SHOT_BATCH, LANES))
            rows = slice(batch * SHOT_BATCH, (batch + 1) * SHOT_BATCH)
            live_out[r, rows] = jnp.where(position < count, 1.0, 0.0).astype(jnp.bfloat16)


def edges_kernel(source, assignment, counts, first_map, edge_out, starts_out, live_out, *refs):
    source_in, assignment_in, counts_in, first_in, sems = refs
    rounds, slots, cells = source.shape
    layer = lax.axis_index("depth")

    @pl.when(layer > 0)
    def _():
        unit = first_unit(layer)
        pairs = [(counts, counts_in), (assignment, assignment_in), (first_map, first_in)]
        pairs += [(source.at[r], source_in.at[r]) for r in range(1, rounds)]
        copies = started(pairs, sems)
        selector = edge_selector(cells)
        copies[0].wait()
        own = [counts_in[unit + r, 0] for r in range(rounds)]
        fill_live(live_out, own)
        copies[1].wait()
        copies[2].wait()
        first_edge = dot(first_in[...], selector).astype(jnp.bfloat16)
        edge_out[:cells] = first_edge
        for r in range(1, rounds):
            copies[2 + r].wait()
            chosen = chosen_of(assignment_in[r : r + 1], own[r])
            starts_out[r] = dot_t(chosen, source_in[r]).astype(jnp.bfloat16)
        edges = dot(starts_out[1:].reshape(-1, cells), first_edge)
        edge_out[cells:] = edges.astype(jnp.bfloat16)


def opening_kernel(early_layers, swaps, source, assignment_in, counts_in, arrival, first_map, *refs):
    starts_out, live_out, edge_cells = refs[2:5]
    messages = refs[5 : 5 + len(swaps)]
    source_in, sems = refs[5 + len(swaps) :]
    rounds, slots, cells = source.shape
    part = slots // 4
    layer = lax.axis_index("depth")
    early = layer < early_layers

    @pl.when(jnp.logical_not(early))
    def _():
        edge_cells[...] = edge_rows_selector(cells)

    @pl.when(early)
    def _():
        unit = first_unit(layer)
        groups = groups_of(swaps)
        copies = started([(source.at[r], source_in.at[r]) for r in range(rounds)], sems)
        edge_cells[...] = edge_rows_selector(cells)
        first_edge = dot(first_map[...], edge_selector(cells)).astype(jnp.bfloat16)
        own = [counts_in[unit + r, 0] for r in range(rounds)]
        fill_live(live_out, own)
        for r in range(rounds):
            chosen = chosen_of(assignment_in[r : r + 1], own[r])
            copies[r].wait()
            picked = dot_t(chosen, source_in[r])
            if r == 0:
                live = live_out[0].astype(jnp.float32)
                live = jnp.concatenate([live] * (cells // LANES), axis=1)
                picked = picked + live * arrival[...].astype(jnp.float32)
            picked = picked.astype(jnp.bfloat16)
            starts_out[r] = picked
            edges = dot(picked, first_edge)
            for message, group in zip(messages, groups):
                message[r * part : (r + 1) * part] = pack(edges, group)


def bands(cells):
    found = []
    for at in range(0, cells, 2 * LANES):
        end = min(at + 2 * LANES, cells)
        found.append((slice(max(at - LANES, 0), min(end + LANES, cells)), slice(at, end)))
    return found


def coupling_band(cells):
    cell = np.arange(cells)
    apart = np.abs(cell[:, None] - cell[None, :])
    same_row = cell[:, None] // FY == cell[None, :] // FY
    linked = (apart == FY) | ((apart == 1) & same_row)
    coupling = np.eye(cells) + coupling_weight * linked
    band = np.zeros((len(bands(cells)), 4 * LANES, 2 * LANES), np.float32)
    for block, (rows, columns) in zip(band, bands(cells)):
        piece = coupling[rows, columns]
        block[: piece.shape[0], : piece.shape[1]] = piece
    return jnp.asarray(band, jnp.bfloat16)


def coupled(x, band):
    pieces = []
    for at, (rows, columns) in enumerate(bands(x.shape[1])):
        height, width = rows.stop - rows.start, columns.stop - columns.start
        pieces.append(dot(x[:, rows], band[at, :height, :width]).astype(jnp.bfloat16))
    return jnp.concatenate(pieces, axis=1)


def fill_whole_map(first_map, band, second_map, whole_ext):
    cells = second_map.shape[0]
    whole_ext[:cells] = dot(coupled(first_map[...], band), second_map[...]).astype(jnp.bfloat16)


def inside_kernel(early_layers, starts, first_map, second_map, edge_cells, damping, band, *refs):
    traces_out, whole_ext, band_in, sem = refs
    slots, cells = starts.shape[1:]
    chains = traces_out.shape[0] // slots
    early = lax.axis_index("depth") < early_layers
    copy = pltpu.make_async_copy(band, band_in, sem)
    copy.start()
    edge_rows = dot(edge_cells[...], second_map[...])
    whole_ext[cells:] = (coupling_weight * edge_rows).astype(jnp.bfloat16)

    @pl.when(early)
    def _():
        start = starts[:chains].reshape(-1, cells)
        mapped = dot(start, first_map[...]).astype(jnp.bfloat16)
        copy.wait()
        image = dot(coupled(mapped, band_in), second_map[...])
        traces_out[...] = blend(image, start, damping[...])

    @pl.when(jnp.logical_not(early))
    def _():
        copy.wait()
        fill_whole_map(first_map, band_in, second_map, whole_ext)


def whole_map_kernel(early_layers, first_map, band, second_map, whole_in, whole_ext):
    del whole_in

    @pl.when(lax.axis_index("depth") < early_layers)
    def _():
        fill_whole_map(first_map, band, second_map, whole_ext)


def halo_of(messages, groups, live):
    halo = 0.0
    for message, group in zip(messages, groups):
        halo = halo + unpack(message.astype(jnp.float32), group)
    return (halo * live.astype(jnp.float32)).astype(jnp.bfloat16)


def blend(image, start, damp):
    return damp * image + (1.0 - damp) * start.astype(jnp.float32)


def takes_part(step, last, early_layers):
    layer = lax.axis_index("depth")
    here = (layer >= step) & (layer < step + early_layers)
    return here | (layer == 0) if last else here


def inner_kernel(part_of, rounds, starts, map_ext, damping, *refs):
    arrived, out = refs[:-1], refs[-1]
    cells = out.shape[1]

    @pl.when(part_of())
    def _():
        start = starts[rounds].reshape(-1, cells).astype(jnp.float32)
        for traces in arrived:
            start = start + traces[...].astype(jnp.float32)
        start = start.astype(jnp.bfloat16)
        out[...] = blend(dot(start, map_ext[:cells]), start, damping[...])


def step_kernel(swaps, step, chains, keeps, part_of, *refs):
    live, map_ext, damping, edge_next, inner = refs[:5]
    received = refs[5 : 5 + len(swaps)]
    opened = refs[5 + len(swaps) : -1 - len(swaps) - keeps]
    outs = refs[-1 - len(swaps) - keeps :]
    traces_out, messages = outs[0], outs[1 + keeps :]
    cells = inner.shape[1]
    slots = inner.shape[0] // chains
    part = slots // 4

    @pl.when(part_of())
    def _():
        groups = groups_of(swaps)
        upper = lax.axis_index("depth") == 0
        halo = []
        for chain in range(chains):
            packed = [ref[chain * part : (chain + 1) * part] for ref in received]
            if opened:
                at = (step + chain) * part
                packed = [
                    jnp.where(upper, ref[at : at + part].astype(jnp.float32), x)
                    for ref, x in zip(opened, packed)
                ]
            halo.append(halo_of(packed, groups, live[step + chain]))
        halo = jnp.concatenate(halo, axis=0)
        ended = inner[...] + damping[...] * dot(halo, map_ext[cells:])
        ended = ended.astype(jnp.bfloat16)
        going = traces_out.shape[0]
        traces_out[...] = ended[:going]
        if keeps:
            outs[1][...] = ended[going:]
        at = cells + step * slots
        edges = dot(ended, edge_next[:cells])
        edges += edge_next[at : at + chains * slots].astype(jnp.float32)
        for message, group in zip(messages, groups):
            for chain in range(chains):
                message[chain * part : (chain + 1) * part] = pack(
                    edges[chain * slots : (chain + 1) * slots], group
                )


def final_kernel(swaps, picks, live, map_ext, damping, inner, *refs):
    slots, cells = inner.shape
    received = refs[:-4]
    traces_out, halo, ended, sems = refs[-4:]
    part = slots // 4
    layer = lax.axis_index("depth")
    groups = groups_of(swaps)

    def take(phase):
        messages = received[phase * len(swaps) : (phase + 1) * len(swaps)]
        messages = [ref[ref.shape[0] - part :] for ref in messages]
        halo[...] = halo_of(messages, groups, live[live.shape[0] - 1])

    by_rule = layer < 0
    for at, phase in picks:
        by_rule = by_rule | (layer == at)
        pl.when(layer == at)(functools.partial(take, phase))
    pl.when(jnp.logical_not(by_rule))(functools.partial(take, len(received) // len(swaps) - 1))
    copies = []
    half = cells // LANES // 2 * LANES
    for at, columns in enumerate([slice(0, half), slice(half, cells)]):
        image = dot(halo[...], map_ext[cells:, columns])
        ended[:, columns] = (inner[:, columns] + damping[:, columns] * image).astype(jnp.bfloat16)
        copies.append(
            pltpu.make_async_copy(ended.at[:, columns], traces_out.at[:, columns], sems.at[at])
        )
        copies[-1].start()
    for copy in copies:
        copy.wait()


def call(kernel, out_shape, operands, in_hbm=(), scratch=(), aliases=None, to_hbm=False):
    spaces = [pltpu.HBM if i in in_hbm else pltpu.VMEM for i in range(len(operands))]
    operands = [
        pltpu.with_memory_space_constraint(x, pltpu.HBM) if i in in_hbm else x
        for i, x in enumerate(operands)
    ]
    return pl.pallas_call(
        kernel,
        out_shape=out_shape,
        in_specs=[pl.BlockSpec(memory_space=space) for space in spaces],
        out_specs=[pl.BlockSpec(memory_space=pl.ANY if to_hbm else pltpu.VMEM)] * len(out_shape),
        scratch_shapes=scratch,
        input_output_aliases=aliases or {},
        compiler_params=pltpu.CompilerParams(vmem_limit_bytes=32 * 1024 * 1024),
    )(*operands)


MESH_AXES = ("depth", "gx", "gy")


def send(x, moves, swap=None):
    sizes = [lax.axis_size(axis) for axis in MESH_AXES]
    pairs = []
    for layer, below in moves:
        for i in range(sizes[1]):
            for j in range(sizes[2]):
                to = {"depth": below, "gx": i, "gy": j}
                if swap is not None:
                    axis, parity, _ = swap
                    to[axis] += 1 if to[axis] % 2 == parity else -1
                spot = [to[axis] for axis in MESH_AXES]
                if all(0 <= s < size for s, size in zip(spot, sizes)):
                    here = (layer * sizes[1] + i) * sizes[2] + j
                    there = (spot[0] * sizes[1] + spot[1]) * sizes[2] + spot[2]
                    pairs.append((here, there))
    return lax.ppermute(x, MESH_AXES, pairs)


def local(arrival, source, assignment, counts, first_map, second_map, damping):
    layers = lax.axis_size("depth")
    slots, cells = arrival.shape[1], arrival.shape[4]
    rounds = source.shape[1]
    arrival = arrival[0, :, 0, 0, :]
    source = source[0, :, :, 0, 0, :]
    counts = counts.transpose(0, 2, 3, 1)
    first_map = first_map[0, 0, 0]
    second_map = second_map[0, 0, 0]
    damping = damping[0, 0]
    swaps = exchanges()
    early_layers = layers - rounds + 1
    soon = rounds - 2

    def array(*shape, kind=jnp.bfloat16):
        return jax.ShapeDtypeStruct(shape, kind)

    def scratch(x):
        return pltpu.VMEM(x.shape, x.dtype)

    part = slots // 4
    band = coupling_band(cells)
    whole = array(cells + LANES, cells)
    own = [array(rounds, slots, cells), array(rounds, slots, LANES)]
    copied = [scratch(source), scratch(assignment), scratch(counts)]
    edge, starts, live = call(
        edges_kernel,
        [array(cells + (rounds - 1) * slots, LANES)] + own,
        [source, assignment, counts, first_map],
        in_hbm=range(4),
        scratch=copied + [scratch(first_map), pltpu.SemaphoreType.DMA((2 + rounds,))],
    )
    edge_next = send(edge, [(layer, layer - 1) for layer in range(1, layers)])
    opened = call(
        functools.partial(opening_kernel, early_layers, swaps),
        own + [array(LANES, cells)] + [array(rounds * part, LANES)] * len(swaps),
        [source, assignment, counts, arrival, first_map, starts, live],
        in_hbm=range(1),
        scratch=[scratch(source), pltpu.SemaphoreType.DMA((rounds,))],
        aliases={5: 0, 6: 1},
    )
    starts, live, edge_cells = opened[:3]
    received = [
        send(m, [(layer, layer) for layer in range(early_layers)], swap)
        for m, swap in zip(opened[3:], swaps)
    ]
    inner, map_ext, band = call(
        functools.partial(inside_kernel, early_layers),
        [array(soon * slots, cells, kind=jnp.float32), whole, array(*band.shape)],
        [starts, first_map, second_map, edge_cells, damping, band],
        in_hbm=(5,),
        scratch=[pltpu.SemaphoreType.DMA],
    )
    opened = received
    arrived = list(opened)
    picks = [(0, 0)]
    kept = []
    for step in range(rounds - 1):
        chains = min(rounds - 1 - step, soon)
        last = step == rounds - 2
        keeps = step + chains == rounds - 1 and not last
        going = (chains - 1 if keeps else chains) * slots
        outs = [array(going, cells)] + [array(slots, cells)] * keeps
        outs += [array(chains * part, LANES)] * len(swaps)
        part_of = functools.partial(takes_part, step, last, early_layers)
        if step > 0:
            now = slice(step, step + chains)
            (inner,) = call(
                functools.partial(inner_kernel, part_of, now),
                [array(chains * slots, cells, kind=jnp.float32)],
                [starts, map_ext, damping, traces],
            )
        operands = [live, map_ext, damping, edge_next, inner] + received
        ended = call(
            functools.partial(step_kernel, swaps, step, chains, keeps, part_of),
            outs,
            operands + (opened if last else []),
        )
        moves = [(layer, layer + 1) for layer in range(step, step + early_layers)]
        if last:
            moves.append((0, 1))
        traces = send(ended[0], moves)
        if keeps:
            kept.append(send(ended[1], [(step, step + 1)]))
            picks.append((step + 1, len(arrived) // len(swaps)))
        received = [send(m, moves, swap) for m, swap in zip(ended[-len(swaps) :], swaps)]
        if step > 0:
            arrived += received
        if step == 0:
            (map_ext,) = call(
                functools.partial(whole_map_kernel, early_layers),
                [whole],
                [first_map, band, second_map, map_ext],
                aliases={3: 0},
            )
    (inner,) = call(
        functools.partial(inner_kernel, lambda: lax.axis_index("depth") >= 0, slice(rounds - 1, rounds)),
        [array(slots, cells, kind=jnp.float32)],
        [starts, map_ext, damping, traces] + kept,
    )
    (ended,) = call(
        functools.partial(final_kernel, swaps, picks),
        [array(slots, cells)],
        [live, map_ext, damping, inner] + arrived,
        scratch=[
            pltpu.VMEM((slots, LANES), jnp.bfloat16),
            scratch(arrival),
            pltpu.SemaphoreType.DMA((2,)),
        ],
        to_hbm=True,
    )
    return ended.reshape(1, slots, 1, 1, cells)


def solution(mesh):
    return jax.shard_map(
        local,
        mesh=mesh,
        in_specs=(
            P("depth", None, "gx", "gy", None),
            P("depth", None, None, "gx", "gy", None),
            P(),
            P(None, None, "gx", "gy"),
            P("depth", "gx", "gy", None, None),
            P("depth", "gx", "gy", None, None),
            P("depth", "gx", "gy", None),
        ),
        out_specs=P("depth", None, "gx", "gy", None),
        check_vma=False,
    )
```

```python
import functools

import jax
import jax.numpy as jnp
import numpy as np
from jax import lax
from jax.experimental import pallas as pl
from jax.experimental.pallas import tpu as pltpu
from jax.sharding import PartitionSpec as P

FX = 32
FY = 28
SHOT_BATCH = 16

coupling_weight = 0.25

LANES = 128
GROUP = LANES // 4
EDGE_AXES = (("gx", 0), ("gy", 2))


def dot(a, b):
    return jnp.dot(a, b, preferred_element_type=jnp.float32)


def dot_t(a, b):
    return lax.dot_general(a, b, (((0,), (0,)), ((), ())), preferred_element_type=jnp.float32)


def group_at(lane):
    return lax.shift_right_logical(lane, GROUP.bit_length() - 1)


def edge_cells_of(lane):
    group, spot = group_at(lane), lane & (GROUP - 1)
    along_y = jnp.where(group == 0, spot, spot + (FX - 1) * FY)
    along_x = jnp.where(group == 2, spot * FY, spot * FY + FY - 1)
    cell = jnp.where(group < 2, along_y, along_x)
    return jnp.where(spot < jnp.where(group < 2, FY, FX), cell, -1)


def edge_selector(cells):
    cell = edge_cells_of(lax.broadcasted_iota(jnp.int32, (1, LANES), 1))
    row = lax.broadcasted_iota(jnp.int32, (cells, LANES), 0)
    return jnp.where(row == cell, 1.0, 0.0).astype(jnp.bfloat16)


def edge_rows_selector(cells):
    cell = edge_cells_of(lax.broadcasted_iota(jnp.int32, (LANES, 1), 0))
    row = lax.broadcasted_iota(jnp.int32, (LANES, cells), 1)
    return jnp.where(row == cell, 1.0, 0.0).astype(jnp.bfloat16)


def exchanges():
    found = []
    for axis, base in EDGE_AXES:
        for parity in range(min(lax.axis_size(axis) - 1, 2)):
            found.append((axis, parity, base))
    return found[::-1]


def groups_of(swaps):
    index = {axis: lax.axis_index(axis) & 1 for axis, _ in EDGE_AXES}
    return [jnp.where(index[axis] == parity, base + 1, base) for axis, parity, base in swaps]


def pack(edges, group):
    rows = edges.shape[0] // 4
    lane_group = group_at(lax.broadcasted_iota(jnp.int32, (rows, LANES), 1))
    packed = jnp.zeros((rows, LANES), jnp.float32)
    for part in range(4):
        piece = edges[part * rows : (part + 1) * rows]
        piece = pltpu.roll(piece, ((part - group) & 3) * GROUP, 1)
        packed = jnp.where(lane_group == part, piece, packed)
    return packed.astype(jnp.bfloat16)


def unpack(packed, group):
    lane_group = group_at(lax.broadcasted_iota(jnp.int32, packed.shape, 1))
    pieces = []
    for part in range(4):
        piece = pltpu.roll(packed, ((group - part) & 3) * GROUP, 1)
        pieces.append(jnp.where(lane_group == group, piece, 0.0))
    return jnp.concatenate(pieces, axis=0)


def first_unit(layer):
    return lax.axis_size("depth") - 1 - layer


def chosen_of(wanted, counts):
    slots = wanted.shape[1]
    shot = lax.broadcasted_iota(jnp.int32, (slots, slots), 0)
    slot = lax.broadcasted_iota(jnp.int32, (1, slots), 1)
    live = jnp.zeros((1, slots), jnp.int32)
    for batch in range(slots // SHOT_BATCH):
        count = jnp.broadcast_to(counts[:, batch : batch + 1], (1, slots))
        live = jnp.where(slot >= batch * SHOT_BATCH, count + batch * SHOT_BATCH, live)
    wanted = jnp.where(slot < live, wanted, -1)
    return jnp.where(shot == wanted, 1.0, 0.0).astype(jnp.bfloat16)


def started(pairs, sems):
    copies = [
        pltpu.make_async_copy(here, there, sems.at[i]) for i, (here, there) in enumerate(pairs)
    ]
    for copy in copies:
        copy.start()
    return copies


def fill_live(live_out, counts):
    position = lax.broadcasted_iota(jnp.int32, (SHOT_BATCH, LANES), 0)
    for r, own in enumerate(counts):
        for batch in range(own.shape[1]):
            count = jnp.broadcast_to(own[:, batch : batch + 1], (SHOT_BATCH, LANES))
            rows = slice(batch * SHOT_BATCH, (batch + 1) * SHOT_BATCH)
            live_out[r, rows] = jnp.where(position < count, 1.0, 0.0).astype(jnp.bfloat16)


def edges_kernel(source, assignment, counts, first_map, edge_out, starts_out, live_out, *refs):
    source_in, assignment_in, counts_in, first_in, sems = refs
    rounds, slots, cells = source.shape
    layer = lax.axis_index("depth")

    @pl.when(layer > 0)
    def _():
        unit = first_unit(layer)
        pairs = [(counts, counts_in), (assignment, assignment_in), (first_map, first_in)]
        pairs += [(source.at[r], source_in.at[r]) for r in range(1, rounds)]
        copies = started(pairs, sems)
        selector = edge_selector(cells)
        copies[0].wait()
        own = [counts_in[unit + r, 0] for r in range(rounds)]
        fill_live(live_out, own)
        copies[1].wait()
        copies[2].wait()
        first_edge = dot(first_in[...], selector).astype(jnp.bfloat16)
        edge_out[:cells] = first_edge
        for r in range(1, rounds):
            copies[2 + r].wait()
            chosen = chosen_of(assignment_in[r : r + 1], own[r])
            starts_out[r] = dot_t(chosen, source_in[r]).astype(jnp.bfloat16)
        edges = dot(starts_out[1:].reshape(-1, cells), first_edge)
        edge_out[cells:] = edges.astype(jnp.bfloat16)


def opening_kernel(early_layers, swaps, source, assignment_in, counts_in, arrival, first_map, *refs):
    starts_out, live_out, edge_cells = refs[2:5]
    messages = refs[5 : 5 + len(swaps)]
    source_in, sems = refs[5 + len(swaps) :]
    rounds, slots, cells = source.shape
    part = slots // 4
    layer = lax.axis_index("depth")
    early = layer < early_layers

    @pl.when(jnp.logical_not(early))
    def _():
        edge_cells[...] = edge_rows_selector(cells)

    @pl.when(early)
    def _():
        unit = first_unit(layer)
        groups = groups_of(swaps)
        copies = started([(source.at[r], source_in.at[r]) for r in range(rounds)], sems)
        edge_cells[...] = edge_rows_selector(cells)
        first_edge = dot(first_map[...], edge_selector(cells)).astype(jnp.bfloat16)
        own = [counts_in[unit + r, 0] for r in range(rounds)]
        fill_live(live_out, own)
        chosen = [chosen_of(assignment_in[r : r + 1], own[r]) for r in range(rounds)]
        for r in range(rounds):
            copies[r].wait()
            picked = dot_t(chosen[r], source_in[r])
            if r == 0:
                live = live_out[0].astype(jnp.float32)
                live = jnp.concatenate([live] * (cells // LANES), axis=1)
                picked = picked + live * arrival[...].astype(jnp.float32)
            picked = picked.astype(jnp.bfloat16)
            starts_out[r] = picked
            edges = dot(picked, first_edge)
            for message, group in zip(messages, groups):
                message[r * part : (r + 1) * part] = pack(edges, group)


def bands(cells):
    found = []
    for at in range(0, cells, 2 * LANES):
        end = min(at + 2 * LANES, cells)
        found.append((slice(max(at - LANES, 0), min(end + LANES, cells)), slice(at, end)))
    return found


def coupling_band(cells):
    cell = np.arange(cells)
    apart = np.abs(cell[:, None] - cell[None, :])
    same_row = cell[:, None] // FY == cell[None, :] // FY
    linked = (apart == FY) | ((apart == 1) & same_row)
    coupling = np.eye(cells) + coupling_weight * linked
    band = np.zeros((len(bands(cells)), 4 * LANES, 2 * LANES), np.float32)
    for block, (rows, columns) in zip(band, bands(cells)):
        piece = coupling[rows, columns]
        block[: piece.shape[0], : piece.shape[1]] = piece
    return jnp.asarray(band, jnp.bfloat16)


def coupled(x, band):
    pieces = []
    for at, (rows, columns) in enumerate(bands(x.shape[1])):
        height, width = rows.stop - rows.start, columns.stop - columns.start
        pieces.append(dot(x[:, rows], band[at, :height, :width]).astype(jnp.bfloat16))
    return jnp.concatenate(pieces, axis=1)


def fill_whole_map(first_map, band, second_map, whole_ext):
    cells = second_map.shape[0]
    whole_ext[:cells] = dot(coupled(first_map[...], band), second_map[...]).astype(jnp.bfloat16)


def inside_kernel(early_layers, starts, first_map, second_map, edge_cells, damping, band, *refs):
    traces_out, whole_ext, band_in, sem = refs
    slots, cells = starts.shape[1:]
    chains = traces_out.shape[0] // slots
    early = lax.axis_index("depth") < early_layers
    copy = pltpu.make_async_copy(band, band_in, sem)
    copy.start()
    edge_rows = dot(edge_cells[...], second_map[...])
    whole_ext[cells:] = (coupling_weight * edge_rows).astype(jnp.bfloat16)

    @pl.when(early)
    def _():
        start = starts[:chains].reshape(-1, cells)
        mapped = dot(start, first_map[...]).astype(jnp.bfloat16)
        copy.wait()
        image = dot(coupled(mapped, band_in), second_map[...])
        traces_out[...] = blend(image, start, damping[...])

    @pl.when(jnp.logical_not(early))
    def _():
        copy.wait()
        fill_whole_map(first_map, band_in, second_map, whole_ext)


def whole_map_kernel(early_layers, first_map, band, second_map, whole_in, whole_ext):
    del whole_in

    @pl.when(lax.axis_index("depth") < early_layers)
    def _():
        fill_whole_map(first_map, band, second_map, whole_ext)


def halo_of(messages, groups, live):
    halo = 0.0
    for message, group in zip(messages, groups):
        halo = halo + unpack(message.astype(jnp.float32), group)
    return (halo * live.astype(jnp.float32)).astype(jnp.bfloat16)


def blend(image, start, damp):
    return damp * image + (1.0 - damp) * start.astype(jnp.float32)


def takes_part(step, early_layers):
    layer = lax.axis_index("depth")
    return (layer >= step) & (layer < step + early_layers)


def inner_kernel(part_of, rounds, extras, starts, map_ext, damping, traces, *refs):
    others, out = refs[:-1], refs[-1]
    rows, cells = out.shape

    @pl.when(part_of())
    def _():
        start = starts[rounds].reshape(-1, cells).astype(jnp.float32)
        came = traces[:rows].astype(jnp.float32)
        for (layer, row), other in zip(extras, others):
            here = lax.axis_index("depth") == layer
            came = jnp.where(here, other[row : row + rows].astype(jnp.float32), came)
        start = (start + came).astype(jnp.bfloat16)
        out[...] = blend(dot(start, map_ext[:cells]), start, damping[...])


def step_kernel(swaps, step, chains, keeps, part_of, *refs):
    live, map_ext, damping, edge_next, inner = refs[:5]
    received = refs[5 : 5 + len(swaps)]
    outs = refs[-1 - len(swaps) - keeps :]
    traces_out, messages = outs[0], outs[1 + keeps :]
    cells = inner.shape[1]
    slots = inner.shape[0] // chains
    part = slots // 4

    @pl.when(part_of())
    def _():
        groups = groups_of(swaps)
        halo = []
        for chain in range(chains):
            packed = [ref[chain * part : (chain + 1) * part] for ref in received]
            halo.append(halo_of(packed, groups, live[step + chain]))
        halo = jnp.concatenate(halo, axis=0)
        ended = inner[...] + damping[...] * dot(halo, map_ext[cells:])
        ended = ended.astype(jnp.bfloat16)
        going = traces_out.shape[0]
        traces_out[...] = ended[:going]
        if keeps:
            outs[1][...] = ended[going:]
        at = cells + step * slots
        edges = dot(ended, edge_next[:cells])
        edges += edge_next[at : at + chains * slots].astype(jnp.float32)
        for message, group in zip(messages, groups):
            for chain in range(chains):
                message[chain * part : (chain + 1) * part] = pack(
                    edges[chain * slots : (chain + 1) * slots], group
                )


def final_kernel(swaps, picks, live, map_ext, damping, inner, *refs):
    slots, cells = inner.shape
    received = refs[:-4]
    traces_out, halo, ended, sems = refs[-4:]
    part = slots // 4
    layer = lax.axis_index("depth")
    groups = groups_of(swaps)

    def take(phase):
        messages = received[phase * len(swaps) : (phase + 1) * len(swaps)]
        messages = [ref[ref.shape[0] - part :] for ref in messages]
        halo[...] = halo_of(messages, groups, live[live.shape[0] - 1])

    by_rule = layer < 0
    for at, phase in picks:
        by_rule = by_rule | (layer == at)
        pl.when(layer == at)(functools.partial(take, phase))
    pl.when(jnp.logical_not(by_rule))(functools.partial(take, len(received) // len(swaps) - 1))
    copies = []
    half = cells // LANES // 2 * LANES
    for at, columns in enumerate([slice(0, half), slice(half, cells)]):
        image = dot(halo[...], map_ext[cells:, columns])
        ended[:, columns] = (inner[:, columns] + damping[:, columns] * image).astype(jnp.bfloat16)
        copies.append(
            pltpu.make_async_copy(ended.at[:, columns], traces_out.at[:, columns], sems.at[at])
        )
        copies[-1].start()
    for copy in copies:
        copy.wait()


def call(kernel, out_shape, operands, in_hbm=(), scratch=(), aliases=None, to_hbm=False):
    spaces = [pltpu.HBM if i in in_hbm else pltpu.VMEM for i in range(len(operands))]
    operands = [
        pltpu.with_memory_space_constraint(x, pltpu.HBM) if i in in_hbm else x
        for i, x in enumerate(operands)
    ]
    return pl.pallas_call(
        kernel,
        out_shape=out_shape,
        in_specs=[pl.BlockSpec(memory_space=space) for space in spaces],
        out_specs=[pl.BlockSpec(memory_space=pl.ANY if to_hbm else pltpu.VMEM)] * len(out_shape),
        scratch_shapes=scratch,
        input_output_aliases=aliases or {},
        compiler_params=pltpu.CompilerParams(vmem_limit_bytes=32 * 1024 * 1024),
    )(*operands)


MESH_AXES = ("depth", "gx", "gy")


def send(x, moves, swap=None):
    sizes = [lax.axis_size(axis) for axis in MESH_AXES]
    pairs = []
    for layer, below in moves:
        for i in range(sizes[1]):
            for j in range(sizes[2]):
                to = {"depth": below, "gx": i, "gy": j}
                if swap is not None:
                    axis, parity, _ = swap
                    to[axis] += 1 if to[axis] % 2 == parity else -1
                spot = [to[axis] for axis in MESH_AXES]
                if all(0 <= s < size for s, size in zip(spot, sizes)):
                    here = (layer * sizes[1] + i) * sizes[2] + j
                    there = (spot[0] * sizes[1] + spot[1]) * sizes[2] + spot[2]
                    pairs.append((here, there))
    return lax.ppermute(x, MESH_AXES, pairs)


def local(arrival, source, assignment, counts, first_map, second_map, damping):
    layers = lax.axis_size("depth")
    slots, cells = arrival.shape[1], arrival.shape[4]
    rounds = source.shape[1]
    arrival = arrival[0, :, 0, 0, :]
    source = source[0, :, :, 0, 0, :]
    counts = counts.transpose(0, 2, 3, 1)
    first_map = first_map[0, 0, 0]
    second_map = second_map[0, 0, 0]
    damping = damping[0, 0]
    swaps = exchanges()
    early_layers = layers - rounds + 1
    soon = rounds - 1

    def array(*shape, kind=jnp.bfloat16):
        return jax.ShapeDtypeStruct(shape, kind)

    def scratch(x):
        return pltpu.VMEM(x.shape, x.dtype)

    part = slots // 4
    band = coupling_band(cells)
    whole = array(cells + LANES, cells)
    own = [array(rounds, slots, cells), array(rounds, slots, LANES)]
    copied = [scratch(source), scratch(assignment), scratch(counts)]
    edge, starts, live = call(
        edges_kernel,
        [array(cells + (rounds - 1) * slots, LANES)] + own,
        [source, assignment, counts, first_map],
        in_hbm=range(4),
        scratch=copied + [scratch(first_map), pltpu.SemaphoreType.DMA((2 + rounds,))],
    )
    edge_next = send(edge, [(layer, layer - 1) for layer in range(1, layers)])
    opened = call(
        functools.partial(opening_kernel, early_layers, swaps),
        own + [array(LANES, cells)] + [array(rounds * part, LANES)] * len(swaps),
        [source, assignment, counts, arrival, first_map, starts, live],
        in_hbm=range(1),
        scratch=[scratch(source), pltpu.SemaphoreType.DMA((rounds,))],
        aliases={5: 0, 6: 1},
    )
    starts, live, edge_cells = opened[:3]
    received = [
        send(m, [(layer, layer) for layer in range(early_layers)], swap)
        for m, swap in zip(opened[3:], swaps)
    ]
    inner, map_ext, band = call(
        functools.partial(inside_kernel, early_layers),
        [array(soon * slots, cells, kind=jnp.float32), whole, array(*band.shape)],
        [starts, first_map, second_map, edge_cells, damping, band],
        in_hbm=(5,),
        scratch=[pltpu.SemaphoreType.DMA],
    )
    arrived = list(received)
    picks = [(0, 0)]
    kept = []
    extras = []
    for step in range(rounds - 1):
        chains = soon - step
        keeps = chains > 1 and step > 0
        going = (chains - 1 if keeps else chains) * slots
        outs = [array(going, cells)] + [array(slots, cells)] * keeps
        outs += [array(chains * part, LANES)] * len(swaps)
        part_of = functools.partial(takes_part, step, early_layers)
        if step > 0:
            now = slice(step, step + chains)
            (inner,) = call(
                functools.partial(inner_kernel, part_of, now, []),
                [array(chains * slots, cells, kind=jnp.float32)],
                [starts, map_ext, damping, traces],
            )
        operands = [live, map_ext, damping, edge_next, inner] + received
        ended = call(
            functools.partial(step_kernel, swaps, step, chains, keeps, part_of),
            outs,
            operands,
        )
        moves = [(layer, layer + 1) for layer in range(step, step + early_layers)]
        traces = send(ended[0], moves)
        if keeps:
            kept.append(send(ended[1], [(step, step + 1)]))
            extras.append((step + 1, 0))
        elif chains > 1:
            kept.append(traces)
            extras.append((step + 1, (chains - 1) * slots))
        if chains > 1:
            picks.append((step + 1, len(arrived) // len(swaps)))
        received = [send(m, moves, swap) for m, swap in zip(ended[-len(swaps) :], swaps)]
        arrived += received
        if step == 0:
            (map_ext,) = call(
                functools.partial(whole_map_kernel, early_layers),
                [whole],
                [first_map, band, second_map, map_ext],
                aliases={3: 0},
            )
    everywhere = functools.partial(takes_part, 0, layers)
    (inner,) = call(
        functools.partial(inner_kernel, everywhere, slice(soon, rounds), extras),
        [array(slots, cells, kind=jnp.float32)],
        [starts, map_ext, damping, traces] + kept,
    )
    (ended,) = call(
        functools.partial(final_kernel, swaps, picks),
        [array(slots, cells)],
        [live, map_ext, damping, inner] + arrived,
        scratch=[
            pltpu.VMEM((slots, LANES), jnp.bfloat16),
            scratch(arrival),
            pltpu.SemaphoreType.DMA((2,)),
        ],
        to_hbm=True,
    )
    return ended.reshape(1, slots, 1, 1, cells)


def solution(mesh):
    return jax.shard_map(
        local,
        mesh=mesh,
        in_specs=(
            P("depth", None, "gx", "gy", None),
            P("depth", None, None, "gx", "gy", None),
            P(),
            P(None, None, "gx", "gy"),
            P("depth", "gx", "gy", None, None),
            P("depth", "gx", "gy", None, None),
            P("depth", "gx", "gy", None),
        ),
        out_specs=P("depth", None, "gx", "gy", None),
        check_vma=False,
    )
```

```python
import functools

import jax
import jax.numpy as jnp
import numpy as np
from jax import lax
from jax.experimental import pallas as pl
from jax.experimental.pallas import tpu as pltpu
from jax.sharding import PartitionSpec as P

FX = 32
FY = 28
SHOT_BATCH = 16

coupling_weight = 0.25

LANES = 128
GROUP = LANES // 4
EDGE_AXES = (("gx", 0), ("gy", 2))


def dot(a, b):
    return jnp.dot(a, b, preferred_element_type=jnp.float32)


def dot_t(a, b):
    return lax.dot_general(a, b, (((0,), (0,)), ((), ())), preferred_element_type=jnp.float32)


def group_at(lane):
    return lax.shift_right_logical(lane, GROUP.bit_length() - 1)


def edge_cells_of(lane):
    group, spot = group_at(lane), lane & (GROUP - 1)
    along_y = jnp.where(group == 0, spot, spot + (FX - 1) * FY)
    along_x = jnp.where(group == 2, spot * FY, spot * FY + FY - 1)
    cell = jnp.where(group < 2, along_y, along_x)
    return jnp.where(spot < jnp.where(group < 2, FY, FX), cell, -1)


def edge_selector(cells):
    cell = edge_cells_of(lax.broadcasted_iota(jnp.int32, (1, LANES), 1))
    row = lax.broadcasted_iota(jnp.int32, (cells, LANES), 0)
    return jnp.where(row == cell, 1.0, 0.0).astype(jnp.bfloat16)


def edge_rows_selector(cells):
    cell = edge_cells_of(lax.broadcasted_iota(jnp.int32, (LANES, 1), 0))
    row = lax.broadcasted_iota(jnp.int32, (LANES, cells), 1)
    return jnp.where(row == cell, 1.0, 0.0).astype(jnp.bfloat16)


def exchanges():
    found = []
    for axis, base in EDGE_AXES:
        for parity in range(min(lax.axis_size(axis) - 1, 2)):
            found.append((axis, parity, base))
    return found[::-1]


def groups_of(swaps):
    index = {axis: lax.axis_index(axis) & 1 for axis, _ in EDGE_AXES}
    return [jnp.where(index[axis] == parity, base + 1, base) for axis, parity, base in swaps]


def pack(edges, group):
    rows = edges.shape[0] // 4
    lane_group = group_at(lax.broadcasted_iota(jnp.int32, (rows, LANES), 1))
    packed = jnp.zeros((rows, LANES), jnp.float32)
    for part in range(4):
        piece = edges[part * rows : (part + 1) * rows]
        piece = pltpu.roll(piece, ((part - group) & 3) * GROUP, 1)
        packed = jnp.where(lane_group == part, piece, packed)
    return packed.astype(jnp.bfloat16)


def unpack(packed, group):
    lane_group = group_at(lax.broadcasted_iota(jnp.int32, packed.shape, 1))
    pieces = []
    for part in range(4):
        piece = pltpu.roll(packed, ((group - part) & 3) * GROUP, 1)
        pieces.append(jnp.where(lane_group == group, piece, 0.0))
    return jnp.concatenate(pieces, axis=0)


def first_unit(layer):
    return lax.axis_size("depth") - 1 - layer


def chosen_of(wanted, counts):
    slots = wanted.shape[1]
    shot = lax.broadcasted_iota(jnp.int32, (slots, slots), 0)
    slot = lax.broadcasted_iota(jnp.int32, (1, slots), 1)
    live = jnp.zeros((1, slots), jnp.int32)
    for batch in range(slots // SHOT_BATCH):
        count = jnp.broadcast_to(counts[:, batch : batch + 1], (1, slots))
        live = jnp.where(slot >= batch * SHOT_BATCH, count + batch * SHOT_BATCH, live)
    wanted = jnp.where(slot < live, wanted, -1)
    return jnp.where(shot == wanted, 1.0, 0.0).astype(jnp.bfloat16)


def started(pairs, sems):
    copies = [
        pltpu.make_async_copy(here, there, sems.at[i]) for i, (here, there) in enumerate(pairs)
    ]
    for copy in copies:
        copy.start()
    return copies


def fill_live(live_out, counts):
    position = lax.broadcasted_iota(jnp.int32, (SHOT_BATCH, LANES), 0)
    for r, own in enumerate(counts):
        for batch in range(own.shape[1]):
            count = jnp.broadcast_to(own[:, batch : batch + 1], (SHOT_BATCH, LANES))
            rows = slice(batch * SHOT_BATCH, (batch + 1) * SHOT_BATCH)
            live_out[r, rows] = jnp.where(position < count, 1.0, 0.0).astype(jnp.bfloat16)


def edges_kernel(source, assignment, counts, first_map, edge_out, starts_out, live_out, *refs):
    source_in, assignment_in, counts_in, first_in, sems = refs
    rounds, slots, cells = source.shape
    layer = lax.axis_index("depth")

    @pl.when(layer > 0)
    def _():
        unit = first_unit(layer)
        pairs = [(counts, counts_in), (assignment, assignment_in), (first_map, first_in)]
        pairs += [(source.at[r], source_in.at[r]) for r in range(1, rounds)]
        copies = started(pairs, sems)
        selector = edge_selector(cells)
        copies[0].wait()
        own = [counts_in[unit + r, 0] for r in range(rounds)]
        fill_live(live_out, own)
        copies[1].wait()
        copies[2].wait()
        first_edge = dot(first_in[...], selector).astype(jnp.bfloat16)
        edge_out[:cells] = first_edge
        for r in range(1, rounds):
            copies[2 + r].wait()
            chosen = chosen_of(assignment_in[r : r + 1], own[r])
            starts_out[r] = dot_t(chosen, source_in[r]).astype(jnp.bfloat16)
        edges = dot(starts_out[1:].reshape(-1, cells), first_edge)
        edge_out[cells:] = edges.astype(jnp.bfloat16)


def opening_kernel(early_layers, swaps, source, assignment_in, counts_in, arrival, first_map, *refs):
    starts_out, live_out, edge_cells = refs[2:5]
    messages = refs[5 : 5 + len(swaps)]
    source_in, sems = refs[5 + len(swaps) :]
    rounds, slots, cells = source.shape
    part = slots // 4
    layer = lax.axis_index("depth")
    early = layer < early_layers

    @pl.when(jnp.logical_not(early))
    def _():
        edge_cells[...] = edge_rows_selector(cells)

    @pl.when(early)
    def _():
        unit = first_unit(layer)
        groups = groups_of(swaps)
        copies = started([(source.at[r], source_in.at[r]) for r in range(rounds)], sems)
        edge_cells[...] = edge_rows_selector(cells)
        first_edge = dot(first_map[...], edge_selector(cells)).astype(jnp.bfloat16)
        own = [counts_in[unit + r, 0] for r in range(rounds)]
        fill_live(live_out, own)
        chosen = [chosen_of(assignment_in[r : r + 1], own[r]) for r in range(rounds)]
        for r in range(rounds):
            copies[r].wait()
            picked = dot_t(chosen[r], source_in[r])
            if r == 0:
                live = live_out[0].astype(jnp.float32)
                live = jnp.concatenate([live] * (cells // LANES), axis=1)
                picked = picked + live * arrival[...].astype(jnp.float32)
            picked = picked.astype(jnp.bfloat16)
            starts_out[r] = picked
            edges = dot(picked, first_edge)
            for message, group in zip(messages, groups):
                message[r * part : (r + 1) * part] = pack(edges, group)


def bands(cells):
    found = []
    for at in range(0, cells, 2 * LANES):
        end = min(at + 2 * LANES, cells)
        found.append((slice(max(at - LANES, 0), min(end + LANES, cells)), slice(at, end)))
    return found


def coupling_band(cells):
    cell = np.arange(cells)
    apart = np.abs(cell[:, None] - cell[None, :])
    same_row = cell[:, None] // FY == cell[None, :] // FY
    linked = (apart == FY) | ((apart == 1) & same_row)
    coupling = np.eye(cells) + coupling_weight * linked
    band = np.zeros((len(bands(cells)), 4 * LANES, 2 * LANES), np.float32)
    for block, (rows, columns) in zip(band, bands(cells)):
        piece = coupling[rows, columns]
        block[: piece.shape[0], : piece.shape[1]] = piece
    return jnp.asarray(band, jnp.bfloat16)


def coupled(x, band):
    pieces = []
    for at, (rows, columns) in enumerate(bands(x.shape[1])):
        height, width = rows.stop - rows.start, columns.stop - columns.start
        pieces.append(dot(x[:, rows], band[at, :height, :width]).astype(jnp.bfloat16))
    return jnp.concatenate(pieces, axis=1)


def fill_whole_map(first_map, band, second_map, whole_ext):
    cells = second_map.shape[0]
    whole_ext[:cells] = dot(coupled(first_map[...], band), second_map[...]).astype(jnp.bfloat16)


def inside_kernel(early_layers, starts, first_map, second_map, edge_cells, damping, band, *refs):
    traces_out, whole_ext, band_in, sem = refs
    slots, cells = starts.shape[1:]
    chains = traces_out.shape[0] // slots
    early = lax.axis_index("depth") < early_layers
    copy = pltpu.make_async_copy(band, band_in, sem)
    copy.start()

    @pl.when(early)
    def _():
        start = starts[:chains].reshape(-1, cells)
        mapped = dot(start, first_map[...]).astype(jnp.bfloat16)
        copy.wait()
        rows = jnp.concatenate([coupled(mapped, band_in), edge_cells[...]], axis=0)
        image = dot(rows, second_map[...])
        traces_out[...] = blend(image[: chains * slots], start, damping[...])
        whole_ext[cells:] = (coupling_weight * image[chains * slots :]).astype(jnp.bfloat16)

    @pl.when(jnp.logical_not(early))
    def _():
        edge_rows = dot(edge_cells[...], second_map[...])
        whole_ext[cells:] = (coupling_weight * edge_rows).astype(jnp.bfloat16)
        copy.wait()
        fill_whole_map(first_map, band_in, second_map, whole_ext)


def whole_map_kernel(early_layers, first_map, band, second_map, whole_in, whole_ext):
    del whole_in

    @pl.when(lax.axis_index("depth") < early_layers)
    def _():
        fill_whole_map(first_map, band, second_map, whole_ext)


def halo_of(messages, groups, live):
    halo = 0.0
    for message, group in zip(messages, groups):
        halo = halo + unpack(message.astype(jnp.float32), group)
    return (halo * live.astype(jnp.float32)).astype(jnp.bfloat16)


def blend(image, start, damp):
    return damp * image + (1.0 - damp) * start.astype(jnp.float32)


def takes_part(step, early_layers):
    layer = lax.axis_index("depth")
    return (layer >= step) & (layer < step + early_layers)


def inner_of(start, map_ext, damping):
    cells = start.shape[1]
    return blend(dot(start, map_ext[:cells]), start, damping[...])


def inner_kernel(part_of, step, chains, starts, map_ext, damping, edge_next, traces, *outs):
    inner_out, edges_out, halo_map = outs
    rows, cells = inner_out.shape
    slots = rows // chains

    @pl.when(part_of())
    def _():
        start = starts[step : step + chains].reshape(-1, cells).astype(jnp.float32)
        start = (start + traces[:rows].astype(jnp.float32)).astype(jnp.bfloat16)
        inner = inner_of(start, map_ext, damping)
        inner_out[...] = inner
        at = cells + step * slots
        edges = dot(inner.astype(jnp.bfloat16), edge_next[:cells])
        edges_out[...] = edges + edge_next[at : at + rows].astype(jnp.float32)
        brings = (damping[...] * map_ext[cells:].astype(jnp.float32)).astype(jnp.bfloat16)
        halo_map[:, :cells] = brings
        halo_map[:, cells:] = dot(brings, edge_next[:cells]).astype(jnp.bfloat16)


def last_inner_kernel(extras, starts, map_ext, damping, traces, *refs):
    others, out = refs[:-1], refs[-1]
    rows = out.shape[0]
    came = traces[...].astype(jnp.float32)
    for (layer, row), other in zip(extras, others):
        here = lax.axis_index("depth") == layer
        came = jnp.where(here, other[row : row + rows].astype(jnp.float32), came)
    start = starts[starts.shape[0] - 1].astype(jnp.float32) + came
    out[...] = inner_of(start.astype(jnp.bfloat16), map_ext, damping)


def step_kernel(swaps, step, chains, keeps, part_of, live, inner, *refs):
    operands = refs[:3] if step == 0 else refs[:2]
    refs = refs[len(operands) :]
    received = refs[: len(swaps)]
    outs = refs[len(swaps) :]
    traces_out, messages = outs[0], outs[1 + keeps :]
    cells = inner.shape[1]
    slots = inner.shape[0] // chains
    part = slots // 4

    @pl.when(part_of())
    def _():
        groups = groups_of(swaps)
        halo = []
        for chain in range(chains):
            packed = [ref[chain * part : (chain + 1) * part] for ref in received]
            halo.append(halo_of(packed, groups, live[step + chain]))
        halo = jnp.concatenate(halo, axis=0)
        if step == 0:
            map_ext, damping, edge_next = operands
            ended = inner[...] + damping[...] * dot(halo, map_ext[cells:])
            ended = ended.astype(jnp.bfloat16)
            edges = dot(ended, edge_next[:cells])
            edges += edge_next[cells : cells + chains * slots].astype(jnp.float32)
        else:
            edges_but, halo_map = operands
            edges = edges_but[...] + dot(halo, halo_map[:, cells:])
            ended = (inner[...] + dot(halo, halo_map[:, :cells])).astype(jnp.bfloat16)
        going = traces_out.shape[0]
        traces_out[...] = ended[:going]
        if keeps:
            outs[1][...] = ended[going:]
        for message, group in zip(messages, groups):
            for chain in range(chains):
                message[chain * part : (chain + 1) * part] = pack(
                    edges[chain * slots : (chain + 1) * slots], group
                )


def final_kernel(swaps, picks, live, map_ext, damping, inner, *refs):
    slots, cells = inner.shape
    received = refs[:-3]
    traces_out, ended, sems = refs[-3:]
    part = slots // 4
    layer = lax.axis_index("depth")
    packed = []
    for at in range(len(swaps)):
        phases = [ref[ref.shape[0] - part :].astype(jnp.float32) for ref in received[at :: len(swaps)]]
        message = phases[-1]
        for own, phase in picks:
            message = jnp.where(layer == own, phases[phase], message)
        packed.append(message)
    halo = halo_of(packed, groups_of(swaps), live[live.shape[0] - 1])
    copies = []
    half = cells // LANES // 2 * LANES
    for at, columns in enumerate([slice(0, half), slice(half, cells)]):
        image = dot(halo, map_ext[cells:, columns])
        ended[:, columns] = (inner[:, columns] + damping[:, columns] * image).astype(jnp.bfloat16)
        copies.append(
            pltpu.make_async_copy(ended.at[:, columns], traces_out.at[:, columns], sems.at[at])
        )
        copies[-1].start()
    for copy in copies:
        copy.wait()


def call(kernel, out_shape, operands, in_hbm=(), scratch=(), aliases=None, to_hbm=False):
    spaces = [pltpu.HBM if i in in_hbm else pltpu.VMEM for i in range(len(operands))]
    operands = [
        pltpu.with_memory_space_constraint(x, pltpu.HBM) if i in in_hbm else x
        for i, x in enumerate(operands)
    ]
    return pl.pallas_call(
        kernel,
        out_shape=out_shape,
        in_specs=[pl.BlockSpec(memory_space=space) for space in spaces],
        out_specs=[pl.BlockSpec(memory_space=pl.ANY if to_hbm else pltpu.VMEM)] * len(out_shape),
        scratch_shapes=scratch,
        input_output_aliases=aliases or {},
        compiler_params=pltpu.CompilerParams(vmem_limit_bytes=32 * 1024 * 1024),
    )(*operands)


MESH_AXES = ("depth", "gx", "gy")


def send(x, moves, swap=None):
    sizes = [lax.axis_size(axis) for axis in MESH_AXES]
    pairs = []
    for layer, below in moves:
        for i in range(sizes[1]):
            for j in range(sizes[2]):
                to = {"depth": below, "gx": i, "gy": j}
                if swap is not None:
                    axis, parity, _ = swap
                    to[axis] += 1 if to[axis] % 2 == parity else -1
                spot = [to[axis] for axis in MESH_AXES]
                if all(0 <= s < size for s, size in zip(spot, sizes)):
                    here = (layer * sizes[1] + i) * sizes[2] + j
                    there = (spot[0] * sizes[1] + spot[1]) * sizes[2] + spot[2]
                    pairs.append((here, there))
    return lax.ppermute(x, MESH_AXES, pairs)


def local(arrival, source, assignment, counts, first_map, second_map, damping):
    layers = lax.axis_size("depth")
    slots, cells = arrival.shape[1], arrival.shape[4]
    rounds = source.shape[1]
    arrival = arrival[0, :, 0, 0, :]
    source = source[0, :, :, 0, 0, :]
    counts = counts.transpose(0, 2, 3, 1)
    first_map = first_map[0, 0, 0]
    second_map = second_map[0, 0, 0]
    damping = damping[0, 0]
    swaps = exchanges()
    early_layers = layers - rounds + 1
    soon = rounds - 1

    def array(*shape, kind=jnp.bfloat16):
        return jax.ShapeDtypeStruct(shape, kind)

    def scratch(x):
        return pltpu.VMEM(x.shape, x.dtype)

    part = slots // 4
    band = coupling_band(cells)
    whole = array(cells + LANES, cells)
    own = [array(rounds, slots, cells), array(rounds, slots, LANES)]
    copied = [scratch(source), scratch(assignment), scratch(counts)]
    edge, starts, live = call(
        edges_kernel,
        [array(cells + (rounds - 1) * slots, LANES)] + own,
        [source, assignment, counts, first_map],
        in_hbm=range(4),
        scratch=copied + [scratch(first_map), pltpu.SemaphoreType.DMA((2 + rounds,))],
    )
    edge_next = send(edge, [(layer, layer - 1) for layer in range(1, layers)])
    opened = call(
        functools.partial(opening_kernel, early_layers, swaps),
        own + [array(LANES, cells)] + [array(rounds * part, LANES)] * len(swaps),
        [source, assignment, counts, arrival, first_map, starts, live],
        in_hbm=range(1),
        scratch=[scratch(source), pltpu.SemaphoreType.DMA((rounds,))],
        aliases={5: 0, 6: 1},
    )
    starts, live, edge_cells = opened[:3]
    received = [
        send(m, [(layer, layer) for layer in range(early_layers)], swap)
        for m, swap in zip(opened[3:], swaps)
    ]
    inner, map_ext, band = call(
        functools.partial(inside_kernel, early_layers),
        [array(soon * slots, cells, kind=jnp.float32), whole, array(*band.shape)],
        [starts, first_map, second_map, edge_cells, damping, band],
        in_hbm=(5,),
        scratch=[pltpu.SemaphoreType.DMA],
    )
    arrived = list(received)
    picks = [(0, 0)]
    kept = []
    extras = []
    for step in range(rounds - 1):
        chains = soon - step
        keeps = chains > 1 and step > 0
        going = (chains - 1 if keeps else chains) * slots
        outs = [array(going, cells)] + [array(slots, cells)] * keeps
        outs += [array(chains * part, LANES)] * len(swaps)
        part_of = functools.partial(takes_part, step, early_layers)
        operands = [map_ext, damping, edge_next]
        if step > 0:
            rows = chains * slots
            inner, *operands = call(
                functools.partial(inner_kernel, part_of, step, chains),
                [
                    array(rows, cells, kind=jnp.float32),
                    array(rows, LANES, kind=jnp.float32),
                    array(LANES, cells + LANES),
                ],
                [starts, map_ext, damping, edge_next, traces],
            )
        operands = [live, inner] + operands + received
        ended = call(
            functools.partial(step_kernel, swaps, step, chains, keeps, part_of),
            outs,
            operands,
        )
        moves = [(layer, layer + 1) for layer in range(step, step + early_layers)]
        traces = send(ended[0], moves)
        if keeps:
            kept.append(send(ended[1], [(step, step + 1)]))
            extras.append((step + 1, 0))
        elif chains > 1:
            kept.append(traces)
            extras.append((step + 1, (chains - 1) * slots))
        if chains > 1:
            picks.append((step + 1, len(arrived) // len(swaps)))
        received = [send(m, moves, swap) for m, swap in zip(ended[-len(swaps) :], swaps)]
        arrived += received
        if step == 0:
            (map_ext,) = call(
                functools.partial(whole_map_kernel, early_layers),
                [whole],
                [first_map, band, second_map, map_ext],
                aliases={3: 0},
            )
    (inner,) = call(
        functools.partial(last_inner_kernel, extras),
        [array(slots, cells, kind=jnp.float32)],
        [starts, map_ext, damping, traces] + kept,
    )
    (ended,) = call(
        functools.partial(final_kernel, swaps, picks),
        [array(slots, cells)],
        [live, map_ext, damping, inner] + arrived,
        scratch=[
            scratch(arrival),
            pltpu.SemaphoreType.DMA((2,)),
        ],
        to_hbm=True,
    )
    return ended.reshape(1, slots, 1, 1, cells)


def solution(mesh):
    return jax.shard_map(
        local,
        mesh=mesh,
        in_specs=(
            P("depth", None, "gx", "gy", None),
            P("depth", None, None, "gx", "gy", None),
            P(),
            P(None, None, "gx", "gy"),
            P("depth", "gx", "gy", None, None),
            P("depth", "gx", "gy", None, None),
            P("depth", "gx", "gy", None),
        ),
        out_specs=P("depth", None, "gx", "gy", None),
        check_vma=False,
    )
```

```python
import functools

import jax
import jax.numpy as jnp
import numpy as np
from jax import lax
from jax.experimental import pallas as pl
from jax.experimental.pallas import tpu as pltpu
from jax.sharding import PartitionSpec as P

FX = 32
FY = 28
SHOT_BATCH = 16

coupling_weight = 0.25

LANES = 128
GROUP = LANES // 4
EDGE_AXES = (("gx", 0), ("gy", 2))


def dot(a, b):
    return jnp.dot(a, b, preferred_element_type=jnp.float32)


def dot_t(a, b):
    return lax.dot_general(a, b, (((0,), (0,)), ((), ())), preferred_element_type=jnp.float32)


def group_at(lane):
    return lax.shift_right_logical(lane, GROUP.bit_length() - 1)


def edge_cells_of(lane):
    group, spot = group_at(lane), lane & (GROUP - 1)
    along_y = jnp.where(group == 0, spot, spot + (FX - 1) * FY)
    along_x = jnp.where(group == 2, spot * FY, spot * FY + FY - 1)
    cell = jnp.where(group < 2, along_y, along_x)
    return jnp.where(spot < jnp.where(group < 2, FY, FX), cell, -1)


def edge_selector(cells):
    cell = edge_cells_of(lax.broadcasted_iota(jnp.int32, (1, LANES), 1))
    row = lax.broadcasted_iota(jnp.int32, (cells, LANES), 0)
    return jnp.where(row == cell, 1.0, 0.0).astype(jnp.bfloat16)


def edge_rows_selector(cells):
    cell = edge_cells_of(lax.broadcasted_iota(jnp.int32, (LANES, 1), 0))
    row = lax.broadcasted_iota(jnp.int32, (LANES, cells), 1)
    return jnp.where(row == cell, 1.0, 0.0).astype(jnp.bfloat16)


def exchanges():
    found = []
    for axis, base in EDGE_AXES:
        for parity in range(min(lax.axis_size(axis) - 1, 2)):
            found.append((axis, parity, base))
    return found[::-1]


def groups_of(swaps):
    index = {axis: lax.axis_index(axis) & 1 for axis, _ in EDGE_AXES}
    return [jnp.where(index[axis] == parity, base + 1, base) for axis, parity, base in swaps]


def pack(edges, group):
    rows = edges.shape[0] // 4
    lane_group = group_at(lax.broadcasted_iota(jnp.int32, (rows, LANES), 1))
    packed = jnp.zeros((rows, LANES), jnp.float32)
    for part in range(4):
        piece = edges[part * rows : (part + 1) * rows]
        piece = pltpu.roll(piece, ((part - group) & 3) * GROUP, 1)
        packed = jnp.where(lane_group == part, piece, packed)
    return packed.astype(jnp.bfloat16)


def unpack(packed, group):
    lane_group = group_at(lax.broadcasted_iota(jnp.int32, packed.shape, 1))
    pieces = []
    for part in range(4):
        piece = pltpu.roll(packed, ((group - part) & 3) * GROUP, 1)
        pieces.append(jnp.where(lane_group == group, piece, 0.0))
    return jnp.concatenate(pieces, axis=0)


def first_unit(layer):
    return lax.axis_size("depth") - 1 - layer


def chosen_of(wanted, counts):
    slots = wanted.shape[1]
    shot = lax.broadcasted_iota(jnp.int32, (slots, slots), 0)
    slot = lax.broadcasted_iota(jnp.int32, (1, slots), 1)
    live = jnp.zeros((1, slots), jnp.int32)
    for batch in range(slots // SHOT_BATCH):
        count = jnp.broadcast_to(counts[:, batch : batch + 1], (1, slots))
        live = jnp.where(slot >= batch * SHOT_BATCH, count + batch * SHOT_BATCH, live)
    wanted = jnp.where(slot < live, wanted, -1)
    return jnp.where(shot == wanted, 1.0, 0.0).astype(jnp.bfloat16)


def started(pairs, sems):
    copies = [
        pltpu.make_async_copy(here, there, sems.at[i]) for i, (here, there) in enumerate(pairs)
    ]
    for copy in copies:
        copy.start()
    return copies


def fill_live(live_out, counts):
    position = lax.broadcasted_iota(jnp.int32, (SHOT_BATCH, LANES), 0)
    for r, own in enumerate(counts):
        for batch in range(own.shape[1]):
            count = jnp.broadcast_to(own[:, batch : batch + 1], (SHOT_BATCH, LANES))
            rows = slice(batch * SHOT_BATCH, (batch + 1) * SHOT_BATCH)
            live_out[r, rows] = jnp.where(position < count, 1.0, 0.0).astype(jnp.bfloat16)


def edges_kernel(source, assignment, counts, first_map, edge_out, starts_out, live_out, *refs):
    source_in, assignment_in, counts_in, first_in, sems = refs
    rounds, slots, cells = source.shape
    layer = lax.axis_index("depth")

    @pl.when(layer > 0)
    def _():
        unit = first_unit(layer)
        pairs = [(counts, counts_in), (assignment, assignment_in), (first_map, first_in)]
        pairs += [(source.at[r], source_in.at[r]) for r in range(1, rounds)]
        copies = started(pairs, sems)
        selector = edge_selector(cells)
        copies[0].wait()
        own = [counts_in[unit + r, 0] for r in range(rounds)]
        fill_live(live_out, own)
        copies[1].wait()
        copies[2].wait()
        first_edge = dot(first_in[...], selector).astype(jnp.bfloat16)
        edge_out[:cells] = first_edge
        for r in range(1, rounds):
            copies[2 + r].wait()
            chosen = chosen_of(assignment_in[r : r + 1], own[r])
            starts_out[r] = dot_t(chosen, source_in[r]).astype(jnp.bfloat16)
        edges = dot(starts_out[1:].reshape(-1, cells), first_edge)
        edge_out[cells:] = edges.astype(jnp.bfloat16)


def opening_kernel(early_layers, swaps, source, assignment_in, counts_in, arrival, first_map, *refs):
    starts_out, live_out, edge_cells = refs[2:5]
    messages = refs[5 : 5 + len(swaps)]
    source_in, sems = refs[5 + len(swaps) :]
    rounds, slots, cells = source.shape
    part = slots // 4
    layer = lax.axis_index("depth")
    early = layer < early_layers

    @pl.when(jnp.logical_not(early))
    def _():
        edge_cells[...] = edge_rows_selector(cells)

    @pl.when(early)
    def _():
        unit = first_unit(layer)
        groups = groups_of(swaps)
        copies = started([(source.at[r], source_in.at[r]) for r in range(rounds)], sems)
        edge_cells[...] = edge_rows_selector(cells)
        first_edge = dot(first_map[...], edge_selector(cells)).astype(jnp.bfloat16)
        own = [counts_in[unit + r, 0] for r in range(rounds)]
        fill_live(live_out, own)
        chosen = [chosen_of(assignment_in[r : r + 1], own[r]) for r in range(rounds)]
        for r in range(rounds):
            copies[r].wait()
            picked = dot_t(chosen[r], source_in[r])
            if r == 0:
                live = live_out[0].astype(jnp.float32)
                live = jnp.concatenate([live] * (cells // LANES), axis=1)
                picked = picked + live * arrival[...].astype(jnp.float32)
            picked = picked.astype(jnp.bfloat16)
            starts_out[r] = picked
            edges = dot(picked, first_edge)
            for message, group in zip(messages, groups):
                message[r * part : (r + 1) * part] = pack(edges, group)


def bands(cells):
    found = []
    for at in range(0, cells, 2 * LANES):
        end = min(at + 2 * LANES, cells)
        found.append((slice(max(at - LANES, 0), min(end + LANES, cells)), slice(at, end)))
    return found


def coupling_band(cells):
    cell = np.arange(cells)
    apart = np.abs(cell[:, None] - cell[None, :])
    same_row = cell[:, None] // FY == cell[None, :] // FY
    linked = (apart == FY) | ((apart == 1) & same_row)
    coupling = np.eye(cells) + coupling_weight * linked
    band = np.zeros((len(bands(cells)), 4 * LANES, 2 * LANES), np.float32)
    for block, (rows, columns) in zip(band, bands(cells)):
        piece = coupling[rows, columns]
        block[: piece.shape[0], : piece.shape[1]] = piece
    return jnp.asarray(band, jnp.bfloat16)


def coupled(x, band):
    pieces = []
    for at, (rows, columns) in enumerate(bands(x.shape[1])):
        height, width = rows.stop - rows.start, columns.stop - columns.start
        pieces.append(dot(x[:, rows], band[at, :height, :width]).astype(jnp.bfloat16))
    return jnp.concatenate(pieces, axis=1)


def fill_whole_map(first_map, band, second_map, whole_ext):
    cells = second_map.shape[0]
    whole_ext[:cells] = dot(coupled(first_map[...], band), second_map[...]).astype(jnp.bfloat16)


def inside_kernel(early_layers, starts, first_map, second_map, edge_cells, damping, band, *refs):
    traces_out, whole_ext, band_in, sem = refs
    slots, cells = starts.shape[1:]
    chains = traces_out.shape[0] // slots
    early = lax.axis_index("depth") < early_layers
    copy = pltpu.make_async_copy(band, band_in, sem)
    copy.start()

    @pl.when(early)
    def _():
        start = starts[:chains].reshape(-1, cells)
        mapped = dot(start, first_map[...]).astype(jnp.bfloat16)
        copy.wait()
        rows = jnp.concatenate([coupled(mapped, band_in), edge_cells[...]], axis=0)
        image = dot(rows, second_map[...])
        traces_out[...] = blend(image[: chains * slots], start, damping[...])
        whole_ext[cells:] = (coupling_weight * image[chains * slots :]).astype(jnp.bfloat16)

    @pl.when(jnp.logical_not(early))
    def _():
        edge_rows = dot(edge_cells[...], second_map[...])
        whole_ext[cells:] = (coupling_weight * edge_rows).astype(jnp.bfloat16)
        copy.wait()
        fill_whole_map(first_map, band_in, second_map, whole_ext)


def whole_map_kernel(early_layers, first_map, band, second_map, damping, edge_next, *refs):
    whole_in, whole_ext, halo_map = refs
    cells = first_map.shape[0]
    brings = (damping[...] * whole_in[cells:].astype(jnp.float32)).astype(jnp.bfloat16)
    halo_map[:, :cells] = brings
    halo_map[:, cells:] = dot(brings, edge_next[:cells]).astype(jnp.bfloat16)

    @pl.when(lax.axis_index("depth") < early_layers)
    def _():
        fill_whole_map(first_map, band, second_map, whole_ext)


def halo_of(messages, groups, live):
    halo = 0.0
    for message, group in zip(messages, groups):
        halo = halo + unpack(message.astype(jnp.float32), group)
    return (halo * live.astype(jnp.float32)).astype(jnp.bfloat16)


def blend(image, start, damp):
    return damp * image + (1.0 - damp) * start.astype(jnp.float32)


def takes_part(step, early_layers):
    layer = lax.axis_index("depth")
    return (layer >= step) & (layer < step + early_layers)


def inner_of(start, map_ext, damping):
    cells = start.shape[1]
    return blend(dot(start, map_ext[:cells]), start, damping[...])


def inner_kernel(part_of, step, chains, starts, map_ext, damping, edge_next, traces, *outs):
    inner_out, edges_out = outs
    rows, cells = inner_out.shape
    slots = rows // chains

    @pl.when(part_of())
    def _():
        start = starts[step : step + chains].reshape(-1, cells).astype(jnp.float32)
        start = (start + traces[:rows].astype(jnp.float32)).astype(jnp.bfloat16)
        inner = inner_of(start, map_ext, damping)
        inner_out[...] = inner
        at = cells + step * slots
        edges = dot(inner.astype(jnp.bfloat16), edge_next[:cells])
        edges_out[...] = edges + edge_next[at : at + rows].astype(jnp.float32)


def last_inner_kernel(extras, starts, map_ext, damping, traces, *refs):
    others, out = refs[:-1], refs[-1]
    rows = out.shape[0]
    came = traces[...].astype(jnp.float32)
    for (layer, row), other in zip(extras, others):
        here = lax.axis_index("depth") == layer
        came = jnp.where(here, other[row : row + rows].astype(jnp.float32), came)
    start = starts[starts.shape[0] - 1].astype(jnp.float32) + came
    out[...] = inner_of(start.astype(jnp.bfloat16), map_ext, damping)


def step_kernel(swaps, step, chains, keeps, part_of, live, inner, *refs):
    operands = refs[:3] if step == 0 else refs[:2]
    refs = refs[len(operands) :]
    received = refs[: len(swaps)]
    outs = refs[len(swaps) :]
    traces_out, messages = outs[0], outs[1 + keeps :]
    cells = inner.shape[1]
    slots = inner.shape[0] // chains
    part = slots // 4

    @pl.when(part_of())
    def _():
        groups = groups_of(swaps)
        halo = []
        for chain in range(chains):
            packed = [ref[chain * part : (chain + 1) * part] for ref in received]
            halo.append(halo_of(packed, groups, live[step + chain]))
        halo = jnp.concatenate(halo, axis=0)
        if step == 0:
            map_ext, damping, edge_next = operands
            ended = inner[...] + damping[...] * dot(halo, map_ext[cells:])
            ended = ended.astype(jnp.bfloat16)
            edges = dot(ended, edge_next[:cells])
            edges += edge_next[cells : cells + chains * slots].astype(jnp.float32)
        else:
            edges_but, halo_map = operands
            edges = edges_but[...] + dot(halo, halo_map[:, cells:])
            ended = (inner[...] + dot(halo, halo_map[:, :cells])).astype(jnp.bfloat16)
        going = traces_out.shape[0]
        traces_out[...] = ended[:going]
        if keeps:
            outs[1][...] = ended[going:]
        for message, group in zip(messages, groups):
            for chain in range(chains):
                message[chain * part : (chain + 1) * part] = pack(
                    edges[chain * slots : (chain + 1) * slots], group
                )


def final_kernel(swaps, picks, live, map_ext, damping, inner, *refs):
    slots, cells = inner.shape
    received = refs[:-3]
    traces_out, ended, sems = refs[-3:]
    part = slots // 4
    layer = lax.axis_index("depth")
    packed = []
    for at in range(len(swaps)):
        phases = [ref[ref.shape[0] - part :].astype(jnp.float32) for ref in received[at :: len(swaps)]]
        message = phases[-1]
        for own, phase in picks:
            message = jnp.where(layer == own, phases[phase], message)
        packed.append(message)
    halo = halo_of(packed, groups_of(swaps), live[live.shape[0] - 1])
    copies = []
    half = cells // LANES // 2 * LANES
    for at, columns in enumerate([slice(0, half), slice(half, cells)]):
        image = dot(halo, map_ext[cells:, columns])
        ended[:, columns] = (inner[:, columns] + damping[:, columns] * image).astype(jnp.bfloat16)
        copies.append(
            pltpu.make_async_copy(ended.at[:, columns], traces_out.at[:, columns], sems.at[at])
        )
        copies[-1].start()
    for copy in copies:
        copy.wait()


def call(kernel, out_shape, operands, in_hbm=(), scratch=(), aliases=None, to_hbm=False):
    spaces = [pltpu.HBM if i in in_hbm else pltpu.VMEM for i in range(len(operands))]
    operands = [
        pltpu.with_memory_space_constraint(x, pltpu.HBM) if i in in_hbm else x
        for i, x in enumerate(operands)
    ]
    return pl.pallas_call(
        kernel,
        out_shape=out_shape,
        in_specs=[pl.BlockSpec(memory_space=space) for space in spaces],
        out_specs=[pl.BlockSpec(memory_space=pl.ANY if to_hbm else pltpu.VMEM)] * len(out_shape),
        scratch_shapes=scratch,
        input_output_aliases=aliases or {},
        compiler_params=pltpu.CompilerParams(vmem_limit_bytes=32 * 1024 * 1024),
    )(*operands)


MESH_AXES = ("depth", "gx", "gy")


def send(x, moves, swap=None):
    sizes = [lax.axis_size(axis) for axis in MESH_AXES]
    pairs = []
    for layer, below in moves:
        for i in range(sizes[1]):
            for j in range(sizes[2]):
                to = {"depth": below, "gx": i, "gy": j}
                if swap is not None:
                    axis, parity, _ = swap
                    to[axis] += 1 if to[axis] % 2 == parity else -1
                spot = [to[axis] for axis in MESH_AXES]
                if all(0 <= s < size for s, size in zip(spot, sizes)):
                    here = (layer * sizes[1] + i) * sizes[2] + j
                    there = (spot[0] * sizes[1] + spot[1]) * sizes[2] + spot[2]
                    pairs.append((here, there))
    return lax.ppermute(x, MESH_AXES, pairs)


def local(arrival, source, assignment, counts, first_map, second_map, damping):
    layers = lax.axis_size("depth")
    slots, cells = arrival.shape[1], arrival.shape[4]
    rounds = source.shape[1]
    arrival = arrival[0, :, 0, 0, :]
    source = source[0, :, :, 0, 0, :]
    counts = counts.transpose(0, 2, 3, 1)
    first_map = first_map[0, 0, 0]
    second_map = second_map[0, 0, 0]
    damping = damping[0, 0]
    swaps = exchanges()
    early_layers = layers - rounds + 1
    soon = rounds - 1

    def array(*shape, kind=jnp.bfloat16):
        return jax.ShapeDtypeStruct(shape, kind)

    def scratch(x):
        return pltpu.VMEM(x.shape, x.dtype)

    part = slots // 4
    band = coupling_band(cells)
    whole = array(cells + LANES, cells)
    own = [array(rounds, slots, cells), array(rounds, slots, LANES)]
    copied = [scratch(source), scratch(assignment), scratch(counts)]
    edge, starts, live = call(
        edges_kernel,
        [array(cells + (rounds - 1) * slots, LANES)] + own,
        [source, assignment, counts, first_map],
        in_hbm=range(4),
        scratch=copied + [scratch(first_map), pltpu.SemaphoreType.DMA((2 + rounds,))],
    )
    edge_next = send(edge, [(layer, layer - 1) for layer in range(1, layers)])
    opened = call(
        functools.partial(opening_kernel, early_layers, swaps),
        own + [array(LANES, cells)] + [array(rounds * part, LANES)] * len(swaps),
        [source, assignment, counts, arrival, first_map, starts, live],
        in_hbm=range(1),
        scratch=[scratch(source), pltpu.SemaphoreType.DMA((rounds,))],
        aliases={5: 0, 6: 1},
    )
    starts, live, edge_cells = opened[:3]
    received = [
        send(m, [(layer, layer) for layer in range(early_layers)], swap)
        for m, swap in zip(opened[3:], swaps)
    ]
    inner, map_ext, band = call(
        functools.partial(inside_kernel, early_layers),
        [array(soon * slots, cells, kind=jnp.float32), whole, array(*band.shape)],
        [starts, first_map, second_map, edge_cells, damping, band],
        in_hbm=(5,),
        scratch=[pltpu.SemaphoreType.DMA],
    )
    arrived = list(received)
    picks = [(0, 0)]
    kept = []
    extras = []
    for step in range(rounds - 1):
        chains = soon - step
        keeps = chains > 1 and step > 0
        going = (chains - 1 if keeps else chains) * slots
        outs = [array(going, cells)] + [array(slots, cells)] * keeps
        outs += [array(chains * part, LANES)] * len(swaps)
        part_of = functools.partial(takes_part, step, early_layers)
        operands = [map_ext, damping, edge_next]
        if step > 0:
            rows = chains * slots
            inner, edges = call(
                functools.partial(inner_kernel, part_of, step, chains),
                [
                    array(rows, cells, kind=jnp.float32),
                    array(rows, LANES, kind=jnp.float32),
                ],
                [starts, map_ext, damping, edge_next, traces],
            )
            operands = [edges, halo_map]
        operands = [live, inner] + operands + received
        ended = call(
            functools.partial(step_kernel, swaps, step, chains, keeps, part_of),
            outs,
            operands,
        )
        moves = [(layer, layer + 1) for layer in range(step, step + early_layers)]
        traces = send(ended[0], moves)
        if keeps:
            kept.append(send(ended[1], [(step, step + 1)]))
            extras.append((step + 1, 0))
        elif chains > 1:
            kept.append(traces)
            extras.append((step + 1, (chains - 1) * slots))
        if chains > 1:
            picks.append((step + 1, len(arrived) // len(swaps)))
        received = [send(m, moves, swap) for m, swap in zip(ended[-len(swaps) :], swaps)]
        arrived += received
        if step == 0:
            map_ext, halo_map = call(
                functools.partial(whole_map_kernel, early_layers),
                [whole, array(LANES, cells + LANES)],
                [first_map, band, second_map, damping, edge_next, map_ext],
                aliases={5: 0},
            )
    (inner,) = call(
        functools.partial(last_inner_kernel, extras),
        [array(slots, cells, kind=jnp.float32)],
        [starts, map_ext, damping, traces] + kept,
    )
    (ended,) = call(
        functools.partial(final_kernel, swaps, picks),
        [array(slots, cells)],
        [live, map_ext, damping, inner] + arrived,
        scratch=[
            scratch(arrival),
            pltpu.SemaphoreType.DMA((2,)),
        ],
        to_hbm=True,
    )
    return ended.reshape(1, slots, 1, 1, cells)


def solution(mesh):
    return jax.shard_map(
        local,
        mesh=mesh,
        in_specs=(
            P("depth", None, "gx", "gy", None),
            P("depth", None, None, "gx", "gy", None),
            P(),
            P(None, None, "gx", "gy"),
            P("depth", "gx", "gy", None, None),
            P("depth", "gx", "gy", None, None),
            P("depth", "gx", "gy", None),
        ),
        out_specs=P("depth", None, "gx", "gy", None),
        check_vma=False,
    )
```
